128 devices in a mesh: gx: 8 (over y_lo, z), gy: 8 (over y_hi, x), gz: 2 (over core).
Axes of the slice: x: 4, y: 4 (y_hi: 2, y_lo: 2; y = y_hi * 2 + y_lo), z: 4, core: 2. Of those that a mesh axis runs over, the one named last changes fastest.
Arguments:
- velocity: float32 [3, 128, 256, 512], P(None, 'gx', 'gy', 'gz'), may hold values from -6 to 6
- stress: float32 [6, 128, 256, 512], P(None, 'gx', 'gy', 'gz'), may hold values from -6 to 6
- material: int32 [128, 256, 512], P('gx', 'gy', 'gz'), may hold values from 0 to 15
- properties: float32 [16, 3], replicated, may hold values from 0.5 to 2
- owner_map: int32 [64, 512, 1], replicated, may hold values from 0 to 127; in each aligned block of 512 rows (0 to 511, 512 to 1023, ..., all dimensions but the last counted through in order) at most 8 rows name the same one
- cell_map: int32 [64, 512], replicated, may hold values from 0 to 4095
- height: float32 [256, 2048], P('gx', ('gy', 'gz')), may hold values from -6 to 6
- current: float32 [256, 2048], P('gx', ('gy', 'gz')), may hold values from -6 to 6
- sea_depth: float32 [256, 2048], P('gx', ('gy', 'gz')), may hold values from 120 to 240
- wet_mask: int32 [256, 2048], P('gx', ('gy', 'gz')), may hold values 0 or 1
Outputs:
- velocity_out: float32 [3, 128, 256, 512], P(None, 'gx', 'gy', 'gz')
- stress_out: float32 [6, 128, 256, 512], P(None, 'gx', 'gy', 'gz')
- height_out: float32 [256, 2048], P('gx', ('gy', 'gz'))
- current_out: float32 [256, 2048], P('gx', ('gy', 'gz'))
The draws below stay inside these ranges and needn't reach their ends.
Inputs may be any that keep to these rules, and one draw needn't show every extreme that they name: `owner_map`: among the 512 cells of one tile at most 8 have the same owner, and in some tile exactly 8 do.
All inputs are finite; a program needn't handle non-finite values. No bound on the sum of `wet_mask` on one device may be relied on, other than what follows from the above.
Results may differ from the reference program's by a relative error of at most 0.0003.
Values sent between devices are 32-bit elements; how exact they have to be, the bound alone decides.
No kernel may reach another device: no remote copies, remote signals or barrier semaphores. Data moves between devices by JAX's collectives and lax.ppermute only.
A program may use at most 128 MiB of HBM per device.

```python
import math
import jax
import jax.numpy as jnp
import numpy as np
from jax import lax

CX = 16
CY = 32
SUBSTEPS = 2
NMAT = 16
OL = 32
OR = 128
NX = 128
NY = 256
NZ = 512
SURF = 512
TILES = 64
CAP = 8
OLON = 256
OLAT = 2048
N_GX = 8
N_GY = 8
N_GZ = 2


def draw_sea_depth(key, part):
    return jax.random.uniform(key, (OLON, OLAT), jnp.float32, 120.0, 240.0)


def plant(array, rng, smallest, top_value):
    longest = array.shape.index(max(array.shape))
    spots = []
    for shift in (0, 1):
        where = [jax.random.randint(jax.random.fold_in(rng, axis), (), 0, length) for axis, length in enumerate(array.shape)]
        where[longest] = (where[longest] + shift) % array.shape[longest]
        spots.append(tuple(where))
    return array.at[spots[0]].set(smallest).at[spots[1]].set(top_value)


def shard_levels(key, dims, split, least, top_value):
    def one(axis_at, shards_of):
        draws = jax.random.uniform(jax.random.fold_in(jax.random.fold_in(key, 6), axis_at), (shards_of,), jnp.float32, least / len(split), top_value / len(split))
        return jnp.repeat(jnp.exp(draws), dims[axis_at] // shards_of).reshape((-1,) + (1,) * (len(dims) - axis_at - 1))

    factor_of = one(*split[0])
    for cut in split[1:]:
        factor_of = factor_of * one(*cut)
    return factor_of


def deal_out(own_key, own, number, rows, amount, top, limit, slope):
    ranking = jax.random.permutation(own_key, amount)
    crowded, usual = shares(amount, rows * top, limit, slope, True), shares(amount, rows * top, limit, slope, False)
    places = jnp.arange(amount)

    def named(tallies, offset_by):
        used = int((tallies > 0).sum())
        fixed = max(1, used // 4)
        shifted = fixed + (places - fixed + offset_by * (used - fixed)) % max(1, amount - fixed)
        return jnp.zeros((amount,), jnp.int32).at[ranking[jnp.where(places < fixed, places, shifted)]].set(jnp.asarray(tallies, jnp.int32))

    tallies = jnp.where(number % 4 == 0, named(crowded, number // 4), named(usual, number - number // 4 - 1))
    mixed = jax.random.permutation(jax.random.fold_in(own, 3), amount)
    giver, taker = mixed[0:amount // 2 * 2:2], mixed[1:amount // 2 * 2:2]
    margin = jnp.minimum(tallies[giver] - 1, limit - tallies[taker]) // 2
    margin = jnp.where((giver == ranking[0]) | (taker == ranking[0]) | (tallies[taker] == 0), 0, jnp.maximum(margin, 0))
    shifted = jax.random.randint(jax.random.fold_in(own, 4), (amount // 2,), 0, 1 << 20) % (margin + 1)
    tallies = tallies.at[giver].add(-shifted).at[taker].add(shifted)
    items = jnp.searchsorted(jnp.cumsum(tallies), jnp.arange(rows * top), side="right").astype(jnp.int32)
    grid = items.reshape(top, rows).T
    grid = grid[jax.random.permutation(jax.random.fold_in(own, 1), rows)]
    offset_by = jax.random.randint(jax.random.fold_in(own, 2), (rows, 1), 0, top)
    return jnp.take_along_axis(grid, (jnp.arange(top)[None, :] + offset_by) % top, axis=1)


def shares(count, total, limit, lean, full):
    weights = [(1 << 20) // math.isqrt(rank ** lean) + 1 for rank in range(1, count + 1)]
    largest = limit if full else min(limit, max(-(-total // count), total * weights[0] // sum(weights)))
    least = 1 if total - largest >= count - 1 else 0
    counts, rest = [largest] + [least] * (count - 1), total - largest - least * (count - 1)
    while rest > 0:
        candidates = [i for i in range(1, count) if counts[i] < largest] or [i for i in range(1, count) if counts[i] < limit]
        pool, budget = sum([weights[i] for i in candidates]), rest
        for i in candidates:
            addition = min(limit - counts[i], max(1, budget * weights[i] // pool), rest)
            counts[i] = counts[i] + addition
            rest = rest - addition
    return np.array(counts)


def gaussian(key, extent, width, most, pieces=(), dtype=jnp.bfloat16):
    factor_of = shard_levels(key, extent, pieces, -0.22, 0.18) if pieces else 1.0
    values = jax.random.normal(key, extent, jnp.float32) * width * factor_of
    return jnp.minimum(jnp.maximum(values, -most), most).astype(dtype)


def setup_inputs(seed: int = 0) -> dict:
    keys = jax.random.split(jax.random.key(seed), 11)
    velocity = gaussian(keys[0], (3, NX, NY, NZ), 1.0, 6.0, ((1, 8), (2, 8), (3, 2)), jnp.float32)
    stress = gaussian(keys[1], (6, NX, NY, NZ), 1.0, 6.0, ((1, 8), (2, 8), (3, 2)), jnp.float32)
    material = plant(jax.random.randint(keys[2], (NX, NY, NZ), 0, NMAT), jax.random.fold_in(keys[2], 1), 0, NMAT - 1).astype(jnp.int32)
    properties = jnp.clip(jnp.exp(jax.random.uniform(keys[3], (NMAT, 3), jnp.float32, math.log(0.5), math.log(2.0))), 0.5, 2.0)
    owner_map_keys = jax.random.split(jax.random.fold_in(keys[4], 1), TILES * SURF // SURF)
    owner_map_turns = jax.random.permutation(jax.random.fold_in(keys[4], 3), TILES * SURF // SURF)
    owner_map = jax.vmap(lambda own, number: deal_out(jax.random.fold_in(keys[4], 2), own, number, SURF, N_GX * N_GY * N_GZ, 1, CAP, 2))(owner_map_keys, owner_map_turns).reshape((TILES, SURF, 1))
    cell_map = plant(jax.random.randint(keys[5], (TILES, SURF), 0, OL * OR), jax.random.fold_in(keys[5], 1), 0, (OL * OR) - 1).astype(jnp.int32)
    height = gaussian(keys[6], (OLON, OLAT), 1.0, 6.0, ((0, 8), (1, 16)), jnp.float32)
    current = gaussian(keys[7], (OLON, OLAT), 1.0, 6.0, ((0, 8), (1, 16)), jnp.float32)
    sea_depth = draw_sea_depth(jax.random.fold_in(keys[10], 71), 0)
    wet_mask = plant((jax.random.randint(keys[9], (OLON, OLAT), 0, 10) < 9).astype(jnp.int32), jax.random.fold_in(keys[9], 1), 0, 1)
    return dict(velocity=velocity, stress=stress, material=material, properties=properties, owner_map=owner_map, cell_map=cell_map, height=height, current=current, sea_depth=sea_depth, wet_mask=wet_mask)


TIME_STEP = 0.25
GRAV_STEP = 400.0


def central(padded, direction):
    low_cut = [slice(None), slice(1, -1), slice(1, -1), slice(1, -1)]
    high_cut = list(low_cut)
    low_cut[direction] = slice(0, -2)
    high_cut[direction] = slice(2, None)
    return (padded[tuple(high_cut)] - padded[tuple(low_cut)]) * 0.5


def advance_velocity(velocity, stress_pad, buoyancy):
    tension_x = stress_pad[0:1]
    tension_y = stress_pad[1:2]
    tension_z = stress_pad[2:3]
    shear_x = stress_pad[3:4]
    shear_y = stress_pad[4:5]
    shear_z = stress_pad[5:6]
    force_x = central(tension_x, 1) + central(shear_z, 2) + central(shear_y, 3)
    force_y = central(shear_z, 1) + central(tension_y, 2) + central(shear_x, 3)
    force_z = central(shear_y, 1) + central(shear_x, 2) + central(tension_z, 3)
    forces = jnp.concatenate([force_x, force_y, force_z], axis=0)
    return velocity + TIME_STEP * (buoyancy * forces)


def advance_stress(stress, velocity_pad, lame_first, lame_second):
    speed_x = velocity_pad[0:1]
    speed_y = velocity_pad[1:2]
    speed_z = velocity_pad[2:3]
    strain_x = central(speed_x, 1)
    strain_y = central(speed_y, 2)
    strain_z = central(speed_z, 3)
    twist_x = (central(speed_y, 3) + central(speed_z, 2)) * 0.5
    twist_y = (central(speed_x, 3) + central(speed_z, 1)) * 0.5
    twist_z = (central(speed_x, 2) + central(speed_y, 1)) * 0.5
    volume = strain_x + strain_y + strain_z
    bulk_term = lame_first * volume
    double = 2.0 * lame_second
    change = jnp.concatenate([bulk_term + double * strain_x, bulk_term + double * strain_y,
                              bulk_term + double * strain_z, double * twist_x,
                              double * twist_y, double * twist_z], axis=0)
    return stress + TIME_STEP * change


def eliminate(spread, forcing, incoming):
    def one_row(state_next, row_pair):
        weight_next, offset_next = state_next
        spread_row, forcing_row = row_pair
        denominator = 1.0 + 2.0 * spread_row - spread_row * weight_next
        weight_here = spread_row / denominator
        offset_here = (forcing_row + spread_row * offset_next) / denominator
        return (weight_here, offset_here), (weight_here, offset_here)

    outgoing, (weights, offsets) = lax.scan(one_row, incoming, (spread, forcing), reverse=True)
    return outgoing, weights, offsets


def substitute(weights, offsets, before):
    def one_row(previous, row_pair):
        weight_row, offset_row = row_pair
        solved = offset_row + weight_row * previous
        return solved, solved

    final_value, values = lax.scan(one_row, before, (weights, offsets))
    return values


def reference(velocity, stress, material, properties, owner_map, cell_map, height, current, sea_depth, wet_mask):
    lame_first = properties[:, 0][material][None]
    lame_second = properties[:, 1][material][None]
    buoyancy = properties[:, 2][material][None]
    widths = ((0, 0), (1, 1), (1, 1), (1, 1))
    lift = jnp.zeros((NX, NY), jnp.float32)
    for substep in range(SUBSTEPS):
        velocity = advance_velocity(velocity, jnp.pad(stress, widths), buoyancy)
        stress = advance_stress(stress, jnp.pad(velocity, widths), lame_first, lame_second)
        lift = lift - TIME_STEP * velocity[2, :, :, 0]
    tile_count = N_GX * N_GY
    lift_tiles = lift.reshape(N_GX, CX, N_GY, CY).transpose(0, 2, 1, 3).reshape(tile_count, CX * CY)
    target = owner_map[:, :, 0]
    longitude = (target // (N_GY * N_GZ)) * OL + cell_map // OR
    latitude = (target % (N_GY * N_GZ)) * OR + cell_map % OR
    flat_index = (longitude * OLAT + latitude).reshape(-1).astype(jnp.int32)
    source = jnp.zeros((OLON * OLAT,), jnp.float32).at[flat_index].add(lift_tiles.reshape(-1))
    source = source.reshape(OLON, OLAT)
    wet_float = wet_mask.astype(jnp.float32)
    height_out = wet_float * (height + source)
    beyond = jnp.concatenate([height_out[1:], jnp.zeros((1, OLAT), jnp.float32)], axis=0)
    forcing = -GRAV_STEP * (beyond - height_out)
    spread = sea_depth * sea_depth / 3.0
    empty_row = jnp.zeros((OLAT,), jnp.float32)
    edge_state, weights, offsets = eliminate(spread, forcing, (empty_row, empty_row))
    increment = substitute(weights, offsets, empty_row)
    current_out = wet_float * (current + increment)
    return velocity, stress, height_out, current_out
```

```python
import functools

import jax
import jax.numpy as jnp
from jax import lax
from jax.experimental import pallas as pl
from jax.experimental.pallas import tpu as pltpu
from jax.sharding import PartitionSpec as P

F32 = jnp.float32
CX, CY, CZ = 16, 32, 256
LAT = 128
LON = 32
NB = 8
SX, SY, SZ = (0, 5, 4), (5, 1, 3), (4, 3, 2)
VA = (0, 1, 2)
XF = 3 * 2 * CY
OCR = 80
XR = XF + OCR
YR = 3 * 2 * CX
ZR = 3 * CX * CY
HIGH = lax.Precision.HIGHEST
VM = pl.BlockSpec(memory_space=pltpu.VMEM)
SM = pl.BlockSpec(memory_space=pltpu.SMEM)


def iotas():
    return (
        lax.broadcasted_iota(jnp.int32, (8, 128), 0),
        lax.broadcasted_iota(jnp.int32, (8, 128), 1),
    )


def tile(ref, c, x, t, h):
    return ref[c, x, t * 8 : t * 8 + 8, h * 128 : h * 128 + 128]


def call(body, outs, *args, scratch=(), limit=40):
    return pl.pallas_call(
        body,
        out_shape=outs,
        in_specs=[SM] + [VM] * (len(args) - 1),
        out_specs=[VM] * len(outs),
        scratch_shapes=list(scratch),
        compiler_params=pltpu.CompilerParams(vmem_limit_bytes=limit * 1024 * 1024),
    )(*args)


def shape(*dims):
    return jax.ShapeDtypeStruct(dims, F32)


PAYLOAD = [shape(XR, 128), shape(XR, 128), shape(YR, 128), shape(YR, 128)]


def put_x_faces(ref, comps, pxu, pxd):
    for i, c in enumerate(comps):
        for h in range(2):
            rows = slice(i * 64 + h * 32, i * 64 + h * 32 + 32)
            lanes = slice(h * 128, h * 128 + 128)
            pxu[rows, :] = ref[c, CX - 1, :, lanes]
            pxd[rows, :] = ref[c, 0, :, lanes]


def put_yz(gz, x, i, tiles, pyu, pyd, pz):
    for h in range(2):
        pyu[pl.ds(i * 32 + h * 16 + x, 1), :] = tiles[3][h][7:8, :]
        pyd[pl.ds(i * 32 + h * 16 + x, 1), :] = tiles[0][h][0:1, :]
    put_z(gz, x, i, tiles, pz)


def put_y(x, i, tiles, pyu, pyd):
    for h in range(2):
        pyu[pl.ds(i * 32 + h * 16 + x, 1), :] = tiles[3][h][7:8, :]
        pyd[pl.ds(i * 32 + h * 16 + x, 1), :] = tiles[0][h][0:1, :]


def put_z(gz, x, i, tiles, pz):
    for t in range(4):
        row = pl.multiple_of(i * 512 + x * 32 + t * 8, 8)
        pz[pl.ds(row, 8), :] = jnp.where(gz == 0, tiles[t][1], tiles[t][0])


def prepare(pos, s, depth, height, wet, pxu, pxd, pyu, pyd, pz, fac, rows):
    gz = pos[2]
    put_x_faces(s, SX, pxu, pxd)

    def plane(x, carry):
        for i, c in enumerate(SY):
            put_y(x, i, [[tile(s, c, x, t, h) for h in range(2)] for t in range(4)], pyu, pyd)
        for i, c in enumerate(SZ):
            put_z(gz, x, i, [[tile(s, c, x, t, h) for h in range(2)] for t in range(4)], pz)
        return carry

    lax.fori_loop(0, CX, plane, 0)
    factor(depth, height, wet, pxu, fac, rows)
    pxd[XF:, :] = pxu[XF:, :]


def factor(depth, height, wet, pxu, fac, rows):
    spread = depth[...] * depth[...] / 3.0
    rows[0:32, :] = spread
    w = [None] * LON
    inv = [None] * LON
    right = [None] * LON
    after = jnp.zeros((1, LAT), F32)
    link = jnp.ones((1, LAT), F32)
    for j in reversed(range(LON)):
        sp = rows[j : j + 1, :]
        inv[j] = 1.0 / (1.0 + 2.0 * sp - sp * after)
        w[j] = after = sp * inv[j]
        right[j] = link = w[j] * link
    left_run = jnp.ones((1, LAT), F32)
    right_run = jnp.zeros((1, LAT), F32)
    past = jnp.zeros((1, LAT), F32)
    weight = [None] * LON
    weight[LON - 1] = jnp.ones((1, LAT), F32)
    for j in reversed(range(LON - 1)):
        weight[j] = w[j + 1] * weight[j + 1]
    total = jnp.zeros((1, LAT), F32)
    p_before = q_before = jnp.zeros((1, LAT), F32)
    for j in range(LON):
        p_now = left_run * inv[j]
        total = weight[j] + (w[j - 1] * total if j else 0.0)
        q_now = inv[j] * total
        left_run = w[j] * left_run
        right_run = right[j] + w[j] * right_run
        fac[j : j + 1, :] = left_run
        fac[32 + j : 33 + j, :] = right_run
        fac[64 + j : 65 + j, :] = w[j]
        fac[96 + j : 97 + j, :] = inv[j]
        rows[j : j + 1, :] = p_now - p_before
        rows[32 + j : 33 + j, :] = q_now - q_before
        p_before, q_before = p_now, q_now
    wet_float = wet[...].astype(F32)
    high = height[...]
    a1 = 400.0 * rows[0:32, :] * wet_float
    a2 = 400.0 * rows[32:64, :] * wet_float
    pxu[XF : XF + 32, :] = a1
    pxu[XF + 32 : XF + 64, :] = a2
    base = XF + 64
    pxu[base : base + 1, :] = jnp.sum(a1 * high, axis=0, keepdims=True)
    pxu[base + 1 : base + 2, :] = jnp.sum(a2 * high, axis=0, keepdims=True)
    pxu[base + 2 : base + 3, :] = fac[0:1, :]
    pxu[base + 3 : base + 4, :] = fac[31:32, :]
    pxu[base + 4 : base + 5, :] = fac[32:33, :]
    pxu[base + 5 : base + 6, :] = fac[63:64, :]
    pxu[base + 6 : base + 7, :] = -400.0 * p_before
    pxu[base + 7 : base + 8, :] = -400.0 * q_before
    pxu[base + 8 : base + 9, :] = wet_float[0:1, :]
    pxu[base + 9 : base + 10, :] = wet_float[0:1, :] * high[0:1, :]
    pxu[base + 10 : base + 16, :] = jnp.zeros((6, LAT), F32)


def differences(pos, src, comps, xdn, xup, ydn, yup, zs):
    gx, gy, gz = pos[0], pos[1], pos[2]
    sub, lane = iotas()
    cx, cy, cz = comps
    zero = jnp.zeros((8, 128), F32)

    def flag(cond):
        return jnp.where(cond, 1.0, 0.0).astype(F32)

    m_xd, m_xu = flag(gx > 0), flag(gx < NB - 1)
    m_yd, m_yu = flag(gy > 0), flag(gy < NB - 1)
    m_zd, m_zu = flag(gz == 1), flag(gz == 0)
    top, bottom = sub == 7, sub == 0
    far, near = lane == 127, lane == 0

    def halo_x(ref, mask, i, t, h):
        row = i * 64 + h * 32 + t * 8
        return ref[row : row + 8, :] * mask

    def dx(x, i, t, h, place):
        c = cx[i]
        low = halo_x(xdn, m_xd, i, t, h) if place == "first" else tile(src, c, x - 1, t, h)
        high = halo_x(xup, m_xu, i, t, h) if place == "last" else tile(src, c, x + 1, t, h)
        return high - low

    def dy(x, i, tiles):
        out = [[None, None] for _ in range(4)]
        for h in range(2):
            up = [pltpu.roll(tiles[t][h], 7, 0) for t in range(4)]
            dn = [pltpu.roll(tiles[t][h], 1, 0) for t in range(4)]
            row = i * 32 + h * 16 + x
            up.append(jnp.broadcast_to(yup[pl.ds(row, 1), :] * m_yu, (8, 128)))
            dn.insert(0, jnp.broadcast_to(ydn[pl.ds(row, 1), :] * m_yd, (8, 128)))
            for t in range(4):
                out[t][h] = jnp.where(top, up[t + 1], up[t]) - jnp.where(bottom, dn[t], dn[t + 1])
        return out

    def dz(x, i, tiles):
        out = [[None, None] for _ in range(4)]
        for t in range(4):
            row = pl.multiple_of(i * 512 + x * 32 + t * 8, 8)
            slab = zs[pl.ds(row, 8), :]
            up = [pltpu.roll(tiles[t][h], 127, 1) for h in range(2)] + [pltpu.roll(slab, 127, 1) * m_zu]
            dn = [pltpu.roll(slab, 1, 1) * m_zd] + [pltpu.roll(tiles[t][h], 1, 1) for h in range(2)]
            for h in range(2):
                out[t][h] = jnp.where(far, up[h + 1], up[h]) - jnp.where(near, dn[h], dn[h + 1])
        return out

    return dx, dy, dz


def planes(body):
    body(0, "first")
    lax.fori_loop(1, CX - 1, lambda x, carry: (body(x, "inner"), carry)[1], 0)
    body(CX - 1, "last")


def grab(ref, c, x):
    return [[tile(ref, c, x, t, h) for h in range(2)] for t in range(4)]


def gather(table, index):
    return jnp.take_along_axis(table, index, axis=1, mode="promise_in_bounds")


def move(has_lift, pos, v, s, mat, tab, xdn, xup, ydn, yup, zs, *refs):
    if has_lift:
        lift_in, vo, pxu, pxd, pyu, pyd, pz = refs
    else:
        vo, pxu, pxd, pyu, pyd, pz, lift_out = refs
    gz = pos[2]
    sub, lane = iotas()
    dx, dy, dz = differences(pos, s, (SX, SY, SZ), xdn, xup, ydn, yup, zs)
    buoy = tab[0:8, :]
    lift_rows = (lambda t: slice(ZR + t * 8, ZR + t * 8 + 8)) if has_lift else (lambda t: slice(t * 8, t * 8 + 8))
    lift_ref = pz if has_lift else lift_out
    for t in range(4):
        lift_ref[lift_rows(t), :] = lift_in[t * 8 : t * 8 + 8, :] if has_lift else jnp.zeros((8, 128), F32)

    def plane(x, place):
        weight = [
            [gather(buoy, mat[x, t * 8 : t * 8 + 8, h * 128 : h * 128 + 128]) for h in range(2)]
            for t in range(4)
        ]
        for i in range(3):
            ey = dy(x, i, grab(s, SY[i], x))
            ez = dz(x, i, grab(s, SZ[i], x))
            new = [[None, None] for _ in range(4)]
            for t in range(4):
                for h in range(2):
                    force = dx(x, i, t, h, place) + ey[t][h] + ez[t][h]
                    new[t][h] = tile(v, i, x, t, h) + weight[t][h] * force
                    vo[i, x, t * 8 : t * 8 + 8, h * 128 : h * 128 + 128] = new[t][h]
            put_yz(gz, x, i, new, pyu, pyd, pz)
            if i == 2:
                for t in range(4):
                    old = lift_ref[lift_rows(t), :]
                    column = pltpu.roll(new[t][0], x, 1)
                    lift_ref[lift_rows(t), :] = jnp.where(lane == x, old - 0.25 * column, old)

    planes(plane)
    put_x_faces(vo, VA, pxu, pxd)
    pxu[XF:, :] = xdn[XF:, :]
    pxd[XF:, :] = xup[XF:, :]


def strain(last, pos, s, v, mat, tab, xdn, xup, ydn, yup, zs, *refs):
    if last:
        (so,) = refs
    else:
        so, pxu, pxd, pyu, pyd, pz = refs
    gz = pos[2]
    dx, dy, dz = differences(pos, v, (VA, VA, VA), xdn, xup, ydn, yup, zs)
    first8, second8 = tab[8:16, :], tab[16:24, :]

    def plane(x, place):
        vel = [grab(v, c, x) for c in range(3)]
        ey = [dy(x, c, vel[c]) for c in range(3)]
        ez = [dz(x, c, vel[c]) for c in range(3)]
        new = [[[None, None] for _ in range(4)] for _ in range(6)]
        for t in range(4):
            for h in range(2):
                ex = [dx(x, c, t, h, place) for c in range(3)]
                index = mat[x, t * 8 : t * 8 + 8, h * 128 : h * 128 + 128]
                mu = gather(second8, index)
                bulk = gather(first8, index) * (ex[0] + ey[1][t][h] + ez[2][t][h])
                mu2 = mu + mu
                change = (
                    bulk + mu2 * ex[0],
                    bulk + mu2 * ey[1][t][h],
                    bulk + mu2 * ez[2][t][h],
                    mu * (ez[1][t][h] + ey[2][t][h]),
                    mu * (ez[0][t][h] + ex[2]),
                    mu * (ey[0][t][h] + ex[1]),
                )
                for c in range(6):
                    new[c][t][h] = tile(s, c, x, t, h) + change[c]
                    so[c, x, t * 8 : t * 8 + 8, h * 128 : h * 128 + 128] = new[c][t][h]
        if not last:
            for i in range(3):
                put_y(x, i, new[SY[i]], pyu, pyd)
                put_z(gz, x, i, new[SZ[i]], pz)

    planes(plane)
    if not last:
        put_x_faces(so, SX, pxu, pxd)
        pxu[XF:, :] = xdn[XF:, :]
        pxd[XF:, :] = xup[XF:, :]


def as_column(row, sub, lane):
    parts = []
    for i in range(4):
        part = jnp.broadcast_to(row[:, i * 128 : i * 128 + 128], (128, 128))
        parts.append(jnp.sum(jnp.where(sub == lane, part, 0.0), axis=1, keepdims=True))
    return jnp.concatenate(parts, axis=0)


def address(pos, owner, cell, group, slot, code):
    gz = pos[2]
    sub = lax.broadcasted_iota(jnp.int32, (128, 128), 0)
    lane = lax.broadcasted_iota(jnp.int32, (128, 128), 1)
    own = owner[...]
    column = as_column(own.astype(F32), sub, lane).astype(jnp.int32)
    cells = as_column(cell[...].astype(F32) + 1.0, sub, lane)
    wide = lax.broadcasted_iota(jnp.int32, (512, 128), 1)
    same = (jnp.broadcast_to(column, (512, 128)) == wide).astype(F32)
    earlier = (
        lax.broadcasted_iota(jnp.int32, (512, 512), 1) < lax.broadcasted_iota(jnp.int32, (512, 512), 0)
    ).astype(F32)
    before = jnp.dot(earlier, same, preferred_element_type=F32)
    position = jnp.sum(same * before, axis=1, keepdims=True).astype(jnp.int32)
    place = (column >> 4) * 8 + position
    taken = (jnp.broadcast_to(place, (512, 128)) == wide).astype(F32)
    slot[...] = taken
    rows = lax.broadcasted_iota(jnp.int32, (8, 512), 0)
    mine = jnp.broadcast_to(own, (8, 512))
    chosen = ((((mine >> 1) & 7) == rows) & ((mine & 1) == gz)).astype(F32)
    group[...] = chosen
    found = jnp.dot(chosen, taken * cells, precision=HIGH, preferred_element_type=F32)
    code[...] = pltpu.roll(found, 64, 1)


def pack_lift(pos, pz, zs, group, slot, code, out, wide):
    lift = jnp.where(pos[2] == 0, pz[ZR:, :], zs[ZR:, :])
    for x in range(CX):
        rows = slice(x * 32, x * 32 + 32)
        wide[rows, :] = slot[rows, :] * jnp.broadcast_to(lift[:, x : x + 1], (32, 128))
    row = jnp.dot(group[...], wide[...], precision=HIGH, preferred_element_type=F32) + code[...]
    for i in range(8):
        out[i * 8 : i * 8 + 8, :] = row


def ocean(pos, arrived, height, current, wet, fac, own, d1, u1, d2, u2, d3, u3, d4, ho, co, oc, hot, val, pair, src, ends, sweep):
    gx = pos[0]
    b16 = jnp.bfloat16
    lane = lax.broadcasted_iota(jnp.int32, (32, 128), 1)
    half = lane < 64
    one, two = arrived[0:32, :], arrived[32:64, :]
    value = jnp.where(half, one, pltpu.roll(two, 64, 1))
    cell = jnp.where(half, pltpu.roll(one, 64, 1), two).astype(jnp.int32) - 1
    band = (lane & 63) >> 3
    pair[0:32, :] = jnp.where(cell >= 0, band * 32 + (cell >> 7), -1)
    pair[32:64, :] = cell & 127
    coarse = value.astype(b16).astype(F32)
    val[0:32, :] = coarse
    val[32:64, :] = value - coarse
    lon_rows = lax.broadcasted_iota(jnp.int32, (256, 128), 0)
    lat_rows = lax.broadcasted_iota(jnp.int32, (128, 128), 0)
    for r in range(32):
        cols = slice(r * 128, r * 128 + 128)
        hot[0:256, cols] = (lon_rows == pair[r : r + 1, :]).astype(F32).astype(b16)
        here = lat_rows == pair[32 + r : 33 + r, :]
        hot[256:384, cols] = jnp.where(here, val[r : r + 1, :], 0.0).astype(b16)
        hot[384:512, cols] = jnp.where(here, val[32 + r : 33 + r, :], 0.0).astype(b16)
    both = lax.dot_general(
        hot[0:256, :], hot[256:512, :], (((1,), (1,)), ((), ())), preferred_element_type=F32
    )
    src[...] = both[:, 0:128] + both[:, 128:256]
    for steps, ref in ((0, own), (1, u1), (2, u2), (3, u3), (4, d4), (5, d3), (6, d2), (7, d1)):
        oc[pl.ds(lax.rem(gx + steps, NB), 1), :, :] = ref[XF:, :][None]
    zero = jnp.zeros((1, LAT), F32)

    def extra(b, k):
        return oc[b, 64 + k : 65 + k, :]

    head = [extra(b, 8) * src[b * 32 : b * 32 + 1, :] + extra(b, 9) for b in range(NB)] + [zero]
    y0, yl = [], []
    for b in range(NB):
        s_b = src[b * 32 : b * 32 + 32, :]
        y0.append(jnp.sum(oc[b, 0:32, :] * s_b, axis=0, keepdims=True) + extra(b, 0) + extra(b, 6) * head[b + 1])
        yl.append(jnp.sum(oc[b, 32:64, :] * s_b, axis=0, keepdims=True) + extra(b, 1) + extra(b, 7) * head[b + 1])
    a = [zero] * (NB + 1)
    m = [zero] * (NB + 1)
    zc = [zero] * NB
    zl = [zero] * NB
    for b in reversed(range(NB)):
        scale = 1.0 / (1.0 - extra(b, 5) * m[b + 1])
        zc[b] = scale * (yl[b] + extra(b, 5) * a[b + 1])
        zl[b] = scale * extra(b, 3)
        a[b] = y0[b] + extra(b, 4) * (a[b + 1] + m[b + 1] * zc[b])
        m[b] = extra(b, 2) + extra(b, 4) * m[b + 1] * zl[b]
    z = zero
    ends[0:1, :] = zero
    ends[16 + NB : 17 + NB, :] = zero
    for b in range(NB):
        ends[16 + b : 17 + b, :] = a[b] + m[b] * z
        z = zc[b] + zl[b] * z
        ends[b + 1 : b + 2, :] = z
    left = ends[pl.ds(gx, 1), :]
    right = ends[pl.ds(gx + 17, 1), :]
    wet_float = wet[...].astype(F32)
    new_height = wet_float * (height[...] + src[pl.ds(pl.multiple_of(gx * 32, 32), 32), :])
    ho[...] = new_height
    sweep[0:32, :] = new_height
    nxt = lax.rem(gx + 1, NB)
    next_head = oc[pl.ds(nxt, 1), 72:73, :][0] * src[pl.ds(nxt * 32, 1), :] + oc[pl.ds(nxt, 1), 73:74, :][0]
    sweep[32:33, :] = jnp.where(gx == NB - 1, 0.0, next_head)
    forced = fac[96:128, :] * (-400.0 * (sweep[1:33, :] - new_height))
    sweep[40:72, :] = forced
    run = zero
    offs = [None] * LON
    for j in reversed(range(LON)):
        offs[j] = run = sweep[40 + j : 41 + j, :] + fac[64 + j : 65 + j, :] * run
    run = zero
    for j in range(LON):
        run = offs[j] + fac[64 + j : 65 + j, :] * run
        sweep[40 + j : 41 + j, :] = run
    increment = sweep[40:72, :] + fac[0:32, :] * left + fac[32:64, :] * right
    co[...] = wet_float * (current[...] + increment)


def ring(value, axis, step):
    n = lax.axis_size(axis)
    return lax.ppermute(value, axis, [(i, (i + step) % n) for i in range(n)])


def exchange(payload):
    pxu, pxd, pyu, pyd, pz = payload
    zs = ring(pz, "gz", 1)
    xdn, xup = ring(pxu, "gx", 1), ring(pxd, "gx", -1)
    ydn, yup = ring(pyu, "gy", 1), ring(pyd, "gy", -1)
    return xdn, xup, ydn, yup, zs


def local(velocity, stress, material, properties, owner_map, cell_map, height, current, sea_depth, wet_mask):
    pos = jnp.stack([lax.axis_index(a) for a in ("gx", "gy", "gz")]).astype(jnp.int32)
    scaled = 0.125 * properties.T
    tab = jnp.pad(jnp.concatenate([scaled[2:3], scaled[0:1], scaled[1:2]]), ((0, 0), (0, 112)))
    tab = jnp.repeat(tab, 8, axis=0)
    tile_here = pos[0] * NB + pos[1]
    owner = lax.dynamic_slice_in_dim(owner_map[:, :, 0], tile_here, 1, 0)
    cell = lax.dynamic_slice_in_dim(cell_map, tile_here, 1, 0)

    pz_shape, pz_lift = shape(ZR, 128), shape(ZR + 32, 128)
    v_shape, s_shape = shape(3, CX, CY, CZ), shape(6, CX, CY, CZ)
    *first, fac = call(
        prepare,
        PAYLOAD + [pz_shape, shape(128, LAT)],
        pos, stress, sea_depth, height, wet_mask,
        scratch=[pltpu.VMEM((64, LAT), F32)],
    )
    group, slot, code = call(address, [shape(8, 512), shape(512, 128), shape(8, 128)], pos, owner, cell)
    r1 = exchange(first)
    v1, *sent, lift = call(
        functools.partial(move, False),
        [v_shape] + PAYLOAD + [pz_shape, shape(32, 128)],
        pos, velocity, stress, material, tab, *r1,
    )
    r2 = exchange(sent)
    s1, *sent = call(
        functools.partial(strain, False),
        [s_shape] + PAYLOAD + [pz_shape],
        pos, stress, v1, material, tab, *r2,
    )
    r3 = exchange(sent)
    v2, *sent = call(
        functools.partial(move, True),
        [v_shape] + PAYLOAD + [pz_lift],
        pos, v1, s1, material, tab, *r3, lift,
    )
    r4 = exchange(sent)
    (out,) = call(
        pack_lift, [shape(64, 128)], pos, sent[4], r4[4], group, slot, code,
        scratch=[pltpu.VMEM((512, 128), F32)],
    )
    arrived = lax.all_to_all(out, ("gx", "gy"), split_axis=0, concat_axis=0, tiled=True)
    (s2,) = call(
        functools.partial(strain, True), [s_shape], pos, s1, v2, material, tab, *r4
    )
    height_out, current_out = call(
        ocean, [shape(LON, LAT)] * 2,
        pos, arrived, height, current, wet_mask, fac, first[0],
        r1[0], r1[1], r2[0], r2[1], r3[0], r3[1], r4[0],
        scratch=[
            pltpu.VMEM((NB, OCR, LAT), F32),
            pltpu.VMEM((512, 4096), jnp.bfloat16),
            pltpu.VMEM((64, 128), F32),
            pltpu.VMEM((64, 128), jnp.int32),
            pltpu.VMEM((256, 128), F32),
            pltpu.VMEM((32, 128), F32),
            pltpu.VMEM((72, 128), F32),
        ],
    )
    return v2, s2, height_out, current_out


def solution(mesh):
    return jax.shard_map(
        local,
        mesh=mesh,
        in_specs=(
            P(None, "gx", "gy", "gz"),
            P(None, "gx", "gy", "gz"),
            P("gx", "gy", "gz"),
            P(),
            P(),
            P(),
            P("gx", ("gy", "gz")),
            P("gx", ("gy", "gz")),
            P("gx", ("gy", "gz")),
            P("gx", ("gy", "gz")),
        ),
        out_specs=(
            P(None, "gx", "gy", "gz"),
            P(None, "gx", "gy", "gz"),
            P("gx", ("gy", "gz")),
            P("gx", ("gy", "gz")),
        ),
        check_vma=False,
    )
```

```python
import functools

import jax
import jax.numpy as jnp
from jax import lax
from jax.experimental import pallas as pl
from jax.experimental.pallas import tpu as pltpu
from jax.sharding import PartitionSpec as P

F32 = jnp.float32
CX, CY, CZ = 16, 32, 256
LAT = 128
LON = 32
NB = 8
SX, SY, SZ = (0, 5, 4), (5, 1, 3), (4, 3, 2)
VA = (0, 1, 2)
XF = 3 * 2 * CY
OCR = 80
XR = XF + OCR
YR = 3 * 2 * CX
FAC = NB * OCR
BAG = FAC + 128
HIGH = lax.Precision.HIGHEST
VM = pl.BlockSpec(memory_space=pltpu.VMEM)
HB = pl.BlockSpec(memory_space=pltpu.HBM)


def iotas():
    return (
        lax.broadcasted_iota(jnp.int32, (8, 128), 0),
        lax.broadcasted_iota(jnp.int32, (8, 128), 1),
    )


def tile(ref, c, x, t, h):
    return ref[c, x, t * 8 : t * 8 + 8, h * 128 : h * 128 + 128]


def call(body, outs, *args, scratch=(), ins=None, outs_at=None, aliases=None, limit=20):
    return pl.pallas_call(
        body,
        out_shape=outs,
        in_specs=[VM] * len(args) if ins is None else ins,
        out_specs=[VM] * len(outs) if outs_at is None else outs_at,
        scratch_shapes=list(scratch),
        input_output_aliases=aliases or {},
        compiler_params=pltpu.CompilerParams(vmem_limit_bytes=limit * 1024 * 1024),
    )(*args)


def place():
    return lax.axis_index("gx"), lax.axis_index("gy"), lax.axis_index("gz")


def shape(*dims):
    return jax.ShapeDtypeStruct(dims, F32)


PARTS = 3
def resident(*dims):
    return pltpu.VMEM(dims, F32)


def outside(*arrays):
    return [pltpu.with_memory_space_constraint(a, pltpu.HBM) for a in arrays]


PAYLOAD = [shape(XR, 128), shape(XR, 128), shape(YR, 128), shape(YR, 128)]


def put_x_faces(ref, comps, pxu, pxd):
    for i, c in enumerate(comps):
        for h in range(2):
            rows = slice(i * 64 + h * 32, i * 64 + h * 32 + 32)
            lanes = slice(h * 128, h * 128 + 128)
            pxu[rows, :] = ref[c, CX - 1, :, lanes]
            pxd[rows, :] = ref[c, 0, :, lanes]


def put_y(x, i, tiles, pyu, pyd):
    for h in range(2):
        row = i * 32 + h * 16 + x
        pyu[row : row + 1, :] = tiles[3][h][7:8, :]
        pyd[row : row + 1, :] = tiles[0][h][0:1, :]


def put_z(gz, x, i, tiles, pz):
    for t in range(4):
        pz[i * CX + x, t * 8 : t * 8 + 8, :] = jnp.where(gz == 0, tiles[t][1], tiles[t][0])


def prepare(s, depth, height, wet, pxu, pxd, pyu, pyd, pz, bag, rows, high, deep, damp, edge, sems):
    gx, _, gz = place()
    copies = []

    def start(src, dst):
        copy = pltpu.make_async_copy(src, dst, sems.at[len(copies)])
        copy.start()
        copies.append(copy)

    start(depth, deep)
    start(height, high)
    start(wet, damp)
    for i, c in enumerate(SX):
        for h in range(2):
            lanes = pl.ds(h * 128, 128)
            start(s.at[c, CX - 1, :, lanes], pxu.at[pl.ds(i * 64 + h * 32, 32), :])
            start(s.at[c, 0, :, lanes], pxd.at[pl.ds(i * 64 + h * 32, 32), :])
    for i, c in enumerate(SY):
        start(s.at[c, :, pl.ds(24, 8), :], edge.at[0, i])
        start(s.at[c, :, pl.ds(0, 8), :], edge.at[1, i])
    lanes = pl.ds(pl.multiple_of(128 * (1 - gz), 128), 128)
    for i, c in enumerate(SZ):
        start(s.at[c, :, :, lanes], pz.at[pl.ds(i * CX, CX)])
    for copy in copies[:3]:
        copy.wait()
    factor(deep, high, damp, pxu, bag, rows)
    pxd[XF:, :] = pxu[XF:, :]
    bag[pl.ds(pl.multiple_of(gx * OCR, 8), OCR), :] = pxu[XF:, :]
    for copy in copies[3:]:
        copy.wait()
    for i in range(3):
        for x in range(CX):
            for h in range(2):
                row = i * 32 + h * 16 + x
                lanes = slice(h * 128, h * 128 + 128)
                pyu[row : row + 1, :] = edge[0, i, x, 7:8, lanes]
                pyd[row : row + 1, :] = edge[1, i, x, 0:1, lanes]


def factor(depth, height, wet, pxu, bag, rows):
    spread = depth[...] * depth[...] / 3.0
    rows[0:32, :] = spread
    w = [None] * LON
    inv = [None] * LON
    right = [None] * LON
    after = jnp.zeros((1, LAT), F32)
    link = jnp.ones((1, LAT), F32)
    for j in reversed(range(LON)):
        sp = rows[j : j + 1, :]
        inv[j] = 1.0 / (1.0 + 2.0 * sp - sp * after)
        w[j] = after = sp * inv[j]
        right[j] = link = w[j] * link
    left_run = jnp.ones((1, LAT), F32)
    right_run = jnp.zeros((1, LAT), F32)
    past = jnp.zeros((1, LAT), F32)
    weight = [None] * LON
    weight[LON - 1] = jnp.ones((1, LAT), F32)
    for j in reversed(range(LON - 1)):
        weight[j] = w[j + 1] * weight[j + 1]
    total = jnp.zeros((1, LAT), F32)
    p_before = q_before = jnp.zeros((1, LAT), F32)
    for j in range(LON):
        p_now = left_run * inv[j]
        total = weight[j] + (w[j - 1] * total if j else 0.0)
        q_now = inv[j] * total
        left_run = w[j] * left_run
        right_run = right[j] + w[j] * right_run
        bag[FAC + j : FAC + j + 1, :] = left_run
        bag[FAC + 32 + j : FAC + 33 + j, :] = right_run
        bag[FAC + 64 + j : FAC + 65 + j, :] = w[j]
        bag[FAC + 96 + j : FAC + 97 + j, :] = inv[j]
        if j == 0:
            first_left, first_right = left_run, right_run
        rows[j : j + 1, :] = p_now - p_before
        rows[32 + j : 33 + j, :] = q_now - q_before
        p_before, q_before = p_now, q_now
    wet_float = wet[...].astype(F32)
    high = height[...]
    a1 = 400.0 * rows[0:32, :] * wet_float
    a2 = 400.0 * rows[32:64, :] * wet_float
    pxu[XF : XF + 32, :] = a1
    pxu[XF + 32 : XF + 64, :] = a2
    base = XF + 64
    pxu[base : base + 1, :] = jnp.sum(a1 * high, axis=0, keepdims=True)
    pxu[base + 1 : base + 2, :] = jnp.sum(a2 * high, axis=0, keepdims=True)
    pxu[base + 2 : base + 3, :] = first_left
    pxu[base + 3 : base + 4, :] = left_run
    pxu[base + 4 : base + 5, :] = first_right
    pxu[base + 5 : base + 6, :] = right_run
    pxu[base + 6 : base + 7, :] = -400.0 * p_before
    pxu[base + 7 : base + 8, :] = -400.0 * q_before
    pxu[base + 8 : base + 9, :] = wet_float[0:1, :]
    pxu[base + 9 : base + 10, :] = wet_float[0:1, :] * high[0:1, :]
    pxu[base + 10 : base + 16, :] = jnp.zeros((6, LAT), F32)


def slopes_z(src, comps, out):
    k = lax.broadcasted_iota(jnp.int32, (CZ, CZ), 0)
    n = lax.broadcasted_iota(jnp.int32, (CZ, CZ), 1)
    step = jnp.where(k == n + 1, 1.0, 0.0) - jnp.where(k == n - 1, 1.0, 0.0)
    step = step.astype(jnp.bfloat16)
    for i, c in enumerate(comps):
        full = src[c].reshape(CX * CY, CZ)
        total = None
        for _ in range(PARTS):
            part = full.astype(jnp.bfloat16)
            full = full - part.astype(F32)
            product = jnp.dot(part, step, preferred_element_type=F32)
            total = product if total is None else total + product
        out[i] = total.reshape(CX, CY, CZ)


def differences(src, comps, dzs, xdn, xup, ydn, yup, zs):
    gx, gy, gz = place()
    sub, lane = iotas()
    cx, cy, cz = comps

    def flag(cond):
        return jnp.where(cond, 1.0, 0.0).astype(F32)

    m_xd, m_xu = flag(gx > 0), flag(gx < NB - 1)
    m_yd, m_yu = flag(gy > 0), flag(gy < NB - 1)
    top, bottom = sub == 7, sub == 0
    far, near = (lane == 127) & (gz == 0), (lane == 0) & (gz == 1)
    shift = jnp.where(gz == 0, 127, 1)

    def halo_x(ref, mask, i, t, h):
        row = i * 64 + h * 32 + t * 8
        return ref[row : row + 8, :] * mask

    def dx(x, i, t, h):
        c = cx[i]
        low = halo_x(xdn, m_xd, i, t, h) if x == 0 else tile(src, c, x - 1, t, h)
        high = halo_x(xup, m_xu, i, t, h) if x == CX - 1 else tile(src, c, x + 1, t, h)
        return high - low

    def dy(x, i, tiles):
        out = [[None, None] for _ in range(4)]
        for h in range(2):
            up = [pltpu.roll(tiles[t][h], 7, 0) for t in range(4)]
            dn = [pltpu.roll(tiles[t][h], 1, 0) for t in range(4)]
            row = i * 32 + h * 16 + x
            up.append(jnp.broadcast_to(yup[row : row + 1, :] * m_yu, (8, 128)))
            dn.insert(0, jnp.broadcast_to(ydn[row : row + 1, :] * m_yd, (8, 128)))
            for t in range(4):
                out[t][h] = jnp.where(top, up[t + 1], up[t]) - jnp.where(bottom, dn[t], dn[t + 1])
        return out

    def dz(x, i):
        out = [[None, None] for _ in range(4)]
        for t in range(4):
            slab = pltpu.roll(zs[i * CX + x, t * 8 : t * 8 + 8, :], shift, 1)
            out[t][0] = tile(dzs, i, x, t, 0) - jnp.where(near, slab, 0.0)
            out[t][1] = tile(dzs, i, x, t, 1) + jnp.where(far, slab, 0.0)
        return out

    return dx, dy, dz


def grab(ref, c, x):
    return [[tile(ref, c, x, t, h) for h in range(2)] for t in range(4)]


def lookup(tab, mat, coef, rows):
    table = [tab[i * 8 : i * 8 + 8, :] for i in rows]

    def plane(x, carry):
        for t in range(4):
            for h in range(2):
                index = mat[x, t * 8 : t * 8 + 8, h * 128 : h * 128 + 128]
                for i in range(len(rows)):
                    coef[i, x, t * 8 : t * 8 + 8, h * 128 : h * 128 + 128] = jnp.take_along_axis(
                        table[i], index, axis=1, mode="promise_in_bounds"
                    )
        return carry

    lax.fori_loop(0, CX, plane, 0)


def fetch(v_hbm, s_hbm, mat_hbm, tab, v, s, mat, coef, sems):
    copies = [
        pltpu.make_async_copy(a, b, sems.at[i])
        for i, (a, b) in enumerate(((mat_hbm, mat), (s_hbm, s), (v_hbm, v)))
    ]
    for copy in copies:
        copy.start()
    copies[0].wait()
    lookup(tab, mat, coef, (0,))
    copies[1].wait()
    copies[2].wait()


def lame(tab, mat, coef):
    lookup(tab, mat, coef, (1, 2))


def collect(distance, xdn, xup, bag):
    gx = lax.axis_index("gx")
    for ref, steps in ((xdn, NB - distance), (xup, distance)):
        row = pl.multiple_of(lax.rem(gx + steps, NB) * OCR, 8)
        bag[pl.ds(row, OCR), :] = ref[XF:, :]


def move(distance, has_lift, v, s, coef, xdn, xup, ydn, yup, zs, bag_in, *refs):
    if has_lift:
        lift_in, vo, pxu, pxd, pyu, pyd, pz, lift_out, bag, dzs = refs
    else:
        vo, pxu, pxd, pyu, pyd, pz, lift_out, bag, dzs = refs
    gz = lax.axis_index("gz")
    sub, lane = iotas()
    collect(distance, xdn, xup, bag)
    slopes_z(s, SZ, dzs)
    dx, dy, dz = differences(s, (SX, SY, SZ), dzs, xdn, xup, ydn, yup, zs)
    lift = [lift_in[t * 8 : t * 8 + 8, :] if has_lift else jnp.zeros((8, 128), F32) for t in range(4)]
    for x in range(CX):
        for i in range(3):
            ey = dy(x, i, grab(s, SY[i], x))
            ez = dz(x, i)
            new = [[None, None] for _ in range(4)]
            for t in range(4):
                for h in range(2):
                    force = dx(x, i, t, h) + ey[t][h] + ez[t][h]
                    new[t][h] = tile(v, i, x, t, h) + tile(coef, 0, x, t, h) * force
                    vo[i, x, t * 8 : t * 8 + 8, h * 128 : h * 128 + 128] = new[t][h]
            put_y(x, i, new, pyu, pyd)
            put_z(gz, x, i, new, pz)
        for t in range(4):
            lift[t] = jnp.where(lane == x, lift[t] - 0.25 * pltpu.roll(new[t][0], x, 1), lift[t])
    for t in range(4):
        lift_out[t * 8 : t * 8 + 8, :] = lift[t]
        if has_lift:
            pz[3 * CX, t * 8 : t * 8 + 8, :] = lift[t]
    put_x_faces(vo, VA, pxu, pxd)
    pxu[XF:, :] = xdn[XF:, :]
    pxd[XF:, :] = xup[XF:, :]


def strain(distance, last, s, v, coef, xdn, xup, ydn, yup, zs, *refs):
    if last:
        bag, lift, group, slot, code, v_hbm, s_hbm, out_hbm, bag_hbm, far_hbm, so, dzs, out, wide, sems = refs
        copies = [
            pltpu.make_async_copy(v, v_hbm, sems.at[CX]),
            pltpu.make_async_copy(bag, bag_hbm, sems.at[CX + 1]),
            pltpu.make_async_copy(xdn.at[pl.ds(XF, OCR), :], far_hbm, sems.at[CX + 2]),
            pltpu.make_async_copy(out, out_hbm, sems.at[CX + 3]),
        ]
        pack_lift(jnp.where(lax.axis_index("gz") == 0, lift[...], zs[3 * CX]), group, slot, code, out, wide)
        for copy in copies:
            copy.start()
    else:
        bag_in, so, pxu, pxd, pyu, pyd, pz, bag, dzs = refs
        collect(distance, xdn, xup, bag)
    gz = lax.axis_index("gz")
    slopes_z(v, VA, dzs)
    dx, dy, dz = differences(v, (VA, VA, VA), dzs, xdn, xup, ydn, yup, zs)
    for x in range(CX):
        ey = [dy(x, c, grab(v, c, x)) for c in range(3)]
        ez = [dz(x, c) for c in range(3)]
        new = [[[None, None] for _ in range(4)] for _ in range(6)]
        for t in range(4):
            for h in range(2):
                ex = [dx(x, c, t, h) for c in range(3)]
                mu = tile(coef, 1, x, t, h)
                bulk = tile(coef, 0, x, t, h) * (ex[0] + ey[1][t][h] + ez[2][t][h])
                mu2 = mu + mu
                change = (
                    bulk + mu2 * ex[0],
                    bulk + mu2 * ey[1][t][h],
                    bulk + mu2 * ez[2][t][h],
                    mu * (ez[1][t][h] + ey[2][t][h]),
                    mu * (ez[0][t][h] + ex[2]),
                    mu * (ey[0][t][h] + ex[1]),
                )
                for c in range(6):
                    new[c][t][h] = tile(s, c, x, t, h) + change[c]
                    so[c, x, t * 8 : t * 8 + 8, h * 128 : h * 128 + 128] = new[c][t][h]
        if last:
            copies.append(pltpu.make_async_copy(so.at[:, x], s_hbm.at[:, x], sems.at[x]))
            copies[-1].start()
        else:
            for i in range(3):
                put_y(x, i, new[SY[i]], pyu, pyd)
                put_z(gz, x, i, new[SZ[i]], pz)
    if last:
        for copy in copies:
            copy.wait()
    else:
        put_x_faces(so, SX, pxu, pxd)
        pxu[XF:, :] = xdn[XF:, :]
        pxd[XF:, :] = xup[XF:, :]


def as_column(row, sub, lane):
    parts = []
    for i in range(4):
        part = jnp.broadcast_to(row[:, i * 128 : i * 128 + 128], (128, 128))
        parts.append(jnp.sum(jnp.where(sub == lane, part, 0.0), axis=1, keepdims=True))
    return jnp.concatenate(parts, axis=0)


def address(owners, cell_rows, group, slot, code, owner, cell, sems):
    gx, gy, gz = place()
    copies = [
        pltpu.make_async_copy(owners.at[gx * NB + gy], owner, sems.at[0]),
        pltpu.make_async_copy(cell_rows.at[pl.ds(pl.multiple_of(gx * NB, 8), 8), :], cell, sems.at[1]),
    ]
    for copy in copies:
        copy.start()
    for copy in copies:
        copy.wait()
    sub = lax.broadcasted_iota(jnp.int32, (128, 128), 0)
    lane = lax.broadcasted_iota(jnp.int32, (128, 128), 1)
    own = owner[...]
    column = as_column(own.astype(F32), sub, lane).astype(jnp.int32)
    cells = as_column(cell[pl.ds(gy, 1), :].astype(F32) + 1.0, sub, lane)
    wide = lax.broadcasted_iota(jnp.int32, (512, 128), 1)
    same = (jnp.broadcast_to(column, (512, 128)) == wide).astype(F32)
    earlier = (
        lax.broadcasted_iota(jnp.int32, (512, 512), 1) < lax.broadcasted_iota(jnp.int32, (512, 512), 0)
    ).astype(F32)
    before = jnp.dot(earlier, same, preferred_element_type=F32)
    position = jnp.sum(same * before, axis=1, keepdims=True).astype(jnp.int32)
    spot = (column >> 4) * 8 + position
    taken = (jnp.broadcast_to(spot, (512, 128)) == wide).astype(F32)
    slot[...] = taken
    rows = lax.broadcasted_iota(jnp.int32, (8, 512), 0)
    mine = jnp.broadcast_to(own, (8, 512))
    chosen = ((((mine >> 1) & 7) == rows) & ((mine & 1) == gz)).astype(F32)
    group[...] = chosen
    found = jnp.dot(chosen, taken * cells, precision=HIGH, preferred_element_type=F32)
    code[...] = pltpu.roll(found, 64, 1)


def pack_lift(lift, group, slot, code, out, wide):
    for x in range(CX):
        rows = slice(x * 32, x * 32 + 32)
        wide[rows, :] = slot[rows, :] * jnp.broadcast_to(lift[:, x : x + 1], (32, 128))
    row = jnp.dot(group[...], wide[...], precision=HIGH, preferred_element_type=F32) + code[...]
    for i in range(8):
        out[i * 8 : i * 8 + 8, :] = row


def ocean(arrived_in, far_in, bag_in, height_in, current_in, wet_in, ho, co, arrived, far, bag, height, current, wet, hot, val, pair, src, ends, sweep, sems):
    gx = lax.axis_index("gx")
    copies = [
        pltpu.make_async_copy(a, b, sems.at[i])
        for i, (a, b) in enumerate(
            (
                (arrived_in, arrived),
                (far_in, far),
                (bag_in, bag),
                (height_in, height),
                (current_in, current),
                (wet_in, wet),
            )
        )
    ]
    for copy in copies:
        copy.start()
    copies[0].wait()
    b16 = jnp.bfloat16
    lane = lax.broadcasted_iota(jnp.int32, (32, 128), 1)
    half = lane < 64
    one, two = arrived[0:32, :], arrived[32:64, :]
    value = jnp.where(half, one, pltpu.roll(two, 64, 1))
    cell = jnp.where(half, pltpu.roll(one, 64, 1), two).astype(jnp.int32) - 1
    band = (lane & 63) >> 3
    pair[0:32, :] = jnp.where(cell >= 0, band * 32 + (cell >> 7), -1)
    pair[32:64, :] = cell & 127
    coarse = value.astype(b16).astype(F32)
    val[0:32, :] = coarse
    val[32:64, :] = value - coarse
    lon_rows = lax.broadcasted_iota(jnp.int32, (256, 128), 0)
    lat_rows = lax.broadcasted_iota(jnp.int32, (128, 128), 0)
    for r in range(32):
        cols = slice(r * 128, r * 128 + 128)
        hot[0:256, cols] = (lon_rows == pair[r : r + 1, :]).astype(F32).astype(b16)
        here = lat_rows == pair[32 + r : 33 + r, :]
        hot[256:384, cols] = jnp.where(here, val[r : r + 1, :], 0.0).astype(b16)
        hot[384:512, cols] = jnp.where(here, val[32 + r : 33 + r, :], 0.0).astype(b16)
    both = lax.dot_general(
        hot[0:256, :], hot[256:512, :], (((1,), (1,)), ((), ())), preferred_element_type=F32
    )
    src[...] = both[:, 0:128] + both[:, 128:256]
    for copy in copies[1:]:
        copy.wait()
    opposite = lax.rem(gx + 4, NB) * OCR
    bag_rows = lambda b, k, n: jnp.where(opposite == b * OCR, far[k : k + n, :], bag[b * OCR + k : b * OCR + k + n, :])
    zero = jnp.zeros((1, LAT), F32)

    def extra(b, k):
        return bag_rows(b, 64 + k, 1)

    head = [extra(b, 8) * src[b * 32 : b * 32 + 1, :] + extra(b, 9) for b in range(NB)] + [zero]
    y0, yl = [], []
    for b in range(NB):
        s_b = src[b * 32 : b * 32 + 32, :]
        y0.append(jnp.sum(bag_rows(b, 0, 32) * s_b, axis=0, keepdims=True) + extra(b, 0) + extra(b, 6) * head[b + 1])
        yl.append(jnp.sum(bag_rows(b, 32, 32) * s_b, axis=0, keepdims=True) + extra(b, 1) + extra(b, 7) * head[b + 1])
    a = [zero] * (NB + 1)
    m = [zero] * (NB + 1)
    zc = [zero] * NB
    zl = [zero] * NB
    for b in reversed(range(NB)):
        scale = 1.0 / (1.0 - extra(b, 5) * m[b + 1])
        zc[b] = scale * (yl[b] + extra(b, 5) * a[b + 1])
        zl[b] = scale * extra(b, 3)
        a[b] = y0[b] + extra(b, 4) * (a[b + 1] + m[b + 1] * zc[b])
        m[b] = extra(b, 2) + extra(b, 4) * m[b + 1] * zl[b]
    z = zero
    ends[0:1, :] = zero
    ends[16 + NB : 17 + NB, :] = zero
    for b in range(NB):
        ends[16 + b : 17 + b, :] = a[b] + m[b] * z
        z = zc[b] + zl[b] * z
        ends[b + 1 : b + 2, :] = z
    left = ends[pl.ds(gx, 1), :]
    right = ends[pl.ds(gx + 17, 1), :]
    wet_float = wet[...].astype(F32)
    new_height = wet_float * (height[...] + src[pl.ds(pl.multiple_of(gx * 32, 32), 32), :])
    ho[...] = new_height
    sweep[0:32, :] = new_height
    nxt = lax.rem(gx + 1, NB)
    next_head = bag[pl.ds(nxt * OCR + 72, 1), :] * src[pl.ds(nxt * 32, 1), :] + bag[pl.ds(nxt * OCR + 73, 1), :]
    sweep[32:33, :] = jnp.where(gx == NB - 1, 0.0, next_head)
    forced = bag[FAC + 96 : FAC + 128, :] * (-400.0 * (sweep[1:33, :] - new_height))
    sweep[40:72, :] = forced
    run = zero
    offs = [None] * LON
    for j in reversed(range(LON)):
        offs[j] = run = sweep[40 + j : 41 + j, :] + bag[FAC + 64 + j : FAC + 65 + j, :] * run
    run = zero
    for j in range(LON):
        run = offs[j] + bag[FAC + 64 + j : FAC + 65 + j, :] * run
        sweep[40 + j : 41 + j, :] = run
    increment = sweep[40:72, :] + bag[FAC : FAC + 32, :] * left + bag[FAC + 32 : FAC + 64, :] * right
    co[...] = wet_float * (current[...] + increment)


def ring(value, axis, step):
    n = lax.axis_size(axis)
    return lax.ppermute(value, axis, [(i, (i + step) % n) for i in range(n)])


def exchange(payload):
    pxu, pxd, pyu, pyd, pz = payload
    zs = ring(pz, "gz", 1)
    xdn, xup = ring(pxu, "gx", 1), ring(pxd, "gx", -1)
    ydn, yup = ring(pyu, "gy", 1), ring(pyd, "gy", -1)
    return xdn, xup, ydn, yup, zs


def local(velocity, stress, material, properties, owner_map, cell_map, height, current, sea_depth, wet_mask):
    scaled = 0.125 * properties.T
    tab = jnp.pad(jnp.concatenate([scaled[2:3], scaled[0:1], scaled[1:2]]), ((0, 0), (0, 112)))
    tab = jnp.repeat(tab, 8, axis=0)
    pz_shape, pz_lift = shape(3 * CX, CY, 128), shape(3 * CX + 1, CY, 128)
    v_shape, s_shape = resident(3, CX, CY, CZ), resident(6, CX, CY, CZ)
    bag_shape = shape(BAG, 128)
    plane_z = pltpu.VMEM((3, CX, CY, CZ), F32)
    *sent, bag = call(
        prepare,
        PAYLOAD + [pz_shape, bag_shape],
        *outside(stress, sea_depth, height, wet_mask),
        ins=[HB] * 4,
        scratch=[
            pltpu.VMEM((64, LAT), F32),
            pltpu.VMEM((LON, LAT), F32),
            pltpu.VMEM((LON, LAT), F32),
            pltpu.VMEM((LON, LAT), jnp.int32),
            pltpu.VMEM((2, 3, CX, 8, CZ), F32),
            pltpu.SemaphoreType.DMA((24,)),
        ],
    )
    r1 = exchange(sent)
    velocity, stress, mat, coef = call(
        fetch,
        [v_shape, s_shape, pltpu.VMEM((CX, CY, CZ), jnp.int32), resident(1, CX, CY, CZ)],
        *outside(velocity, stress, material), tab,
        ins=[HB] * 3 + [VM],
        scratch=[pltpu.SemaphoreType.DMA((3,))],
    )
    v1, *sent, lift, bag = call(
        functools.partial(move, 1, False),
        [v_shape] + PAYLOAD + [pz_shape, shape(32, 128), bag_shape],
        velocity, stress, coef, *r1, bag,
        scratch=[plane_z], aliases={0: 0, 8: 7},
    )
    r2 = exchange(sent)
    mat, v1 = lax.optimization_barrier((mat, v1))
    (coef2,) = call(lame, [resident(2, CX, CY, CZ)], tab, mat)
    s1, *sent, bag = call(
        functools.partial(strain, 2, False),
        [s_shape] + PAYLOAD + [pz_shape, bag_shape],
        stress, v1, coef2, *r2, bag,
        scratch=[plane_z], aliases={0: 0, 8: 6},
    )
    r3 = exchange(sent)
    owners, cells, s1 = lax.optimization_barrier((owner_map.reshape(64, 1, 512), cell_map, s1))
    group, slot, code = call(
        address,
        [shape(8, 512), shape(512, 128), shape(8, 128)],
        *outside(owners, cells),
        ins=[HB] * 2,
        scratch=[
            pltpu.VMEM((1, 512), jnp.int32),
            pltpu.VMEM((8, 512), jnp.int32),
            pltpu.SemaphoreType.DMA((2,)),
        ],
    )
    r3, group, slot, code = lax.optimization_barrier((r3, group, slot, code))
    v2, *sent, lift, bag = call(
        functools.partial(move, 3, True),
        [v_shape] + PAYLOAD + [pz_lift, shape(32, 128), bag_shape],
        v1, s1, coef, *r3, bag, lift,
        scratch=[plane_z], aliases={0: 0, 8: 7},
    )
    r4 = exchange(sent)
    v_out, s2, out, bag, far = call(
        functools.partial(strain, 4, True),
        [pltpu.HBM(dims, F32) for dims in ((3, CX, CY, CZ), (6, CX, CY, CZ), (64, 128), (BAG, 128), (OCR, 128))],
        s1, v2, coef2, *r4, bag, lift, group, slot, code,
        outs_at=[HB] * 5,
        scratch=[
            pltpu.VMEM((6, CX, CY, CZ), F32),
            plane_z,
            pltpu.VMEM((64, 128), F32),
            pltpu.VMEM((512, 128), F32),
            pltpu.SemaphoreType.DMA((CX + 4,)),
        ],
    )
    arrived = lax.all_to_all(out, ("gx", "gy"), split_axis=0, concat_axis=0, tiled=True)
    block = pltpu.VMEM((LON, LAT), F32)
    height_out, current_out = call(
        ocean, [shape(LON, LAT)] * 2,
        *outside(arrived, far, bag, height, current, wet_mask),
        ins=[HB] * 6,
        scratch=[
            pltpu.VMEM((64, 128), F32), pltpu.VMEM((OCR, 128), F32), pltpu.VMEM((BAG, 128), F32),
            block, block, pltpu.VMEM((LON, LAT), jnp.int32),
            pltpu.VMEM((512, 4096), jnp.bfloat16),
            pltpu.VMEM((64, 128), F32),
            pltpu.VMEM((64, 128), jnp.int32),
            pltpu.VMEM((256, 128), F32),
            pltpu.VMEM((32, 128), F32),
            pltpu.VMEM((72, 128), F32),
            pltpu.SemaphoreType.DMA((6,)),
        ],
    )
    return v_out, s2, height_out, current_out


def solution(mesh):
    return jax.shard_map(
        local,
        mesh=mesh,
        in_specs=(
            P(None, "gx", "gy", "gz"),
            P(None, "gx", "gy", "gz"),
            P("gx", "gy", "gz"),
            P(),
            P(),
            P(),
            P("gx", ("gy", "gz")),
            P("gx", ("gy", "gz")),
            P("gx", ("gy", "gz")),
            P("gx", ("gy", "gz")),
        ),
        out_specs=(
            P(None, "gx", "gy", "gz"),
            P(None, "gx", "gy", "gz"),
            P("gx", ("gy", "gz")),
            P("gx", ("gy", "gz")),
        ),
        check_vma=False,
    )
```

```python
import functools

import jax
import jax.numpy as jnp
from jax import lax
from jax.experimental import pallas as pl
from jax.experimental.pallas import tpu as pltpu
from jax.sharding import PartitionSpec as P

F32 = jnp.float32
CX, CY, CZ = 16, 32, 256
LAT = 128
LON = 32
NB = 8
SX, SY, SZ = (0, 5, 4), (5, 1, 3), (4, 3, 2)
VA = (0, 1, 2)
XF = 3 * 2 * CY
OCR = 80
XR = XF + OCR
YR = 3 * 2 * CX
FAC = NB * OCR
BAG = FAC + 128
HIGH = lax.Precision.HIGHEST
VM = pl.BlockSpec(memory_space=pltpu.VMEM)
HB = pl.BlockSpec(memory_space=pltpu.HBM)


def iotas():
    return (
        lax.broadcasted_iota(jnp.int32, (8, 128), 0),
        lax.broadcasted_iota(jnp.int32, (8, 128), 1),
    )


def tile(ref, c, x, t, h):
    return ref[c, x, t * 8 : t * 8 + 8, h * 128 : h * 128 + 128]


def call(body, outs, *args, scratch=(), ins=None, outs_at=None, aliases=None, limit=20):
    return pl.pallas_call(
        body,
        out_shape=outs,
        in_specs=[VM] * len(args) if ins is None else ins,
        out_specs=[VM] * len(outs) if outs_at is None else outs_at,
        scratch_shapes=list(scratch),
        input_output_aliases=aliases or {},
        compiler_params=pltpu.CompilerParams(vmem_limit_bytes=limit * 1024 * 1024),
    )(*args)


def place():
    return lax.axis_index("gx"), lax.axis_index("gy"), lax.axis_index("gz")


def shape(*dims):
    return jax.ShapeDtypeStruct(dims, F32)


PARTS = 3
def resident(*dims):
    return pltpu.VMEM(dims, F32)


def outside(*arrays):
    return [pltpu.with_memory_space_constraint(a, pltpu.HBM) for a in arrays]


PAYLOAD = [shape(XR, 128), shape(XR, 128), shape(YR, 128), shape(YR, 128)]


def odd(axis):
    return lax.rem(lax.axis_index(axis), 2) == 1


def put_x_faces(ref, comps, pxe, pxo):
    flip = odd("gx")
    for i, c in enumerate(comps):
        for h in range(2):
            rows = slice(i * 64 + h * 32, i * 64 + h * 32 + 32)
            lanes = slice(h * 128, h * 128 + 128)
            above, below = ref[c, CX - 1, :, lanes], ref[c, 0, :, lanes]
            pxe[rows, :] = jnp.where(flip, below, above)
            pxo[rows, :] = jnp.where(flip, above, below)


def put_y(flip, x, i, tiles, pye, pyo):
    for h in range(2):
        row = i * 32 + h * 16 + x
        above, below = tiles[3][h][7:8, :], tiles[0][h][0:1, :]
        pye[row : row + 1, :] = jnp.where(flip, below, above)
        pyo[row : row + 1, :] = jnp.where(flip, above, below)


def put_z(gz, x, i, tiles, pz):
    for t in range(4):
        pz[i * CX + x, t * 8 : t * 8 + 8, :] = jnp.where(gz == 0, tiles[t][1], tiles[t][0])


def prepare(s, depth, height, wet, pxe, pxo, pye, pyo, pz, bag, rows, high, deep, damp, edge, sems):
    gx, _, gz = place()
    copies = []

    def start(src, dst):
        copy = pltpu.make_async_copy(src, dst, sems.at[len(copies)])
        copy.start()
        copies.append(copy)

    start(depth, deep)
    start(height, high)
    start(wet, damp)
    first_face = jnp.where(odd("gx"), 0, CX - 1)
    flip = odd("gy")
    for i, c in enumerate(SX):
        for h in range(2):
            lanes = pl.ds(h * 128, 128)
            start(s.at[c, first_face, :, lanes], pxe.at[pl.ds(i * 64 + h * 32, 32), :])
            start(s.at[c, CX - 1 - first_face, :, lanes], pxo.at[pl.ds(i * 64 + h * 32, 32), :])
    for i, c in enumerate(SY):
        start(s.at[c, :, pl.ds(24, 8), :], edge.at[0, i])
        start(s.at[c, :, pl.ds(0, 8), :], edge.at[1, i])
    lanes = pl.ds(pl.multiple_of(128 * (1 - gz), 128), 128)
    for i, c in enumerate(SZ):
        start(s.at[c, :, :, lanes], pz.at[pl.ds(i * CX, CX)])
    for copy in copies[:3]:
        copy.wait()
    factor(deep, high, damp, pxe, bag, rows)
    pxo[XF:, :] = pxe[XF:, :]
    bag[pl.ds(pl.multiple_of(gx * OCR, 8), OCR), :] = pxe[XF:, :]
    for copy in copies[3:]:
        copy.wait()
    for i in range(3):
        for x in range(CX):
            for h in range(2):
                row = i * 32 + h * 16 + x
                lanes = slice(h * 128, h * 128 + 128)
                above, below = edge[0, i, x, 7:8, lanes], edge[1, i, x, 0:1, lanes]
                pye[row : row + 1, :] = jnp.where(flip, below, above)
                pyo[row : row + 1, :] = jnp.where(flip, above, below)


def factor(depth, height, wet, pxe, bag, rows):
    spread = depth[...] * depth[...] / 3.0
    rows[0:32, :] = spread
    w = [None] * LON
    inv = [None] * LON
    right = [None] * LON
    after = jnp.zeros((1, LAT), F32)
    link = jnp.ones((1, LAT), F32)
    for j in reversed(range(LON)):
        sp = rows[j : j + 1, :]
        inv[j] = 1.0 / (1.0 + 2.0 * sp - sp * after)
        w[j] = after = sp * inv[j]
        right[j] = link = w[j] * link
    left_run = jnp.ones((1, LAT), F32)
    right_run = jnp.zeros((1, LAT), F32)
    past = jnp.zeros((1, LAT), F32)
    weight = [None] * LON
    weight[LON - 1] = jnp.ones((1, LAT), F32)
    for j in reversed(range(LON - 1)):
        weight[j] = w[j + 1] * weight[j + 1]
    total = jnp.zeros((1, LAT), F32)
    p_before = q_before = jnp.zeros((1, LAT), F32)
    for j in range(LON):
        p_now = left_run * inv[j]
        total = weight[j] + (w[j - 1] * total if j else 0.0)
        q_now = inv[j] * total
        left_run = w[j] * left_run
        right_run = right[j] + w[j] * right_run
        bag[FAC + j : FAC + j + 1, :] = left_run
        bag[FAC + 32 + j : FAC + 33 + j, :] = right_run
        bag[FAC + 64 + j : FAC + 65 + j, :] = w[j]
        bag[FAC + 96 + j : FAC + 97 + j, :] = inv[j]
        if j == 0:
            first_left, first_right = left_run, right_run
        rows[j : j + 1, :] = p_now - p_before
        rows[32 + j : 33 + j, :] = q_now - q_before
        p_before, q_before = p_now, q_now
    wet_float = wet[...].astype(F32)
    high = height[...]
    a1 = 400.0 * rows[0:32, :] * wet_float
    a2 = 400.0 * rows[32:64, :] * wet_float
    pxe[XF : XF + 32, :] = a1
    pxe[XF + 32 : XF + 64, :] = a2
    base = XF + 64
    pxe[base : base + 1, :] = jnp.sum(a1 * high, axis=0, keepdims=True)
    pxe[base + 1 : base + 2, :] = jnp.sum(a2 * high, axis=0, keepdims=True)
    pxe[base + 2 : base + 3, :] = first_left
    pxe[base + 3 : base + 4, :] = left_run
    pxe[base + 4 : base + 5, :] = first_right
    pxe[base + 5 : base + 6, :] = right_run
    pxe[base + 6 : base + 7, :] = -400.0 * p_before
    pxe[base + 7 : base + 8, :] = -400.0 * q_before
    pxe[base + 8 : base + 9, :] = wet_float[0:1, :]
    pxe[base + 9 : base + 10, :] = wet_float[0:1, :] * high[0:1, :]
    pxe[base + 10 : base + 16, :] = jnp.zeros((6, LAT), F32)


def slopes_z(src, comps, out):
    k = lax.broadcasted_iota(jnp.int32, (CZ, CZ), 0)
    n = lax.broadcasted_iota(jnp.int32, (CZ, CZ), 1)
    step = jnp.where(k == n + 1, 1.0, 0.0) - jnp.where(k == n - 1, 1.0, 0.0)
    step = step.astype(jnp.bfloat16)
    for i, c in enumerate(comps):
        full = src[c].reshape(CX * CY, CZ)
        total = None
        for _ in range(PARTS):
            part = full.astype(jnp.bfloat16)
            full = full - part.astype(F32)
            product = jnp.dot(part, step, preferred_element_type=F32)
            total = product if total is None else total + product
        out[i] = total.reshape(CX, CY, CZ)


def differences(src, comps, dzs, xe, xo, ye, yo, zs):
    gx, gy, gz = place()
    sub, lane = iotas()
    cx, cy, cz = comps

    def flag(cond):
        return jnp.where(cond, 1.0, 0.0).astype(F32)

    m_xd, m_xu = flag(gx > 0), flag(gx < NB - 1)
    m_yd, m_yu = flag(gy > 0), flag(gy < NB - 1)
    top, bottom = sub == 7, sub == 0
    far, near = (lane == 127) & (gz == 0), (lane == 0) & (gz == 1)
    shift = jnp.where(gz == 0, 127, 1)

    flip_x, flip_y = odd("gx"), odd("gy")

    def halo_x(one, two, mask, i, t, h):
        row = i * 64 + h * 32 + t * 8
        return jnp.where(flip_x, one[row : row + 8, :], two[row : row + 8, :]) * mask

    def halo_y(one, two, mask, row):
        line = jnp.where(flip_y, one[row : row + 1, :], two[row : row + 1, :]) * mask
        return jnp.broadcast_to(line, (8, 128))

    def dx(x, i, t, h):
        c = cx[i]
        low = halo_x(xe, xo, m_xd, i, t, h) if x == 0 else tile(src, c, x - 1, t, h)
        high = halo_x(xo, xe, m_xu, i, t, h) if x == CX - 1 else tile(src, c, x + 1, t, h)
        return high - low

    def dy(x, i, tiles):
        out = [[None, None] for _ in range(4)]
        for h in range(2):
            up = [pltpu.roll(tiles[t][h], 7, 0) for t in range(4)]
            dn = [pltpu.roll(tiles[t][h], 1, 0) for t in range(4)]
            row = i * 32 + h * 16 + x
            up.append(halo_y(yo, ye, m_yu, row))
            dn.insert(0, halo_y(ye, yo, m_yd, row))
            for t in range(4):
                out[t][h] = jnp.where(top, up[t + 1], up[t]) - jnp.where(bottom, dn[t], dn[t + 1])
        return out

    def dz(x, i):
        out = [[None, None] for _ in range(4)]
        for t in range(4):
            slab = pltpu.roll(zs[i * CX + x, t * 8 : t * 8 + 8, :], shift, 1)
            out[t][0] = tile(dzs, i, x, t, 0) - jnp.where(near, slab, 0.0)
            out[t][1] = tile(dzs, i, x, t, 1) + jnp.where(far, slab, 0.0)
        return out

    return dx, dy, dz


def grab(ref, c, x):
    return [[tile(ref, c, x, t, h) for h in range(2)] for t in range(4)]


def lookup(tab, mat, coef, rows):
    table = [tab[i * 8 : i * 8 + 8, :] for i in rows]

    def plane(x, carry):
        for t in range(4):
            for h in range(2):
                index = mat[x, t * 8 : t * 8 + 8, h * 128 : h * 128 + 128]
                for i in range(len(rows)):
                    coef[i, x, t * 8 : t * 8 + 8, h * 128 : h * 128 + 128] = jnp.take_along_axis(
                        table[i], index, axis=1, mode="promise_in_bounds"
                    )
        return carry

    lax.fori_loop(0, CX, plane, 0)


def fetch(v_hbm, s_hbm, mat_hbm, tab, v, s, mat, coef, sems):
    copies = [
        pltpu.make_async_copy(a, b, sems.at[i])
        for i, (a, b) in enumerate(((mat_hbm, mat), (s_hbm, s), (v_hbm, v)))
    ]
    for copy in copies:
        copy.start()
    copies[0].wait()
    lookup(tab, mat, coef, (0,))
    copies[1].wait()
    copies[2].wait()


def lame(tab, mat, coef):
    lookup(tab, mat, coef, (1, 2))


def collect(distance, xe, xo, bag):
    gx = lax.axis_index("gx")
    first = jnp.where(odd("gx"), NB - distance, distance)
    for ref, steps in ((xe, first), (xo, NB - first)):
        row = pl.multiple_of(lax.rem(gx + steps, NB) * OCR, 8)
        bag[pl.ds(row, OCR), :] = ref[XF:, :]


def move(distance, has_lift, v, s, coef, xe, xo, ye, yo, zs, bag_in, *refs):
    if has_lift:
        lift_in, coef2, pxe, pxo, pye, pyo, pz, lift_out, v_hbm, s_hbm, coef_hbm, bag_hbm, vo, bag, dzs, sems = refs
        copies = [
            pltpu.make_async_copy(s, s_hbm, sems.at[CX]),
            pltpu.make_async_copy(coef2, coef_hbm, sems.at[CX + 1]),
            pltpu.make_async_copy(bag, bag_hbm, sems.at[CX + 2]),
        ]
        bag[...] = bag_in[...]
    else:
        vo, pxe, pxo, pye, pyo, pz, lift_out, bag, dzs = refs
    gz = lax.axis_index("gz")
    flip = odd("gy")
    sub, lane = iotas()
    collect(distance, xe, xo, bag)
    if has_lift:
        for copy in copies:
            copy.start()
    slopes_z(s, SZ, dzs)
    dx, dy, dz = differences(s, (SX, SY, SZ), dzs, xe, xo, ye, yo, zs)
    lift = [lift_in[t * 8 : t * 8 + 8, :] if has_lift else jnp.zeros((8, 128), F32) for t in range(4)]
    for x in range(CX):
        for i in range(3):
            ey = dy(x, i, grab(s, SY[i], x))
            ez = dz(x, i)
            new = [[None, None] for _ in range(4)]
            for t in range(4):
                for h in range(2):
                    force = dx(x, i, t, h) + ey[t][h] + ez[t][h]
                    new[t][h] = tile(v, i, x, t, h) + tile(coef, 0, x, t, h) * force
                    vo[i, x, t * 8 : t * 8 + 8, h * 128 : h * 128 + 128] = new[t][h]
            put_y(flip, x, i, new, pye, pyo)
            put_z(gz, x, i, new, pz)
        if has_lift:
            copies.append(pltpu.make_async_copy(vo.at[:, x], v_hbm.at[:, x], sems.at[x]))
            copies[-1].start()
        for t in range(4):
            lift[t] = jnp.where(lane == x, lift[t] - 0.25 * pltpu.roll(new[t][0], x, 1), lift[t])
    for t in range(4):
        lift_out[t * 8 : t * 8 + 8, :] = lift[t]
        if has_lift:
            pz[3 * CX, t * 8 : t * 8 + 8, :] = lift[t]
    put_x_faces(vo, VA, pxe, pxo)
    pxe[XF:, :] = xo[XF:, :]
    pxo[XF:, :] = xe[XF:, :]
    if has_lift:
        for copy in copies:
            copy.wait()


def strain(distance, s, v, coef, xe, xo, ye, yo, zs, bag_in, so, pxe, pxo, pye, pyo, pz, bag, dzs):
    collect(distance, xe, xo, bag)
    slopes_z(v, VA, dzs)
    gz, flip = lax.axis_index("gz"), odd("gy")

    def done(x, new):
        for i in range(3):
            put_y(flip, x, i, new[SY[i]], pye, pyo)
            put_z(gz, x, i, new[SZ[i]], pz)

    stretch(s, v, coef, dzs, xe, xo, ye, yo, zs, so, done)
    put_x_faces(so, SX, pxe, pxo)
    pxe[XF:, :] = xo[XF:, :]
    pxo[XF:, :] = xe[XF:, :]


def finish(s_in, v_in, coef_in, zs_in, xe, xo, ye, yo, s_hbm, far_hbm, s, v, coef, zs, dzs, sems):
    early = [
        pltpu.make_async_copy(v_in, v, sems.at[0]),
        pltpu.make_async_copy(zs_in, zs, sems.at[1]),
        pltpu.make_async_copy(coef_in, coef, sems.at[2]),
        pltpu.make_async_copy(xe.at[pl.ds(XF, OCR), :], far_hbm, sems.at[3]),
    ]
    parts = [
        pltpu.make_async_copy(s_in.at[:, pl.ds(i * 4, 4)], s.at[:, pl.ds(i * 4, 4)], sems.at[4 + i])
        for i in range(4)
    ]
    for copy in early + parts:
        copy.start()
    early[0].wait()
    slopes_z(v, VA, dzs)
    for copy in early[1:] + parts:
        copy.wait()
    late = []

    def done(x, new):
        late.append(pltpu.make_async_copy(s.at[:, x], s_hbm.at[:, x], sems.at[8 + x]))
        late[-1].start()

    stretch(s, v, coef, dzs, xe, xo, ye, yo, zs, s, done)
    for copy in late:
        copy.wait()


def stretch(s, v, coef, dzs, xe, xo, ye, yo, zs, so, done):
    dx, dy, dz = differences(v, (VA, VA, VA), dzs, xe, xo, ye, yo, zs)
    for x in range(CX):
        ey = [dy(x, c, grab(v, c, x)) for c in range(3)]
        ez = [dz(x, c) for c in range(3)]
        new = [[[None, None] for _ in range(4)] for _ in range(6)]
        for t in range(4):
            for h in range(2):
                ex = [dx(x, c, t, h) for c in range(3)]
                mu = tile(coef, 1, x, t, h)
                bulk = tile(coef, 0, x, t, h) * (ex[0] + ey[1][t][h] + ez[2][t][h])
                mu2 = mu + mu
                change = (
                    bulk + mu2 * ex[0],
                    bulk + mu2 * ey[1][t][h],
                    bulk + mu2 * ez[2][t][h],
                    mu * (ez[1][t][h] + ey[2][t][h]),
                    mu * (ez[0][t][h] + ex[2]),
                    mu * (ey[0][t][h] + ex[1]),
                )
                for c in range(6):
                    new[c][t][h] = tile(s, c, x, t, h) + change[c]
                    so[c, x, t * 8 : t * 8 + 8, h * 128 : h * 128 + 128] = new[c][t][h]
        done(x, new)


def as_column(row, sub, lane):
    parts = []
    for i in range(4):
        part = jnp.broadcast_to(row[:, i * 128 : i * 128 + 128], (128, 128))
        parts.append(jnp.sum(jnp.where(sub == lane, part, 0.0), axis=1, keepdims=True))
    return jnp.concatenate(parts, axis=0)


def address(owners, cell_rows, group, slot, code, owner, cell, sems):
    gx, gy, gz = place()
    copies = [
        pltpu.make_async_copy(owners.at[gx * NB + gy], owner, sems.at[0]),
        pltpu.make_async_copy(cell_rows.at[pl.ds(pl.multiple_of(gx * NB, 8), 8), :], cell, sems.at[1]),
    ]
    for copy in copies:
        copy.start()
    for copy in copies:
        copy.wait()
    sub = lax.broadcasted_iota(jnp.int32, (128, 128), 0)
    lane = lax.broadcasted_iota(jnp.int32, (128, 128), 1)
    own = owner[...]
    column = as_column(own.astype(F32), sub, lane).astype(jnp.int32)
    cells = as_column(cell[pl.ds(gy, 1), :].astype(F32) + 1.0, sub, lane)
    wide = lax.broadcasted_iota(jnp.int32, (512, 128), 1)
    same = (jnp.broadcast_to(column, (512, 128)) == wide).astype(F32)
    earlier = (
        lax.broadcasted_iota(jnp.int32, (512, 512), 1) < lax.broadcasted_iota(jnp.int32, (512, 512), 0)
    ).astype(F32)
    before = jnp.dot(earlier, same, preferred_element_type=F32)
    position = jnp.sum(same * before, axis=1, keepdims=True).astype(jnp.int32)
    spot = (column >> 4) * 8 + position
    taken = (jnp.broadcast_to(spot, (512, 128)) == wide).astype(F32)
    slot[...] = taken
    rows = lax.broadcasted_iota(jnp.int32, (8, 512), 0)
    mine = jnp.broadcast_to(own, (8, 512))
    chosen = ((((mine >> 1) & 7) == rows) & ((mine & 1) == gz)).astype(F32)
    group[...] = chosen
    found = jnp.dot(chosen, taken * cells, precision=HIGH, preferred_element_type=F32)
    code[...] = pltpu.roll(found, 64, 1)


def pack_lift(lift_here, zs, group, slot, code, out, wide):
    lift = jnp.where(lax.axis_index("gz") == 0, lift_here[...], zs[3 * CX])
    for x in range(CX):
        rows = slice(x * 32, x * 32 + 32)
        wide[rows, :] = slot[rows, :] * jnp.broadcast_to(lift[:, x : x + 1], (32, 128))
    row = jnp.dot(group[...], wide[...], precision=HIGH, preferred_element_type=F32) + code[...]
    for i in range(8):
        out[i * 8 : i * 8 + 8, :] = row


def ocean(arrived, far_in, bag_in, height_in, current_in, wet_in, ho, co, far, bag, height, current, wet, hot, val, pair, src, ends, sweep, sems):
    gx = lax.axis_index("gx")
    copies = [
        pltpu.make_async_copy(a, b, sems.at[i])
        for i, (a, b) in enumerate(
            (
                (far_in, far),
                (bag_in, bag),
                (height_in, height),
                (current_in, current),
                (wet_in, wet),
            )
        )
    ]
    for copy in copies:
        copy.start()
    b16 = jnp.bfloat16
    lane = lax.broadcasted_iota(jnp.int32, (32, 128), 1)
    half = lane < 64
    one, two = arrived[0:32, :], arrived[32:64, :]
    value = jnp.where(half, one, pltpu.roll(two, 64, 1))
    cell = jnp.where(half, pltpu.roll(one, 64, 1), two).astype(jnp.int32) - 1
    band = (lane & 63) >> 3
    pair[0:32, :] = jnp.where(cell >= 0, band * 32 + (cell >> 7), -1)
    pair[32:64, :] = cell & 127
    coarse = value.astype(b16).astype(F32)
    val[0:32, :] = coarse
    val[32:64, :] = value - coarse
    lon_rows = lax.broadcasted_iota(jnp.int32, (256, 128), 0)
    lat_rows = lax.broadcasted_iota(jnp.int32, (128, 128), 0)
    for r in range(32):
        cols = slice(r * 128, r * 128 + 128)
        hot[0:256, cols] = (lon_rows == pair[r : r + 1, :]).astype(F32).astype(b16)
        here = lat_rows == pair[32 + r : 33 + r, :]
        hot[256:384, cols] = jnp.where(here, val[r : r + 1, :], 0.0).astype(b16)
        hot[384:512, cols] = jnp.where(here, val[32 + r : 33 + r, :], 0.0).astype(b16)
    both = lax.dot_general(
        hot[0:256, :], hot[256:512, :], (((1,), (1,)), ((), ())), preferred_element_type=F32
    )
    src[...] = both[:, 0:128] + both[:, 128:256]
    for copy in copies:
        copy.wait()
    opposite = lax.rem(gx + 4, NB) * OCR
    bag_rows = lambda b, k, n: jnp.where(opposite == b * OCR, far[k : k + n, :], bag[b * OCR + k : b * OCR + k + n, :])
    zero = jnp.zeros((1, LAT), F32)

    def extra(b, k):
        return bag_rows(b, 64 + k, 1)

    head = [extra(b, 8) * src[b * 32 : b * 32 + 1, :] + extra(b, 9) for b in range(NB)] + [zero]
    y0, yl = [], []
    for b in range(NB):
        s_b = src[b * 32 : b * 32 + 32, :]
        y0.append(jnp.sum(bag_rows(b, 0, 32) * s_b, axis=0, keepdims=True) + extra(b, 0) + extra(b, 6) * head[b + 1])
        yl.append(jnp.sum(bag_rows(b, 32, 32) * s_b, axis=0, keepdims=True) + extra(b, 1) + extra(b, 7) * head[b + 1])
    a = [zero] * (NB + 1)
    m = [zero] * (NB + 1)
    zc = [zero] * NB
    zl = [zero] * NB
    for b in reversed(range(NB)):
        scale = 1.0 / (1.0 - extra(b, 5) * m[b + 1])
        zc[b] = scale * (yl[b] + extra(b, 5) * a[b + 1])
        zl[b] = scale * extra(b, 3)
        a[b] = y0[b] + extra(b, 4) * (a[b + 1] + m[b + 1] * zc[b])
        m[b] = extra(b, 2) + extra(b, 4) * m[b + 1] * zl[b]
    z = zero
    ends[0:1, :] = zero
    ends[16 + NB : 17 + NB, :] = zero
    for b in range(NB):
        ends[16 + b : 17 + b, :] = a[b] + m[b] * z
        z = zc[b] + zl[b] * z
        ends[b + 1 : b + 2, :] = z
    left = ends[pl.ds(gx, 1), :]
    right = ends[pl.ds(gx + 17, 1), :]
    wet_float = wet[...].astype(F32)
    new_height = wet_float * (height[...] + src[pl.ds(pl.multiple_of(gx * 32, 32), 32), :])
    ho[...] = new_height
    sweep[0:32, :] = new_height
    nxt = lax.rem(gx + 1, NB)
    next_head = bag[pl.ds(nxt * OCR + 72, 1), :] * src[pl.ds(nxt * 32, 1), :] + bag[pl.ds(nxt * OCR + 73, 1), :]
    sweep[32:33, :] = jnp.where(gx == NB - 1, 0.0, next_head)
    forced = bag[FAC + 96 : FAC + 128, :] * (-400.0 * (sweep[1:33, :] - new_height))
    sweep[40:72, :] = forced
    run = zero
    offs = [None] * LON
    for j in reversed(range(LON)):
        offs[j] = run = sweep[40 + j : 41 + j, :] + bag[FAC + 64 + j : FAC + 65 + j, :] * run
    run = zero
    for j in range(LON):
        run = offs[j] + bag[FAC + 64 + j : FAC + 65 + j, :] * run
        sweep[40 + j : 41 + j, :] = run
    increment = sweep[40:72, :] + bag[FAC : FAC + 32, :] * left + bag[FAC + 32 : FAC + 64, :] * right
    co[...] = wet_float * (current[...] + increment)


def swap(value, axis, first):
    n = lax.axis_size(axis)
    pairs = [(i, (i + 1) % n) for i in range(0 if first else 1, n, 2)]
    return lax.ppermute(value, axis, pairs + [(j, i) for i, j in pairs])


def exchange(payload):
    pxe, pxo, pye, pyo, pz = payload
    zs = swap(pz, "gz", True)
    xe, xo = swap(pxe, "gx", True), swap(pxo, "gx", False)
    ye, yo = swap(pye, "gy", True), swap(pyo, "gy", False)
    return xe, xo, ye, yo, zs


def local(velocity, stress, material, properties, owner_map, cell_map, height, current, sea_depth, wet_mask):
    scaled = 0.125 * properties.T
    tab = jnp.pad(jnp.concatenate([scaled[2:3], scaled[0:1], scaled[1:2]]), ((0, 0), (0, 112)))
    tab = jnp.repeat(tab, 8, axis=0)
    pz_shape, pz_lift = shape(3 * CX, CY, 128), shape(3 * CX + 1, CY, 128)
    v_shape, s_shape = resident(3, CX, CY, CZ), resident(6, CX, CY, CZ)
    bag_shape = shape(BAG, 128)
    plane_z = pltpu.VMEM((3, CX, CY, CZ), F32)
    *sent, bag = call(
        prepare,
        PAYLOAD + [pz_shape, bag_shape],
        *outside(stress, sea_depth, height, wet_mask),
        ins=[HB] * 4,
        scratch=[
            pltpu.VMEM((64, LAT), F32),
            pltpu.VMEM((LON, LAT), F32),
            pltpu.VMEM((LON, LAT), F32),
            pltpu.VMEM((LON, LAT), jnp.int32),
            pltpu.VMEM((2, 3, CX, 8, CZ), F32),
            pltpu.SemaphoreType.DMA((24,)),
        ],
    )
    r1 = exchange(sent)
    velocity, stress, mat, coef = call(
        fetch,
        [v_shape, s_shape, pltpu.VMEM((CX, CY, CZ), jnp.int32), resident(1, CX, CY, CZ)],
        *outside(velocity, stress, material), tab,
        ins=[HB] * 3 + [VM],
        scratch=[pltpu.SemaphoreType.DMA((3,))],
    )
    v1, *sent, lift, bag = call(
        functools.partial(move, 1, False),
        [v_shape] + PAYLOAD + [pz_shape, shape(32, 128), bag_shape],
        velocity, stress, coef, *r1, bag,
        scratch=[plane_z], aliases={0: 0, 8: 7},
    )
    r2 = exchange(sent)
    mat, v1 = lax.optimization_barrier((mat, v1))
    (coef2,) = call(lame, [resident(2, CX, CY, CZ)], tab, mat)
    s1, *sent, bag = call(
        functools.partial(strain, 2),
        [s_shape] + PAYLOAD + [pz_shape, bag_shape],
        stress, v1, coef2, *r2, bag,
        scratch=[plane_z], aliases={0: 0, 8: 6},
    )
    r3 = exchange(sent)
    owners, cells, s1 = lax.optimization_barrier((owner_map.reshape(64, 1, 512), cell_map, s1))
    group, slot, code = call(
        address,
        [shape(8, 512), shape(512, 128), shape(8, 128)],
        *outside(owners, cells),
        ins=[HB] * 2,
        scratch=[
            pltpu.VMEM((1, 512), jnp.int32),
            pltpu.VMEM((8, 512), jnp.int32),
            pltpu.SemaphoreType.DMA((2,)),
        ],
    )
    r3, group, slot, code = lax.optimization_barrier((r3, group, slot, code))
    *sent, lift, v_out, s1, coef2, bag = call(
        functools.partial(move, 3, True),
        PAYLOAD
        + [pz_lift, shape(32, 128)]
        + [pltpu.HBM(dims, F32) for dims in ((3, CX, CY, CZ), (6, CX, CY, CZ), (2, CX, CY, CZ), (BAG, 128))],
        v1, s1, coef, *r3, bag, lift, coef2,
        outs_at=[VM] * 6 + [HB] * 4,
        scratch=[plane_z, pltpu.VMEM((BAG, 128), F32), plane_z, pltpu.SemaphoreType.DMA((CX + 3,))],
    )
    *r4, zs = exchange(sent)
    (out,) = call(
        pack_lift,
        [shape(64, 128)],
        lift, zs, group, slot, code,
        scratch=[pltpu.VMEM((512, 128), F32)],
    )
    s2, far = call(
        finish,
        [pltpu.HBM(dims, F32) for dims in ((6, CX, CY, CZ), (OCR, 128))],
        *outside(s1, v_out, coef2, zs), *r4,
        ins=[HB] * 4 + [VM] * 4,
        outs_at=[HB] * 2,
        scratch=[
            pltpu.VMEM((6, CX, CY, CZ), F32),
            plane_z,
            pltpu.VMEM((2, CX, CY, CZ), F32),
            pltpu.VMEM((3 * CX + 1, CY, 128), F32),
            plane_z,
            pltpu.SemaphoreType.DMA((8 + CX,)),
        ],
    )
    arrived = lax.all_to_all(out, ("gx", "gy"), split_axis=0, concat_axis=0, tiled=True)
    block = pltpu.VMEM((LON, LAT), F32)
    height_out, current_out = call(
        ocean, [shape(LON, LAT)] * 2,
        arrived, *outside(far, bag, height, current, wet_mask),
        ins=[VM] + [HB] * 5,
        scratch=[
            pltpu.VMEM((OCR, 128), F32), pltpu.VMEM((BAG, 128), F32),
            block, block, pltpu.VMEM((LON, LAT), jnp.int32),
            pltpu.VMEM((512, 4096), jnp.bfloat16),
            pltpu.VMEM((64, 128), F32),
            pltpu.VMEM((64, 128), jnp.int32),
            pltpu.VMEM((256, 128), F32),
            pltpu.VMEM((32, 128), F32),
            pltpu.VMEM((72, 128), F32),
            pltpu.SemaphoreType.DMA((5,)),
        ],
    )
    return v_out, s2, height_out, current_out


def solution(mesh):
    return jax.shard_map(
        local,
        mesh=mesh,
        in_specs=(
            P(None, "gx", "gy", "gz"),
            P(None, "gx", "gy", "gz"),
            P("gx", "gy", "gz"),
            P(),
            P(),
            P(),
            P("gx", ("gy", "gz")),
            P("gx", ("gy", "gz")),
            P("gx", ("gy", "gz")),
            P("gx", ("gy", "gz")),
        ),
        out_specs=(
            P(None, "gx", "gy", "gz"),
            P(None, "gx", "gy", "gz"),
            P("gx", ("gy", "gz")),
            P("gx", ("gy", "gz")),
        ),
        check_vma=False,
    )
```

```python
import functools

import jax
import jax.numpy as jnp
from jax import lax
from jax.experimental import pallas as pl
from jax.experimental.pallas import tpu as pltpu
from jax.sharding import PartitionSpec as P

F32 = jnp.float32
CX, CY, CZ = 16, 32, 256
LAT = 128
LON = 32
NB = 8
SX, SY, SZ = (0, 5, 4), (5, 1, 3), (4, 3, 2)
VA = (0, 1, 2)
XF = 3 * 2 * CY
OCR = 80
XR = XF + OCR
YR = 3 * 2 * CX
FAC = NB * OCR
BAG = FAC + 128
HIGH = lax.Precision.HIGHEST
VM = pl.BlockSpec(memory_space=pltpu.VMEM)
HB = pl.BlockSpec(memory_space=pltpu.HBM)


def iotas():
    return (
        lax.broadcasted_iota(jnp.int32, (8, 128), 0),
        lax.broadcasted_iota(jnp.int32, (8, 128), 1),
    )


def tile(ref, c, x, t, h):
    return ref[c, x, t * 8 : t * 8 + 8, h * 128 : h * 128 + 128]


def call(body, outs, *args, scratch=(), ins=None, outs_at=None, aliases=None, limit=20):
    return pl.pallas_call(
        body,
        out_shape=outs,
        in_specs=[VM] * len(args) if ins is None else ins,
        out_specs=[VM] * len(outs) if outs_at is None else outs_at,
        scratch_shapes=list(scratch),
        input_output_aliases=aliases or {},
        compiler_params=pltpu.CompilerParams(vmem_limit_bytes=limit * 1024 * 1024),
    )(*args)


def place():
    return lax.axis_index("gx"), lax.axis_index("gy"), lax.axis_index("gz")


def shape(*dims):
    return jax.ShapeDtypeStruct(dims, F32)


PARTS = 3
def resident(*dims):
    return pltpu.VMEM(dims, F32)


def outside(*arrays):
    return [pltpu.with_memory_space_constraint(a, pltpu.HBM) for a in arrays]


PAYLOAD = [shape(XR, 128), shape(XR, 128), shape(YR, 128), shape(YR, 128)]


def odd(axis):
    return lax.rem(lax.axis_index(axis), 2) == 1


def put_x_faces(ref, comps, pxe, pxo):
    flip = odd("gx")
    for i, c in enumerate(comps):
        for h in range(2):
            rows = slice(i * 64 + h * 32, i * 64 + h * 32 + 32)
            lanes = slice(h * 128, h * 128 + 128)
            above, below = ref[c, CX - 1, :, lanes], ref[c, 0, :, lanes]
            pxe[rows, :] = jnp.where(flip, below, above)
            pxo[rows, :] = jnp.where(flip, above, below)


def put_y(flip, x, i, tiles, pye, pyo):
    for h in range(2):
        row = i * 32 + h * 16 + x
        above, below = tiles[3][h][7:8, :], tiles[0][h][0:1, :]
        pye[row : row + 1, :] = jnp.where(flip, below, above)
        pyo[row : row + 1, :] = jnp.where(flip, above, below)


def put_z(gz, x, i, tiles, pz):
    for t in range(4):
        pz[i * CX + x, t * 8 : t * 8 + 8, :] = jnp.where(gz == 0, tiles[t][1], tiles[t][0])


def prepare(s, depth, height, wet, pxe, pxo, pye, pyo, pz, bag, rows, high, deep, damp, edge, sems):
    gx, _, gz = place()
    copies = []

    def start(src, dst):
        copy = pltpu.make_async_copy(src, dst, sems.at[len(copies)])
        copy.start()
        copies.append(copy)

    start(depth, deep)
    start(height, high)
    start(wet, damp)
    first_face = jnp.where(odd("gx"), 0, CX - 1)
    flip = odd("gy")
    for i, c in enumerate(SX):
        for h in range(2):
            lanes = pl.ds(h * 128, 128)
            start(s.at[c, first_face, :, lanes], pxe.at[pl.ds(i * 64 + h * 32, 32), :])
            start(s.at[c, CX - 1 - first_face, :, lanes], pxo.at[pl.ds(i * 64 + h * 32, 32), :])
    for i, c in enumerate(SY):
        start(s.at[c, :, pl.ds(24, 8), :], edge.at[0, i])
        start(s.at[c, :, pl.ds(0, 8), :], edge.at[1, i])
    lanes = pl.ds(pl.multiple_of(128 * (1 - gz), 128), 128)
    for i, c in enumerate(SZ):
        start(s.at[c, :, :, lanes], pz.at[pl.ds(i * CX, CX)])
    for copy in copies[:3]:
        copy.wait()
    factor(deep, high, damp, pxe, bag, rows)
    pxo[XF:, :] = pxe[XF:, :]
    bag[pl.ds(pl.multiple_of(gx * OCR, 8), OCR), :] = pxe[XF:, :]
    for copy in copies[3:]:
        copy.wait()
    for i in range(3):
        for x in range(CX):
            for h in range(2):
                row = i * 32 + h * 16 + x
                lanes = slice(h * 128, h * 128 + 128)
                above, below = edge[0, i, x, 7:8, lanes], edge[1, i, x, 0:1, lanes]
                pye[row : row + 1, :] = jnp.where(flip, below, above)
                pyo[row : row + 1, :] = jnp.where(flip, above, below)


def factor(depth, height, wet, pxe, bag, rows):
    spread = depth[...] * depth[...] / 3.0
    rows[0:32, :] = spread
    w = [None] * LON
    inv = [None] * LON
    right = [None] * LON
    after = jnp.zeros((1, LAT), F32)
    link = jnp.ones((1, LAT), F32)
    for j in reversed(range(LON)):
        sp = rows[j : j + 1, :]
        inv[j] = 1.0 / (1.0 + 2.0 * sp - sp * after)
        w[j] = after = sp * inv[j]
        right[j] = link = w[j] * link
    left_run = jnp.ones((1, LAT), F32)
    right_run = jnp.zeros((1, LAT), F32)
    past = jnp.zeros((1, LAT), F32)
    weight = [None] * LON
    weight[LON - 1] = jnp.ones((1, LAT), F32)
    for j in reversed(range(LON - 1)):
        weight[j] = w[j + 1] * weight[j + 1]
    total = jnp.zeros((1, LAT), F32)
    p_before = q_before = jnp.zeros((1, LAT), F32)
    for j in range(LON):
        p_now = left_run * inv[j]
        total = weight[j] + (w[j - 1] * total if j else 0.0)
        q_now = inv[j] * total
        left_run = w[j] * left_run
        right_run = right[j] + w[j] * right_run
        bag[FAC + j : FAC + j + 1, :] = left_run
        bag[FAC + 32 + j : FAC + 33 + j, :] = right_run
        bag[FAC + 64 + j : FAC + 65 + j, :] = w[j]
        bag[FAC + 96 + j : FAC + 97 + j, :] = inv[j]
        if j == 0:
            first_left, first_right = left_run, right_run
        rows[j : j + 1, :] = p_now - p_before
        rows[32 + j : 33 + j, :] = q_now - q_before
        p_before, q_before = p_now, q_now
    wet_float = wet[...].astype(F32)
    high = height[...]
    a1 = 400.0 * rows[0:32, :] * wet_float
    a2 = 400.0 * rows[32:64, :] * wet_float
    pxe[XF : XF + 32, :] = a1
    pxe[XF + 32 : XF + 64, :] = a2
    base = XF + 64
    pxe[base : base + 1, :] = jnp.sum(a1 * high, axis=0, keepdims=True)
    pxe[base + 1 : base + 2, :] = jnp.sum(a2 * high, axis=0, keepdims=True)
    pxe[base + 2 : base + 3, :] = first_left
    pxe[base + 3 : base + 4, :] = left_run
    pxe[base + 4 : base + 5, :] = first_right
    pxe[base + 5 : base + 6, :] = right_run
    pxe[base + 6 : base + 7, :] = -400.0 * p_before
    pxe[base + 7 : base + 8, :] = -400.0 * q_before
    pxe[base + 8 : base + 9, :] = wet_float[0:1, :]
    pxe[base + 9 : base + 10, :] = wet_float[0:1, :] * high[0:1, :]
    pxe[base + 10 : base + 16, :] = jnp.zeros((6, LAT), F32)


def slopes_z(src, out, comps):
    k = lax.broadcasted_iota(jnp.int32, (CZ, CZ), 0)
    n = lax.broadcasted_iota(jnp.int32, (CZ, CZ), 1)
    step = jnp.where(k == n + 1, 1.0, 0.0) - jnp.where(k == n - 1, 1.0, 0.0)
    step = step.astype(jnp.bfloat16)
    for i, c in enumerate(comps):
        full = src[c].reshape(CX * CY, CZ)
        total = None
        for _ in range(PARTS):
            part = full.astype(jnp.bfloat16)
            full = full - part.astype(F32)
            product = jnp.dot(part, step, preferred_element_type=F32)
            total = product if total is None else total + product
        out[i] = total.reshape(CX, CY, CZ)


def differences(src, comps, dzs, xe, xo, ye, yo, zs):
    gx, gy, gz = place()
    sub, lane = iotas()
    cx, cy, cz = comps

    def flag(cond):
        return jnp.where(cond, 1.0, 0.0).astype(F32)

    m_xd, m_xu = flag(gx > 0), flag(gx < NB - 1)
    m_yd, m_yu = flag(gy > 0), flag(gy < NB - 1)
    top, bottom = sub == 7, sub == 0
    far, near = (lane == 127) & (gz == 0), (lane == 0) & (gz == 1)
    shift = jnp.where(gz == 0, 127, 1)

    flip_x, flip_y = odd("gx"), odd("gy")

    def halo_x(one, two, mask, i, t, h):
        row = i * 64 + h * 32 + t * 8
        return jnp.where(flip_x, one[row : row + 8, :], two[row : row + 8, :]) * mask

    def halo_y(one, two, mask, row):
        line = jnp.where(flip_y, one[row : row + 1, :], two[row : row + 1, :]) * mask
        return jnp.broadcast_to(line, (8, 128))

    def dx(x, i, t, h):
        c = cx[i]
        low = halo_x(xe, xo, m_xd, i, t, h) if x == 0 else tile(src, c, x - 1, t, h)
        high = halo_x(xo, xe, m_xu, i, t, h) if x == CX - 1 else tile(src, c, x + 1, t, h)
        return high - low

    def dy(x, i, tiles):
        out = [[None, None] for _ in range(4)]
        for h in range(2):
            up = [pltpu.roll(tiles[t][h], 7, 0) for t in range(4)]
            dn = [pltpu.roll(tiles[t][h], 1, 0) for t in range(4)]
            row = i * 32 + h * 16 + x
            up.append(halo_y(yo, ye, m_yu, row))
            dn.insert(0, halo_y(ye, yo, m_yd, row))
            for t in range(4):
                out[t][h] = jnp.where(top, up[t + 1], up[t]) - jnp.where(bottom, dn[t], dn[t + 1])
        return out

    def dz(x, i):
        out = [[None, None] for _ in range(4)]
        for t in range(4):
            slab = pltpu.roll(zs[i * CX + x, t * 8 : t * 8 + 8, :], shift, 1)
            out[t][0] = tile(dzs, i, x, t, 0) - jnp.where(near, slab, 0.0)
            out[t][1] = tile(dzs, i, x, t, 1) + jnp.where(far, slab, 0.0)
        return out

    return dx, dy, dz


def grab(ref, c, x):
    return [[tile(ref, c, x, t, h) for h in range(2)] for t in range(4)]


def lookup(tab, mat, coef, rows):
    table = [tab[i * 8 : i * 8 + 8, :] for i in rows]

    def plane(x, carry):
        for t in range(4):
            for h in range(2):
                index = mat[x, t * 8 : t * 8 + 8, h * 128 : h * 128 + 128]
                for i in range(len(rows)):
                    coef[i, x, t * 8 : t * 8 + 8, h * 128 : h * 128 + 128] = jnp.take_along_axis(
                        table[i], index, axis=1, mode="promise_in_bounds"
                    )
        return carry

    lax.fori_loop(0, CX, plane, 0)


def fetch(v_hbm, s_hbm, mat_hbm, tab, v, s, mat, coef, dzs, sems):
    copies = [
        pltpu.make_async_copy(a, b, sems.at[i])
        for i, (a, b) in enumerate(((mat_hbm, mat), (s_hbm, s), (v_hbm, v)))
    ]
    for copy in copies:
        copy.start()
    copies[0].wait()
    lookup(tab, mat, coef, (0,))
    copies[1].wait()
    slopes_z(s, dzs, SZ)
    copies[2].wait()


def lame(tab, mat, v, coef, dzs):
    slopes_z(v, dzs, VA)
    lookup(tab, mat, coef, (1, 2))


def collect(distance, xe, xo, bag):
    gx = lax.axis_index("gx")
    first = jnp.where(odd("gx"), NB - distance, distance)
    for ref, steps in ((xe, first), (xo, NB - first)):
        row = pl.multiple_of(lax.rem(gx + steps, NB) * OCR, 8)
        bag[pl.ds(row, OCR), :] = ref[XF:, :]


def move(distance, has_lift, v, s, coef, dzs, xe, xo, ye, yo, zs, bag_in, *refs):
    if has_lift:
        lift_in, pxe, pxo, pye, pyo, pz, lift_out, v_hbm, bag_hbm, vo, bag, sems = refs
        copies = [pltpu.make_async_copy(bag, bag_hbm, sems.at[CX])]
        bag[...] = bag_in[...]
    else:
        vo, pxe, pxo, pye, pyo, pz, lift_out, bag = refs
    gz = lax.axis_index("gz")
    flip = odd("gy")
    sub, lane = iotas()
    collect(distance, xe, xo, bag)
    if has_lift:
        for copy in copies:
            copy.start()
    dx, dy, dz = differences(s, (SX, SY, SZ), dzs, xe, xo, ye, yo, zs)
    lift = [lift_in[t * 8 : t * 8 + 8, :] if has_lift else jnp.zeros((8, 128), F32) for t in range(4)]
    for x in range(CX):
        for i in range(3):
            ey = dy(x, i, grab(s, SY[i], x))
            ez = dz(x, i)
            new = [[None, None] for _ in range(4)]
            for t in range(4):
                for h in range(2):
                    force = dx(x, i, t, h) + ey[t][h] + ez[t][h]
                    new[t][h] = tile(v, i, x, t, h) + tile(coef, 0, x, t, h) * force
                    vo[i, x, t * 8 : t * 8 + 8, h * 128 : h * 128 + 128] = new[t][h]
            put_y(flip, x, i, new, pye, pyo)
            put_z(gz, x, i, new, pz)
        if has_lift:
            copies.append(pltpu.make_async_copy(vo.at[:, x], v_hbm.at[:, x], sems.at[x]))
            copies[-1].start()
        for t in range(4):
            lift[t] = jnp.where(lane == x, lift[t] - 0.25 * pltpu.roll(new[t][0], x, 1), lift[t])
    for t in range(4):
        lift_out[t * 8 : t * 8 + 8, :] = lift[t]
        if has_lift:
            pz[3 * CX, t * 8 : t * 8 + 8, :] = lift[t]
    put_x_faces(vo, VA, pxe, pxo)
    pxe[XF:, :] = xo[XF:, :]
    pxo[XF:, :] = xe[XF:, :]
    if has_lift:
        for copy in copies:
            copy.wait()


def strain(distance, s, v, coef, dzs, xe, xo, ye, yo, zs, bag_in, so, pxe, pxo, pye, pyo, pz, bag, s_hbm, coef_hbm, sems):
    copies = [pltpu.make_async_copy(coef, coef_hbm, sems.at[CX])]
    copies[0].start()
    collect(distance, xe, xo, bag)
    gz, flip = lax.axis_index("gz"), odd("gy")

    def done(x, new):
        for i in range(3):
            put_y(flip, x, i, new[SY[i]], pye, pyo)
            put_z(gz, x, i, new[SZ[i]], pz)
        copies.append(pltpu.make_async_copy(so.at[:, x], s_hbm.at[:, x], sems.at[x]))
        copies[-1].start()

    stretch(s, v, coef, dzs, xe, xo, ye, yo, zs, so, done)
    put_x_faces(so, SX, pxe, pxo)
    pxe[XF:, :] = xo[XF:, :]
    pxo[XF:, :] = xe[XF:, :]
    for copy in copies:
        copy.wait()


def finish(s_in, v_in, coef_in, zs_in, xe, xo, ye, yo, s_hbm, far_hbm, s, v, coef, zs, dzs, sems):
    early = [
        pltpu.make_async_copy(v_in, v, sems.at[0]),
        pltpu.make_async_copy(zs_in, zs, sems.at[1]),
        pltpu.make_async_copy(coef_in, coef, sems.at[2]),
        pltpu.make_async_copy(xe.at[pl.ds(XF, OCR), :], far_hbm, sems.at[3]),
    ]
    parts = [
        pltpu.make_async_copy(s_in.at[:, pl.ds(i * 4, 4)], s.at[:, pl.ds(i * 4, 4)], sems.at[4 + i])
        for i in range(4)
    ]
    for copy in early + parts:
        copy.start()
    early[0].wait()
    slopes_z(v, dzs, VA)
    for copy in early[1:]:
        copy.wait()
    late = []

    def done(x, new):
        late.append(pltpu.make_async_copy(s.at[:, x], s_hbm.at[:, x], sems.at[8 + x]))
        late[-1].start()

    def ready(x):
        if x % 4 == 0:
            parts[x // 4].wait()

    stretch(s, v, coef, dzs, xe, xo, ye, yo, zs, s, done, ready)
    for copy in late:
        copy.wait()


def stretch(s, v, coef, dzs, xe, xo, ye, yo, zs, so, done, ready=lambda x: None):
    dx, dy, dz = differences(v, (VA, VA, VA), dzs, xe, xo, ye, yo, zs)
    for x in range(CX):
        ready(x)
        ey = [dy(x, c, grab(v, c, x)) for c in range(3)]
        ez = [dz(x, c) for c in range(3)]
        new = [[[None, None] for _ in range(4)] for _ in range(6)]
        for t in range(4):
            for h in range(2):
                ex = [dx(x, c, t, h) for c in range(3)]
                mu = tile(coef, 1, x, t, h)
                bulk = tile(coef, 0, x, t, h) * (ex[0] + ey[1][t][h] + ez[2][t][h])
                mu2 = mu + mu
                change = (
                    bulk + mu2 * ex[0],
                    bulk + mu2 * ey[1][t][h],
                    bulk + mu2 * ez[2][t][h],
                    mu * (ez[1][t][h] + ey[2][t][h]),
                    mu * (ez[0][t][h] + ex[2]),
                    mu * (ey[0][t][h] + ex[1]),
                )
                for c in range(6):
                    new[c][t][h] = tile(s, c, x, t, h) + change[c]
                    so[c, x, t * 8 : t * 8 + 8, h * 128 : h * 128 + 128] = new[c][t][h]
        done(x, new)


def as_column(row, sub, lane):
    parts = []
    for i in range(4):
        part = jnp.broadcast_to(row[:, i * 128 : i * 128 + 128], (128, 128))
        parts.append(jnp.sum(jnp.where(sub == lane, part, 0.0), axis=1, keepdims=True))
    return jnp.concatenate(parts, axis=0)


def address(owners, cell_rows, group, slot, code, owner, cell, sems):
    gx, gy, gz = place()
    copies = [
        pltpu.make_async_copy(owners.at[gx * NB + gy], owner, sems.at[0]),
        pltpu.make_async_copy(cell_rows.at[pl.ds(pl.multiple_of(gx * NB, 8), 8), :], cell, sems.at[1]),
    ]
    for copy in copies:
        copy.start()
    for copy in copies:
        copy.wait()
    sub = lax.broadcasted_iota(jnp.int32, (128, 128), 0)
    lane = lax.broadcasted_iota(jnp.int32, (128, 128), 1)
    own = owner[...]
    column = as_column(own.astype(F32), sub, lane).astype(jnp.int32)
    cells = as_column(cell[pl.ds(gy, 1), :].astype(F32) + 1.0, sub, lane)
    wide = lax.broadcasted_iota(jnp.int32, (512, 128), 1)
    same = (jnp.broadcast_to(column, (512, 128)) == wide).astype(F32)
    earlier = (
        lax.broadcasted_iota(jnp.int32, (512, 512), 1) < lax.broadcasted_iota(jnp.int32, (512, 512), 0)
    ).astype(F32)
    before = jnp.dot(earlier, same, preferred_element_type=F32)
    position = jnp.sum(same * before, axis=1, keepdims=True).astype(jnp.int32)
    spot = (column >> 4) * 8 + position
    taken = (jnp.broadcast_to(spot, (512, 128)) == wide).astype(F32)
    slot[...] = taken
    rows = lax.broadcasted_iota(jnp.int32, (8, 512), 0)
    mine = jnp.broadcast_to(own, (8, 512))
    chosen = ((((mine >> 1) & 7) == rows) & ((mine & 1) == gz)).astype(F32)
    group[...] = chosen
    found = jnp.dot(chosen, taken * cells, precision=HIGH, preferred_element_type=F32)
    code[...] = pltpu.roll(found, 64, 1)


def pack_lift(lift_here, zs, group, slot, code, out, wide):
    lift = jnp.where(lax.axis_index("gz") == 0, lift_here[...], zs[3 * CX])
    for x in range(CX):
        rows = slice(x * 32, x * 32 + 32)
        wide[rows, :] = slot[rows, :] * jnp.broadcast_to(lift[:, x : x + 1], (32, 128))
    row = jnp.dot(group[...], wide[...], precision=HIGH, preferred_element_type=F32) + code[...]
    for i in range(8):
        out[i * 8 : i * 8 + 8, :] = row


def ocean(arrived, far_in, bag_in, height_in, current_in, wet_in, ho, co, far, bag, height, current, wet, hot, val, pair, src, ends, sweep, sems):
    gx = lax.axis_index("gx")
    copies = [
        pltpu.make_async_copy(a, b, sems.at[i])
        for i, (a, b) in enumerate(
            (
                (far_in, far),
                (bag_in, bag),
                (height_in, height),
                (current_in, current),
                (wet_in, wet),
            )
        )
    ]
    for copy in copies:
        copy.start()
    b16 = jnp.bfloat16
    lane = lax.broadcasted_iota(jnp.int32, (32, 128), 1)
    half = lane < 64
    one, two = arrived[0:32, :], arrived[32:64, :]
    value = jnp.where(half, one, pltpu.roll(two, 64, 1))
    cell = jnp.where(half, pltpu.roll(one, 64, 1), two).astype(jnp.int32) - 1
    band = (lane & 63) >> 3
    pair[0:32, :] = jnp.where(cell >= 0, band * 32 + (cell >> 7), -1)
    pair[32:64, :] = cell & 127
    coarse = value.astype(b16).astype(F32)
    val[0:32, :] = coarse
    val[32:64, :] = value - coarse
    lon_rows = lax.broadcasted_iota(jnp.int32, (256, 128), 0)
    lat_rows = lax.broadcasted_iota(jnp.int32, (128, 128), 0)
    for r in range(32):
        cols = slice(r * 128, r * 128 + 128)
        hot[0:256, cols] = (lon_rows == pair[r : r + 1, :]).astype(F32).astype(b16)
        here = lat_rows == pair[32 + r : 33 + r, :]
        hot[256:384, cols] = jnp.where(here, val[r : r + 1, :], 0.0).astype(b16)
        hot[384:512, cols] = jnp.where(here, val[32 + r : 33 + r, :], 0.0).astype(b16)
    both = lax.dot_general(
        hot[0:256, :], hot[256:512, :], (((1,), (1,)), ((), ())), preferred_element_type=F32
    )
    src[...] = both[:, 0:128] + both[:, 128:256]
    for copy in copies:
        copy.wait()
    opposite = lax.rem(gx + 4, NB) * OCR
    bag_rows = lambda b, k, n: jnp.where(opposite == b * OCR, far[k : k + n, :], bag[b * OCR + k : b * OCR + k + n, :])
    zero = jnp.zeros((1, LAT), F32)

    def extra(b, k):
        return bag_rows(b, 64 + k, 1)

    head = [extra(b, 8) * src[b * 32 : b * 32 + 1, :] + extra(b, 9) for b in range(NB)] + [zero]
    y0, yl = [], []
    for b in range(NB):
        s_b = src[b * 32 : b * 32 + 32, :]
        y0.append(jnp.sum(bag_rows(b, 0, 32) * s_b, axis=0, keepdims=True) + extra(b, 0) + extra(b, 6) * head[b + 1])
        yl.append(jnp.sum(bag_rows(b, 32, 32) * s_b, axis=0, keepdims=True) + extra(b, 1) + extra(b, 7) * head[b + 1])
    a = [zero] * (NB + 1)
    m = [zero] * (NB + 1)
    zc = [zero] * NB
    zl = [zero] * NB
    for b in reversed(range(NB)):
        scale = 1.0 / (1.0 - extra(b, 5) * m[b + 1])
        zc[b] = scale * (yl[b] + extra(b, 5) * a[b + 1])
        zl[b] = scale * extra(b, 3)
        a[b] = y0[b] + extra(b, 4) * (a[b + 1] + m[b + 1] * zc[b])
        m[b] = extra(b, 2) + extra(b, 4) * m[b + 1] * zl[b]
    z = zero
    ends[0:1, :] = zero
    ends[16 + NB : 17 + NB, :] = zero
    for b in range(NB):
        ends[16 + b : 17 + b, :] = a[b] + m[b] * z
        z = zc[b] + zl[b] * z
        ends[b + 1 : b + 2, :] = z
    left = ends[pl.ds(gx, 1), :]
    right = ends[pl.ds(gx + 17, 1), :]
    wet_float = wet[...].astype(F32)
    new_height = wet_float * (height[...] + src[pl.ds(pl.multiple_of(gx * 32, 32), 32), :])
    ho[...] = new_height
    sweep[0:32, :] = new_height
    nxt = lax.rem(gx + 1, NB)
    next_head = bag[pl.ds(nxt * OCR + 72, 1), :] * src[pl.ds(nxt * 32, 1), :] + bag[pl.ds(nxt * OCR + 73, 1), :]
    sweep[32:33, :] = jnp.where(gx == NB - 1, 0.0, next_head)
    forced = bag[FAC + 96 : FAC + 128, :] * (-400.0 * (sweep[1:33, :] - new_height))
    sweep[40:72, :] = forced
    run = zero
    offs = [None] * LON
    for j in reversed(range(LON)):
        offs[j] = run = sweep[40 + j : 41 + j, :] + bag[FAC + 64 + j : FAC + 65 + j, :] * run
    run = zero
    for j in range(LON):
        run = offs[j] + bag[FAC + 64 + j : FAC + 65 + j, :] * run
        sweep[40 + j : 41 + j, :] = run
    increment = sweep[40:72, :] + bag[FAC : FAC + 32, :] * left + bag[FAC + 32 : FAC + 64, :] * right
    co[...] = wet_float * (current[...] + increment)


def swap(value, axis, first):
    n = lax.axis_size(axis)
    pairs = [(i, (i + 1) % n) for i in range(0 if first else 1, n, 2)]
    return lax.ppermute(value, axis, pairs + [(j, i) for i, j in pairs])


def exchange(payload):
    pxe, pxo, pye, pyo, pz = payload
    zs = swap(pz, "gz", True)
    xe, xo = swap(pxe, "gx", True), swap(pxo, "gx", False)
    ye, yo = swap(pye, "gy", True), swap(pyo, "gy", False)
    return xe, xo, ye, yo, zs


def local(velocity, stress, material, properties, owner_map, cell_map, height, current, sea_depth, wet_mask):
    scaled = 0.125 * properties.T
    tab = jnp.pad(jnp.concatenate([scaled[2:3], scaled[0:1], scaled[1:2]]), ((0, 0), (0, 112)))
    tab = jnp.repeat(tab, 8, axis=0)
    pz_shape, pz_lift = shape(3 * CX, CY, 128), shape(3 * CX + 1, CY, 128)
    v_shape, s_shape = resident(3, CX, CY, CZ), resident(6, CX, CY, CZ)
    bag_shape = shape(BAG, 128)
    plane_z = pltpu.VMEM((3, CX, CY, CZ), F32)
    *sent, bag = call(
        prepare,
        PAYLOAD + [pz_shape, bag_shape],
        *outside(stress, sea_depth, height, wet_mask),
        ins=[HB] * 4,
        scratch=[
            pltpu.VMEM((64, LAT), F32),
            pltpu.VMEM((LON, LAT), F32),
            pltpu.VMEM((LON, LAT), F32),
            pltpu.VMEM((LON, LAT), jnp.int32),
            pltpu.VMEM((2, 3, CX, 8, CZ), F32),
            pltpu.SemaphoreType.DMA((24,)),
        ],
    )
    r1 = exchange(sent)
    velocity, stress, mat, coef, dzs = call(
        fetch,
        [v_shape, s_shape, pltpu.VMEM((CX, CY, CZ), jnp.int32), resident(1, CX, CY, CZ), v_shape],
        *outside(velocity, stress, material), tab,
        ins=[HB] * 3 + [VM],
        scratch=[pltpu.SemaphoreType.DMA((3,))],
    )
    v1, *sent, lift, bag = call(
        functools.partial(move, 1, False),
        [v_shape] + PAYLOAD + [pz_shape, shape(32, 128), bag_shape],
        velocity, stress, coef, dzs, *r1, bag,
        aliases={0: 0, 9: 7},
    )
    r2 = exchange(sent)
    mat, v1 = lax.optimization_barrier((mat, v1))
    coef2, dzs = call(lame, [resident(2, CX, CY, CZ), v_shape], tab, mat, v1)
    s1, *sent, bag, s_copy, coef_copy = call(
        functools.partial(strain, 2),
        [s_shape] + PAYLOAD + [pz_shape, bag_shape] + [pltpu.HBM(dims, F32) for dims in ((6, CX, CY, CZ), (2, CX, CY, CZ))],
        stress, v1, coef2, dzs, *r2, bag,
        outs_at=[VM] * 7 + [HB] * 2,
        scratch=[pltpu.SemaphoreType.DMA((CX + 1,))], aliases={0: 0, 9: 6},
    )
    r3 = exchange(sent)
    owners, cells, s1 = lax.optimization_barrier((owner_map.reshape(64, 1, 512), cell_map, s1))
    group, slot, code = call(
        address,
        [shape(8, 512), shape(512, 128), shape(8, 128)],
        *outside(owners, cells),
        ins=[HB] * 2,
        scratch=[
            pltpu.VMEM((1, 512), jnp.int32),
            pltpu.VMEM((8, 512), jnp.int32),
            pltpu.SemaphoreType.DMA((2,)),
        ],
    )
    (dzs,) = call(functools.partial(slopes_z, comps=SZ), [v_shape], s1)
    r3, group, slot, code = lax.optimization_barrier((r3, group, slot, code))
    *sent, lift, v_out, bag = call(
        functools.partial(move, 3, True),
        PAYLOAD
        + [pz_lift, shape(32, 128)]
        + [pltpu.HBM(dims, F32) for dims in ((3, CX, CY, CZ), (BAG, 128))],
        v1, s1, coef, dzs, *r3, bag, lift,
        outs_at=[VM] * 6 + [HB] * 2,
        scratch=[plane_z, pltpu.VMEM((BAG, 128), F32), pltpu.SemaphoreType.DMA((CX + 1,))],
    )
    *r4, zs = exchange(sent)
    (out,) = call(
        pack_lift,
        [shape(64, 128)],
        lift, zs, group, slot, code,
        scratch=[pltpu.VMEM((512, 128), F32)],
    )
    s2, far = call(
        finish,
        [pltpu.HBM(dims, F32) for dims in ((6, CX, CY, CZ), (OCR, 128))],
        *outside(s_copy, v_out, coef_copy, zs), *r4,
        ins=[HB] * 4 + [VM] * 4,
        outs_at=[HB] * 2,
        scratch=[
            pltpu.VMEM((6, CX, CY, CZ), F32),
            plane_z,
            pltpu.VMEM((2, CX, CY, CZ), F32),
            pltpu.VMEM((3 * CX + 1, CY, 128), F32),
            plane_z,
            pltpu.SemaphoreType.DMA((8 + CX,)),
        ],
    )
    arrived = lax.all_to_all(out, ("gx", "gy"), split_axis=0, concat_axis=0, tiled=True)
    block = pltpu.VMEM((LON, LAT), F32)
    height_out, current_out = call(
        ocean, [shape(LON, LAT)] * 2,
        arrived, *outside(far, bag, height, current, wet_mask),
        ins=[VM] + [HB] * 5,
        scratch=[
            pltpu.VMEM((OCR, 128), F32), pltpu.VMEM((BAG, 128), F32),
            block, block, pltpu.VMEM((LON, LAT), jnp.int32),
            pltpu.VMEM((512, 4096), jnp.bfloat16),
            pltpu.VMEM((64, 128), F32),
            pltpu.VMEM((64, 128), jnp.int32),
            pltpu.VMEM((256, 128), F32),
            pltpu.VMEM((32, 128), F32),
            pltpu.VMEM((72, 128), F32),
            pltpu.SemaphoreType.DMA((5,)),
        ],
    )
    return v_out, s2, height_out, current_out


def solution(mesh):
    return jax.shard_map(
        local,
        mesh=mesh,
        in_specs=(
            P(None, "gx", "gy", "gz"),
            P(None, "gx", "gy", "gz"),
            P("gx", "gy", "gz"),
            P(),
            P(),
            P(),
            P("gx", ("gy", "gz")),
            P("gx", ("gy", "gz")),
            P("gx", ("gy", "gz")),
            P("gx", ("gy", "gz")),
        ),
        out_specs=(
            P(None, "gx", "gy", "gz"),
            P(None, "gx", "gy", "gz"),
            P("gx", ("gy", "gz")),
            P("gx", ("gy", "gz")),
        ),
        check_vma=False,
    )
```

```python
import functools

import jax
import jax.numpy as jnp
from jax import lax
from jax.experimental import pallas as pl
from jax.experimental.pallas import tpu as pltpu
from jax.sharding import PartitionSpec as P

F32 = jnp.float32
CX, CY, CZ = 16, 32, 256
LAT = 128
LON = 32
NB = 8
SX, SY, SZ = (0, 5, 4), (5, 1, 3), (4, 3, 2)
VA = (0, 1, 2)
XF = 3 * 2 * CY
OCR = 80
XR = XF + OCR
YR = 3 * 2 * CX
FAC = NB * OCR
BAG = FAC + 128
HIGH = lax.Precision.HIGHEST
VM = pl.BlockSpec(memory_space=pltpu.VMEM)
HB = pl.BlockSpec(memory_space=pltpu.HBM)


def iotas():
    return (
        lax.broadcasted_iota(jnp.int32, (8, 128), 0),
        lax.broadcasted_iota(jnp.int32, (8, 128), 1),
    )


def tile(ref, c, x, t, h):
    return ref[c, x, t * 8 : t * 8 + 8, h * 128 : h * 128 + 128]


def call(body, outs, *args, scratch=(), ins=None, outs_at=None, aliases=None, limit=20):
    return pl.pallas_call(
        body,
        out_shape=outs,
        in_specs=[VM] * len(args) if ins is None else ins,
        out_specs=[VM] * len(outs) if outs_at is None else outs_at,
        scratch_shapes=list(scratch),
        input_output_aliases=aliases or {},
        compiler_params=pltpu.CompilerParams(vmem_limit_bytes=limit * 1024 * 1024),
    )(*args)


def place():
    return lax.axis_index("gx"), lax.axis_index("gy"), lax.axis_index("gz")


def shape(*dims):
    return jax.ShapeDtypeStruct(dims, F32)


PARTS = 3
HALF = 8
def resident(*dims):
    return pltpu.VMEM(dims, F32)


def outside(*arrays):
    return [pltpu.with_memory_space_constraint(a, pltpu.HBM) for a in arrays]


PAYLOAD = [shape(XR, 128), shape(XR, 128), shape(YR, 128), shape(YR, 128)]


def odd(axis):
    return lax.rem(lax.axis_index(axis), 2) == 1


def put_x_faces(ref, comps, pxe, pxo):
    flip = odd("gx")
    for i, c in enumerate(comps):
        for h in range(2):
            rows = slice(i * 64 + h * 32, i * 64 + h * 32 + 32)
            lanes = slice(h * 128, h * 128 + 128)
            above, below = ref[c, CX - 1, :, lanes], ref[c, 0, :, lanes]
            pxe[rows, :] = jnp.where(flip, below, above)
            pxo[rows, :] = jnp.where(flip, above, below)


def put_y(flip, x, i, tiles, pye, pyo):
    for h in range(2):
        row = i * 32 + h * 16 + x
        above, below = tiles[3][h][7:8, :], tiles[0][h][0:1, :]
        pye[row : row + 1, :] = jnp.where(flip, below, above)
        pyo[row : row + 1, :] = jnp.where(flip, above, below)


def put_z(gz, x, i, tiles, pz):
    for t in range(4):
        pz[i * CX + x, t * 8 : t * 8 + 8, :] = jnp.where(gz == 0, tiles[t][1], tiles[t][0])


def prepare(s, depth, height, wet, pxe, pxo, pye, pyo, pz, bag, rows, high, deep, damp, edge, sems):
    gx, _, gz = place()
    copies = []

    def start(src, dst):
        copy = pltpu.make_async_copy(src, dst, sems.at[len(copies)])
        copy.start()
        copies.append(copy)

    start(depth, deep)
    start(height, high)
    start(wet, damp)
    first_face = jnp.where(odd("gx"), 0, CX - 1)
    flip = odd("gy")
    for i, c in enumerate(SX):
        for h in range(2):
            lanes = pl.ds(h * 128, 128)
            start(s.at[c, first_face, :, lanes], pxe.at[pl.ds(i * 64 + h * 32, 32), :])
            start(s.at[c, CX - 1 - first_face, :, lanes], pxo.at[pl.ds(i * 64 + h * 32, 32), :])
    for i, c in enumerate(SY):
        start(s.at[c, :, pl.ds(24, 8), :], edge.at[0, i])
        start(s.at[c, :, pl.ds(0, 8), :], edge.at[1, i])
    lanes = pl.ds(pl.multiple_of(128 * (1 - gz), 128), 128)
    for i, c in enumerate(SZ):
        start(s.at[c, :, :, lanes], pz.at[pl.ds(i * CX, CX)])
    for copy in copies[:3]:
        copy.wait()
    factor(deep, high, damp, pxe, bag, rows)
    pxo[XF:, :] = pxe[XF:, :]
    bag[pl.ds(pl.multiple_of(gx * OCR, 8), OCR), :] = pxe[XF:, :]
    for copy in copies[3:]:
        copy.wait()
    for i in range(3):
        for x in range(CX):
            for h in range(2):
                row = i * 32 + h * 16 + x
                lanes = slice(h * 128, h * 128 + 128)
                above, below = edge[0, i, x, 7:8, lanes], edge[1, i, x, 0:1, lanes]
                pye[row : row + 1, :] = jnp.where(flip, below, above)
                pyo[row : row + 1, :] = jnp.where(flip, above, below)


def factor(depth, height, wet, pxe, bag, rows):
    spread = depth[...] * depth[...] / 3.0
    scale = 1.0 / spread
    rows[0:32, :] = scale
    for base, order in ((32, reversed(range(LON))), (65, range(LON))):
        value, slope = jnp.ones((1, LAT), F32), jnp.ones((1, LAT), F32)
        last = base + (LON if base == 32 else 0)
        rows[last : last + 1, :] = value
        for j in order:
            slope = slope + value * rows[j : j + 1, :]
            value = value + slope
            at = base + (j if base == 32 else j + 1)
            rows[at : at + 1, :] = value
    down, down_next = rows[32:64, :], rows[33:65, :]
    up = rows[65:97, :]
    top, end = 1.0 / rows[32:33, :], 1.0 / rows[97:98, :]
    w = down_next / down
    left, right = down_next * top, up * end
    p_now, q_now = left * scale, right * scale
    bag[FAC : FAC + 32, :] = left
    bag[FAC + 32 : FAC + 64, :] = right
    bag[FAC + 64 : FAC + 96, :] = w
    bag[FAC + 96 : FAC + 128, :] = w * scale
    row = lax.broadcasted_iota(jnp.int32, (LON, LAT), 0)
    p_before = jnp.where(row == 0, 0.0, pltpu.roll(p_now, 1, 0))
    q_before = jnp.where(row == 0, 0.0, pltpu.roll(q_now, 1, 0))
    first_left, left_run = left[0:1, :], left[31:32, :]
    first_right, right_run = right[0:1, :], right[31:32, :]
    wet_float = wet[...].astype(F32)
    high = height[...]
    a1 = 400.0 * (p_now - p_before) * wet_float
    a2 = 400.0 * (q_now - q_before) * wet_float
    pxe[XF : XF + 32, :] = a1
    pxe[XF + 32 : XF + 64, :] = a2
    base = XF + 64
    pxe[base : base + 1, :] = jnp.sum(a1 * high, axis=0, keepdims=True)
    pxe[base + 1 : base + 2, :] = jnp.sum(a2 * high, axis=0, keepdims=True)
    pxe[base + 2 : base + 3, :] = first_left
    pxe[base + 3 : base + 4, :] = left_run
    pxe[base + 4 : base + 5, :] = first_right
    pxe[base + 5 : base + 6, :] = right_run
    pxe[base + 6 : base + 7, :] = -400.0 * p_now[31:32, :]
    pxe[base + 7 : base + 8, :] = -400.0 * q_now[31:32, :]
    pxe[base + 8 : base + 9, :] = wet_float[0:1, :]
    pxe[base + 9 : base + 10, :] = wet_float[0:1, :] * high[0:1, :]
    pxe[base + 10 : base + 16, :] = jnp.zeros((6, LAT), F32)


def slopes_z(src, out, comps):
    k = lax.broadcasted_iota(jnp.int32, (CZ, CZ), 0)
    n = lax.broadcasted_iota(jnp.int32, (CZ, CZ), 1)
    step = jnp.where(k == n + 1, 1.0, 0.0) - jnp.where(k == n - 1, 1.0, 0.0)
    step = step.astype(jnp.bfloat16)
    for i, c in enumerate(comps):
        full = src[c].reshape(CX * CY, CZ)
        total = None
        for _ in range(PARTS):
            part = full.astype(jnp.bfloat16)
            full = full - part.astype(F32)
            product = jnp.dot(part, step, preferred_element_type=F32)
            total = product if total is None else total + product
        out[i] = total.reshape(CX, CY, CZ)


def differences(src, comps, dzs, xe, xo, ye, yo, zs):
    gx, gy, gz = place()
    sub, lane = iotas()
    cx, cy, cz = comps

    def flag(cond):
        return jnp.where(cond, 1.0, 0.0).astype(F32)

    m_xd, m_xu = flag(gx > 0), flag(gx < NB - 1)
    m_yd, m_yu = flag(gy > 0), flag(gy < NB - 1)
    top, bottom = sub == 7, sub == 0
    far, near = (lane == 127) & (gz == 0), (lane == 0) & (gz == 1)
    shift = jnp.where(gz == 0, 127, 1)

    flip_x, flip_y = odd("gx"), odd("gy")

    def halo_x(one, two, mask, i, t, h):
        row = i * 64 + h * 32 + t * 8
        return jnp.where(flip_x, one[row : row + 8, :], two[row : row + 8, :]) * mask

    def halo_y(one, two, mask, row):
        line = jnp.where(flip_y, one[row : row + 1, :], two[row : row + 1, :]) * mask
        return jnp.broadcast_to(line, (8, 128))

    def dx(x, i, t, h):
        c = cx[i]
        low = halo_x(xe, xo, m_xd, i, t, h) if x == 0 else tile(src, c, x - 1, t, h)
        high = halo_x(xo, xe, m_xu, i, t, h) if x == CX - 1 else tile(src, c, x + 1, t, h)
        return high - low

    def dy(x, i, tiles):
        out = [[None, None] for _ in range(4)]
        for h in range(2):
            up = [pltpu.roll(tiles[t][h], 7, 0) for t in range(4)]
            dn = [pltpu.roll(tiles[t][h], 1, 0) for t in range(4)]
            row = i * 32 + h * 16 + x
            up.append(halo_y(yo, ye, m_yu, row))
            dn.insert(0, halo_y(ye, yo, m_yd, row))
            for t in range(4):
                out[t][h] = jnp.where(top, up[t + 1], up[t]) - jnp.where(bottom, dn[t], dn[t + 1])
        return out

    def dz(x, i):
        out = [[None, None] for _ in range(4)]
        for t in range(4):
            slab = pltpu.roll(zs[i * CX + x, t * 8 : t * 8 + 8, :], shift, 1)
            out[t][0] = tile(dzs, i, x, t, 0) - jnp.where(near, slab, 0.0)
            out[t][1] = tile(dzs, i, x, t, 1) + jnp.where(far, slab, 0.0)
        return out

    return dx, dy, dz


def grab(ref, c, x):
    return [[tile(ref, c, x, t, h) for h in range(2)] for t in range(4)]


def lookup(tab, mat, coef, rows):
    table = [tab[i * 8 : i * 8 + 8, :] for i in rows]

    def plane(x, carry):
        for t in range(4):
            for h in range(2):
                index = mat[x, t * 8 : t * 8 + 8, h * 128 : h * 128 + 128]
                for i in range(len(rows)):
                    coef[i, x, t * 8 : t * 8 + 8, h * 128 : h * 128 + 128] = jnp.take_along_axis(
                        table[i], index, axis=1, mode="promise_in_bounds"
                    )
        return carry

    lax.fori_loop(0, CX, plane, 0)


def fetch(v_hbm, s_hbm, mat_hbm, owners, cell_rows, tab, v, s, mat, coef, dzs, owner, cell, sems):
    gx, gy, _ = place()
    wanted = [
        (s_hbm.at[pl.ds(2, 3)], s.at[pl.ds(2, 3)]),
        (mat_hbm, mat),
        (s_hbm.at[pl.ds(0, 2)], s.at[pl.ds(0, 2)]),
        (s_hbm.at[5], s.at[5]),
        (v_hbm, v),
        (owners.at[gx * NB + gy], owner),
        (cell_rows.at[pl.ds(pl.multiple_of(gx * NB, 8), 8), :], cell),
    ]
    copies = [pltpu.make_async_copy(a, b, sems.at[i]) for i, (a, b) in enumerate(wanted)]
    for copy in copies:
        copy.start()
    copies[0].wait()
    slopes_z(s, dzs, SZ)
    copies[1].wait()
    lookup(tab, mat, coef, (0,))
    for copy in copies[2:]:
        copy.wait()


def lame(tab, mat, v, coef, dzs):
    slopes_z(v, dzs, VA)
    lookup(tab, mat, coef, (1, 2))


def collect(distance, xe, xo, bag):
    gx = lax.axis_index("gx")
    first = jnp.where(odd("gx"), NB - distance, distance)
    for ref, steps in ((xe, first), (xo, NB - first)):
        row = pl.multiple_of(lax.rem(gx + steps, NB) * OCR, 8)
        bag[pl.ds(row, OCR), :] = ref[XF:, :]


def move(distance, has_lift, v, s, coef, dzs, xe, xo, ye, yo, zs, bag_in, *refs):
    if has_lift:
        lift_in, pxe, pxo, pye, pyo, pz, lift_out, v_hbm, bag_hbm, vo, bag, sems = refs
        copies = [pltpu.make_async_copy(bag, bag_hbm, sems.at[CX])]
        bag[...] = bag_in[...]
    else:
        vo, pxe, pxo, pye, pyo, pz, lift_out, bag = refs
    gz = lax.axis_index("gz")
    flip = odd("gy")
    sub, lane = iotas()
    collect(distance, xe, xo, bag)
    if has_lift:
        copies[0].start()
    dx, dy, dz = differences(s, (SX, SY, SZ), dzs, xe, xo, ye, yo, zs)
    lift = [lift_in[t * 8 : t * 8 + 8, :] if has_lift else jnp.zeros((8, 128), F32) for t in range(4)]
    for x in range(CX):
        for i in range(3):
            ey = dy(x, i, grab(s, SY[i], x))
            ez = dz(x, i)
            new = [[None, None] for _ in range(4)]
            for t in range(4):
                for h in range(2):
                    force = dx(x, i, t, h) + ey[t][h] + ez[t][h]
                    new[t][h] = tile(v, i, x, t, h) + tile(coef, 0, x, t, h) * force
                    vo[i, x, t * 8 : t * 8 + 8, h * 128 : h * 128 + 128] = new[t][h]
            put_y(flip, x, i, new, pye, pyo)
            put_z(gz, x, i, new, pz)
        if has_lift:
            copies.append(pltpu.make_async_copy(vo.at[:, x], v_hbm.at[:, x], sems.at[x]))
            copies[-1].start()
        for t in range(4):
            lift[t] = jnp.where(lane == x, lift[t] - 0.25 * pltpu.roll(new[t][0], x, 1), lift[t])
    for t in range(4):
        lift_out[t * 8 : t * 8 + 8, :] = lift[t]
        if has_lift:
            pz[3 * CX, t * 8 : t * 8 + 8, :] = lift[t]
    put_x_faces(vo, VA, pxe, pxo)
    pxe[XF:, :] = xo[XF:, :]
    pxo[XF:, :] = xe[XF:, :]
    if has_lift:
        for copy in copies:
            copy.wait()


def strain(distance, s, v, coef, dzs, xe, xo, ye, yo, zs, bag_in, so, pxe, pxo, pye, pyo, pz, bag, s_hbm, sems):
    copies = []
    collect(distance, xe, xo, bag)
    gz, flip = lax.axis_index("gz"), odd("gy")

    def done(x, new):
        for i in range(3):
            put_y(flip, x, i, new[SY[i]], pye, pyo)
            put_z(gz, x, i, new[SZ[i]], pz)
        if x < HALF:
            copies.append(pltpu.make_async_copy(so.at[:, x], s_hbm.at[:, x], sems.at[x]))
            copies[-1].start()

    stretch(s, v, coef, dzs, xe, xo, ye, yo, zs, so, done)
    put_x_faces(so, SX, pxe, pxo)
    pxe[XF:, :] = xo[XF:, :]
    pxo[XF:, :] = xe[XF:, :]
    for copy in copies:
        copy.wait()


def finish(s_low, s_high, v_in, coef_in, zs_in, xe, xo, ye, yo, s_hbm, far_hbm, s, v, coef, zs, dzs, sems):
    early = [
        pltpu.make_async_copy(v_in, v, sems.at[0]),
        pltpu.make_async_copy(zs_in, zs, sems.at[1]),
        pltpu.make_async_copy(coef_in, coef, sems.at[2]),
        pltpu.make_async_copy(xe.at[pl.ds(XF, OCR), :], far_hbm, sems.at[3]),
    ]
    parts = [
        pltpu.make_async_copy(ref.at[:, pl.ds(at, 4)], s.at[:, pl.ds(i * 4, 4)], sems.at[4 + i])
        for i, (ref, at) in enumerate(((s_low, 0), (s_low, 4), (s_high, 0), (s_high, 4)))
    ]
    for copy in early + parts:
        copy.start()
    early[0].wait()
    slopes_z(v, dzs, VA)
    for copy in early[1:]:
        copy.wait()
    late = []

    def done(x, new):
        late.append(pltpu.make_async_copy(s.at[:, x], s_hbm.at[:, x], sems.at[8 + x]))
        late[-1].start()

    def ready(x):
        if x % 4 == 0:
            parts[x // 4].wait()

    stretch(s, v, coef, dzs, xe, xo, ye, yo, zs, s, done, ready)
    for copy in late:
        copy.wait()


def stretch(s, v, coef, dzs, xe, xo, ye, yo, zs, so, done, ready=lambda x: None):
    dx, dy, dz = differences(v, (VA, VA, VA), dzs, xe, xo, ye, yo, zs)
    for x in range(CX):
        ready(x)
        ey = [dy(x, c, grab(v, c, x)) for c in range(3)]
        ez = [dz(x, c) for c in range(3)]
        new = [[[None, None] for _ in range(4)] for _ in range(6)]
        for t in range(4):
            for h in range(2):
                ex = [dx(x, c, t, h) for c in range(3)]
                mu = tile(coef, 1, x, t, h)
                bulk = tile(coef, 0, x, t, h) * (ex[0] + ey[1][t][h] + ez[2][t][h])
                mu2 = mu + mu
                change = (
                    bulk + mu2 * ex[0],
                    bulk + mu2 * ey[1][t][h],
                    bulk + mu2 * ez[2][t][h],
                    mu * (ez[1][t][h] + ey[2][t][h]),
                    mu * (ez[0][t][h] + ex[2]),
                    mu * (ey[0][t][h] + ex[1]),
                )
                for c in range(6):
                    new[c][t][h] = tile(s, c, x, t, h) + change[c]
                    so[c, x, t * 8 : t * 8 + 8, h * 128 : h * 128 + 128] = new[c][t][h]
        done(x, new)


def as_column(row, sub, lane):
    parts = []
    for i in range(4):
        part = jnp.broadcast_to(row[:, i * 128 : i * 128 + 128], (128, 128))
        parts.append(jnp.sum(jnp.where(sub == lane, part, 0.0), axis=1, keepdims=True))
    return jnp.concatenate(parts, axis=0)


def address(owner, cell, coef, s, group, slot, code, coef_hbm, s_hbm, sems):
    gx, gy, gz = place()
    copies = [
        pltpu.make_async_copy(s.at[:, pl.ds(HALF, CX - HALF)], s_hbm, sems.at[0]),
        pltpu.make_async_copy(coef, coef_hbm, sems.at[1]),
    ]
    for copy in copies:
        copy.start()
    sub = lax.broadcasted_iota(jnp.int32, (128, 128), 0)
    lane = lax.broadcasted_iota(jnp.int32, (128, 128), 1)
    own = owner[...]
    column = as_column(own.astype(F32), sub, lane).astype(jnp.int32)
    cells = as_column(cell[pl.ds(gy, 1), :].astype(F32) + 1.0, sub, lane)
    wide = lax.broadcasted_iota(jnp.int32, (512, 128), 1)
    same = (jnp.broadcast_to(column, (512, 128)) == wide).astype(F32)
    earlier = (
        lax.broadcasted_iota(jnp.int32, (512, 512), 1) < lax.broadcasted_iota(jnp.int32, (512, 512), 0)
    ).astype(F32)
    before = jnp.dot(earlier, same, preferred_element_type=F32)
    position = jnp.sum(same * before, axis=1, keepdims=True).astype(jnp.int32)
    spot = (column >> 4) * 8 + position
    taken = (jnp.broadcast_to(spot, (512, 128)) == wide).astype(F32)
    slot[...] = taken
    rows = lax.broadcasted_iota(jnp.int32, (8, 512), 0)
    mine = jnp.broadcast_to(own, (8, 512))
    chosen = ((((mine >> 1) & 7) == rows) & ((mine & 1) == gz)).astype(F32)
    group[...] = chosen
    found = jnp.dot(chosen, taken * cells, precision=HIGH, preferred_element_type=F32)
    code[...] = pltpu.roll(found, 64, 1)
    for copy in copies:
        copy.wait()


def pack_lift(lift_here, zs, group, slot, code, out, wide):
    lift = jnp.where(lax.axis_index("gz") == 0, lift_here[...], zs[3 * CX])
    for x in range(CX):
        rows = slice(x * 32, x * 32 + 32)
        wide[rows, :] = slot[rows, :] * jnp.broadcast_to(lift[:, x : x + 1], (32, 128))
    row = jnp.dot(group[...], wide[...], precision=HIGH, preferred_element_type=F32) + code[...]
    for i in range(8):
        out[i * 8 : i * 8 + 8, :] = row


def ocean(arrived, far_in, bag_in, height_in, current_in, wet_in, ho, co, far, bag, height, current, wet, hot, val, pair, src, ends, sweep, sems):
    gx = lax.axis_index("gx")
    copies = [
        pltpu.make_async_copy(a, b, sems.at[i])
        for i, (a, b) in enumerate(
            (
                (far_in, far),
                (bag_in, bag),
                (height_in, height),
                (current_in, current),
                (wet_in, wet),
            )
        )
    ]
    for copy in copies:
        copy.start()
    b16 = jnp.bfloat16
    lane = lax.broadcasted_iota(jnp.int32, (32, 128), 1)
    half = lane < 64
    one, two = arrived[0:32, :], arrived[32:64, :]
    value = jnp.where(half, one, pltpu.roll(two, 64, 1))
    cell = jnp.where(half, pltpu.roll(one, 64, 1), two).astype(jnp.int32) - 1
    band = (lane & 63) >> 3
    pair[0:32, :] = jnp.where(cell >= 0, band * 32 + (cell >> 7), -1).astype(F32)
    pair[32:64, :] = (cell & 127).astype(F32)
    coarse = value.astype(b16).astype(F32)
    val[0:32, :] = coarse
    val[32:64, :] = value - coarse
    lon_rows = lax.broadcasted_iota(jnp.int32, (256, 128), 0).astype(F32).astype(b16)
    lat_rows = lon_rows[0:128, :]
    one16, zero16 = jnp.ones((), b16), jnp.zeros((), b16)

    def line(ref, r, rows):
        return jnp.broadcast_to(jnp.broadcast_to(ref[r : r + 1, :], (16, 128)).astype(b16)[0:1, :], (rows, 128))

    for r in range(32):
        cols = slice(r * 128, r * 128 + 128)
        hot[0:256, cols] = jnp.where(lon_rows == line(pair, r, 256), one16, zero16)
        here = lat_rows == line(pair, 32 + r, 128)
        hot[256:384, cols] = jnp.where(here, line(val, r, 128), zero16)
        hot[384:512, cols] = jnp.where(here, line(val, 32 + r, 128), zero16)
    both = lax.dot_general(
        hot[0:256, :], hot[256:512, :], (((1,), (1,)), ((), ())), preferred_element_type=F32
    )
    src[...] = both[:, 0:128] + both[:, 128:256]
    for copy in copies:
        copy.wait()
    opposite = lax.rem(gx + 4, NB) * OCR
    bag_rows = lambda b, k, n: jnp.where(opposite == b * OCR, far[k : k + n, :], bag[b * OCR + k : b * OCR + k + n, :])
    zero = jnp.zeros((1, LAT), F32)

    def extra(b, k):
        return bag_rows(b, 64 + k, 1)

    head = [extra(b, 8) * src[b * 32 : b * 32 + 1, :] + extra(b, 9) for b in range(NB)] + [zero]
    y0, yl = [], []
    for b in range(NB):
        s_b = src[b * 32 : b * 32 + 32, :]
        y0.append(jnp.sum(bag_rows(b, 0, 32) * s_b, axis=0, keepdims=True) + extra(b, 0) + extra(b, 6) * head[b + 1])
        yl.append(jnp.sum(bag_rows(b, 32, 32) * s_b, axis=0, keepdims=True) + extra(b, 1) + extra(b, 7) * head[b + 1])
    a = [zero] * (NB + 1)
    m = [zero] * (NB + 1)
    zc = [zero] * NB
    zl = [zero] * NB
    for b in reversed(range(NB)):
        scale = 1.0 / (1.0 - extra(b, 5) * m[b + 1])
        zc[b] = scale * (yl[b] + extra(b, 5) * a[b + 1])
        zl[b] = scale * extra(b, 3)
        a[b] = y0[b] + extra(b, 4) * (a[b + 1] + m[b + 1] * zc[b])
        m[b] = extra(b, 2) + extra(b, 4) * m[b + 1] * zl[b]
    z = zero
    ends[0:1, :] = zero
    ends[16 + NB : 17 + NB, :] = zero
    for b in range(NB):
        ends[16 + b : 17 + b, :] = a[b] + m[b] * z
        z = zc[b] + zl[b] * z
        ends[b + 1 : b + 2, :] = z
    left = ends[pl.ds(gx, 1), :]
    right = ends[pl.ds(gx + 17, 1), :]
    wet_float = wet[...].astype(F32)
    new_height = wet_float * (height[...] + src[pl.ds(pl.multiple_of(gx * 32, 32), 32), :])
    ho[...] = new_height
    sweep[0:32, :] = new_height
    nxt = lax.rem(gx + 1, NB)
    next_head = bag[pl.ds(nxt * OCR + 72, 1), :] * src[pl.ds(nxt * 32, 1), :] + bag[pl.ds(nxt * OCR + 73, 1), :]
    sweep[32:33, :] = jnp.where(gx == NB - 1, 0.0, next_head)
    forced = bag[FAC + 96 : FAC + 128, :] * (-400.0 * (sweep[1:33, :] - new_height))
    sweep[40:72, :] = forced
    run = zero
    offs = [None] * LON
    for j in reversed(range(LON)):
        offs[j] = run = sweep[40 + j : 41 + j, :] + bag[FAC + 64 + j : FAC + 65 + j, :] * run
    run = zero
    for j in range(LON):
        run = offs[j] + bag[FAC + 64 + j : FAC + 65 + j, :] * run
        sweep[40 + j : 41 + j, :] = run
    increment = sweep[40:72, :] + bag[FAC : FAC + 32, :] * left + bag[FAC + 32 : FAC + 64, :] * right
    co[...] = wet_float * (current[...] + increment)


def swap(value, axis, first):
    n = lax.axis_size(axis)
    pairs = [(i, (i + 1) % n) for i in range(0 if first else 1, n, 2)]
    return lax.ppermute(value, axis, pairs + [(j, i) for i, j in pairs])


def exchange(payload):
    pxe, pxo, pye, pyo, pz = payload
    zs = swap(pz, "gz", True)
    xe, xo = swap(pxe, "gx", True), swap(pxo, "gx", False)
    ye, yo = swap(pye, "gy", True), swap(pyo, "gy", False)
    return xe, xo, ye, yo, zs


def local(velocity, stress, material, properties, owner_map, cell_map, height, current, sea_depth, wet_mask):
    scaled = 0.125 * properties.T
    tab = jnp.pad(jnp.concatenate([scaled[2:3], scaled[0:1], scaled[1:2]]), ((0, 0), (0, 112)))
    tab = jnp.repeat(tab, 8, axis=0)
    pz_shape, pz_lift = shape(3 * CX, CY, 128), shape(3 * CX + 1, CY, 128)
    v_shape, s_shape = resident(3, CX, CY, CZ), resident(6, CX, CY, CZ)
    bag_shape = shape(BAG, 128)
    plane_z = pltpu.VMEM((3, CX, CY, CZ), F32)
    *sent, bag = call(
        prepare,
        PAYLOAD + [pz_shape, bag_shape],
        *outside(stress, sea_depth, height, wet_mask),
        ins=[HB] * 4,
        scratch=[
            pltpu.VMEM((104, LAT), F32),
            pltpu.VMEM((LON, LAT), F32),
            pltpu.VMEM((LON, LAT), F32),
            pltpu.VMEM((LON, LAT), jnp.int32),
            pltpu.VMEM((2, 3, CX, 8, CZ), F32),
            pltpu.SemaphoreType.DMA((24,)),
        ],
    )
    r1 = exchange(sent)
    velocity, stress, mat, coef, dzs, owner, cell = call(
        fetch,
        [
            v_shape, s_shape, pltpu.VMEM((CX, CY, CZ), jnp.int32), resident(1, CX, CY, CZ), v_shape,
            pltpu.VMEM((1, 512), jnp.int32), pltpu.VMEM((8, 512), jnp.int32),
        ],
        *outside(velocity, stress, material, owner_map.reshape(64, 1, 512), cell_map), tab,
        ins=[HB] * 5 + [VM],
        scratch=[pltpu.SemaphoreType.DMA((7,))],
    )
    v1, *sent, lift, bag = call(
        functools.partial(move, 1, False),
        [v_shape] + PAYLOAD + [pz_shape, shape(32, 128), bag_shape],
        velocity, stress, coef, dzs, *r1, bag,
        aliases={0: 0, 9: 7},
    )
    r2 = exchange(sent)
    mat, v1 = lax.optimization_barrier((mat, v1))
    coef2, dzs = call(lame, [resident(2, CX, CY, CZ), v_shape], tab, mat, v1)
    s1, *sent, bag, s_low = call(
        functools.partial(strain, 2),
        [s_shape] + PAYLOAD + [pz_shape, bag_shape] + [pltpu.HBM((6, HALF, CY, CZ), F32)],
        stress, v1, coef2, dzs, *r2, bag,
        outs_at=[VM] * 7 + [HB],
        scratch=[pltpu.SemaphoreType.DMA((HALF,))], aliases={0: 0, 9: 6},
    )
    r3 = exchange(sent)
    owner, cell, s1 = lax.optimization_barrier((owner, cell, s1))
    group, slot, code, coef_copy, s_high = call(
        address,
        [shape(8, 512), shape(512, 128), shape(8, 128)]
        + [pltpu.HBM((2, CX, CY, CZ), F32), pltpu.HBM((6, CX - HALF, CY, CZ), F32)],
        owner, cell, coef2, s1,
        outs_at=[VM] * 3 + [HB] * 2,
        scratch=[pltpu.SemaphoreType.DMA((2,))],
    )
    (dzs,) = call(functools.partial(slopes_z, comps=SZ), [v_shape], s1)
    r3, group, slot, code, coef_copy, s_high = lax.optimization_barrier((r3, group, slot, code, coef_copy, s_high))
    *sent, lift, v_out, bag = call(
        functools.partial(move, 3, True),
        PAYLOAD + [pz_lift, shape(32, 128)] + [pltpu.HBM(dims, F32) for dims in ((3, CX, CY, CZ), (BAG, 128))],
        v1, s1, coef, dzs, *r3, bag, lift,
        outs_at=[VM] * 6 + [HB] * 2,
        scratch=[plane_z, pltpu.VMEM((BAG, 128), F32), pltpu.SemaphoreType.DMA((CX + 1,))],
    )
    *r4, zs = exchange(sent)
    (out,) = call(
        pack_lift,
        [shape(64, 128)],
        lift, zs, group, slot, code,
        scratch=[pltpu.VMEM((512, 128), F32)],
    )
    s2, far = call(
        finish,
        [pltpu.HBM(dims, F32) for dims in ((6, CX, CY, CZ), (OCR, 128))],
        *outside(s_low, s_high, v_out, coef_copy, zs), *r4,
        ins=[HB] * 5 + [VM] * 4,
        outs_at=[HB] * 2,
        scratch=[
            pltpu.VMEM((6, CX, CY, CZ), F32),
            plane_z,
            pltpu.VMEM((2, CX, CY, CZ), F32),
            pltpu.VMEM((3 * CX + 1, CY, 128), F32),
            plane_z,
            pltpu.SemaphoreType.DMA((8 + CX,)),
        ],
    )
    arrived = lax.all_to_all(out, ("gx", "gy"), split_axis=0, concat_axis=0, tiled=True)
    block = pltpu.VMEM((LON, LAT), F32)
    height_out, current_out = call(
        ocean, [shape(LON, LAT)] * 2,
        arrived, *outside(far, bag, height, current, wet_mask),
        ins=[VM] + [HB] * 5,
        scratch=[
            pltpu.VMEM((OCR, 128), F32), pltpu.VMEM((BAG, 128), F32),
            block, block, pltpu.VMEM((LON, LAT), jnp.int32),
            pltpu.VMEM((512, 4096), jnp.bfloat16),
            pltpu.VMEM((64, 128), F32),
            pltpu.VMEM((64, 128), F32),
            pltpu.VMEM((256, 128), F32),
            pltpu.VMEM((32, 128), F32),
            pltpu.VMEM((72, 128), F32),
            pltpu.SemaphoreType.DMA((5,)),
        ],
    )
    return v_out, s2, height_out, current_out


def solution(mesh):
    return jax.shard_map(
        local,
        mesh=mesh,
        in_specs=(
            P(None, "gx", "gy", "gz"),
            P(None, "gx", "gy", "gz"),
            P("gx", "gy", "gz"),
            P(),
            P(),
            P(),
            P("gx", ("gy", "gz")),
            P("gx", ("gy", "gz")),
            P("gx", ("gy", "gz")),
            P("gx", ("gy", "gz")),
        ),
        out_specs=(
            P(None, "gx", "gy", "gz"),
            P(None, "gx", "gy", "gz"),
            P("gx", ("gy", "gz")),
            P("gx", ("gy", "gz")),
        ),
        check_vma=False,
    )
```

```python
import functools

import jax
import jax.numpy as jnp
from jax import lax
from jax.experimental import pallas as pl
from jax.experimental.pallas import tpu as pltpu
from jax.sharding import PartitionSpec as P

F32 = jnp.float32
CX, CY, CZ = 16, 32, 256
LAT = 128
LON = 32
NB = 8
SX, SY, SZ = (0, 5, 4), (5, 1, 3), (4, 3, 2)
VA = (0, 1, 2)
XF = 3 * 2 * CY
OCR = 80
XR = XF + OCR
YR = 3 * 2 * CX
FAC = NB * OCR
BAG = FAC + 128
HIGH = lax.Precision.HIGHEST
VM = pl.BlockSpec(memory_space=pltpu.VMEM)
HB = pl.BlockSpec(memory_space=pltpu.HBM)


def iotas():
    return (
        lax.broadcasted_iota(jnp.int32, (8, 128), 0),
        lax.broadcasted_iota(jnp.int32, (8, 128), 1),
    )


def tile(ref, c, x, t, h):
    return ref[c, x, t * 8 : t * 8 + 8, h * 128 : h * 128 + 128]


def call(body, outs, *args, scratch=(), ins=None, outs_at=None, aliases=None, limit=20):
    return pl.pallas_call(
        body,
        out_shape=outs,
        in_specs=[VM] * len(args) if ins is None else ins,
        out_specs=[VM] * len(outs) if outs_at is None else outs_at,
        scratch_shapes=list(scratch),
        input_output_aliases=aliases or {},
        compiler_params=pltpu.CompilerParams(vmem_limit_bytes=limit * 1024 * 1024),
    )(*args)


def place():
    return lax.axis_index("gx"), lax.axis_index("gy"), lax.axis_index("gz")


def shape(*dims):
    return jax.ShapeDtypeStruct(dims, F32)


PARTS = 2
HALF = 8
def resident(*dims):
    return pltpu.VMEM(dims, F32)


def outside(*arrays):
    return [pltpu.with_memory_space_constraint(a, pltpu.HBM) for a in arrays]


PAYLOAD = [shape(XR, 128), shape(XR, 128), shape(YR, 128), shape(YR, 128)]


def odd(axis):
    return lax.rem(lax.axis_index(axis), 2) == 1


def put_x_faces(ref, comps, pxe, pxo):
    flip = odd("gx")
    for i, c in enumerate(comps):
        for h in range(2):
            rows = slice(i * 64 + h * 32, i * 64 + h * 32 + 32)
            lanes = slice(h * 128, h * 128 + 128)
            above, below = ref[c, CX - 1, :, lanes], ref[c, 0, :, lanes]
            pxe[rows, :] = jnp.where(flip, below, above)
            pxo[rows, :] = jnp.where(flip, above, below)


def put_y(flip, x, i, tiles, pye, pyo):
    for h in range(2):
        row = i * 32 + h * 16 + x
        above, below = tiles[3][h][7:8, :], tiles[0][h][0:1, :]
        pye[row : row + 1, :] = jnp.where(flip, below, above)
        pyo[row : row + 1, :] = jnp.where(flip, above, below)


def put_z(gz, x, i, tiles, pz):
    for t in range(4):
        pz[i * CX + x, t * 8 : t * 8 + 8, :] = jnp.where(gz == 0, tiles[t][1], tiles[t][0])


def prepare(s, depth, height, wet, pxe, pxo, pye, pyo, pz, bag, rows, high, deep, damp, edge, sems):
    gx, _, gz = place()
    copies = []

    def start(src, dst):
        copy = pltpu.make_async_copy(src, dst, sems.at[len(copies)])
        copy.start()
        copies.append(copy)

    start(depth, deep)
    start(height, high)
    start(wet, damp)
    first_face = jnp.where(odd("gx"), 0, CX - 1)
    flip = odd("gy")
    for i, c in enumerate(SX):
        for h in range(2):
            lanes = pl.ds(h * 128, 128)
            start(s.at[c, first_face, :, lanes], pxe.at[pl.ds(i * 64 + h * 32, 32), :])
            start(s.at[c, CX - 1 - first_face, :, lanes], pxo.at[pl.ds(i * 64 + h * 32, 32), :])
    for i, c in enumerate(SY):
        start(s.at[c, :, pl.ds(24, 8), :], edge.at[0, i])
        start(s.at[c, :, pl.ds(0, 8), :], edge.at[1, i])
    lanes = pl.ds(pl.multiple_of(128 * (1 - gz), 128), 128)
    for i, c in enumerate(SZ):
        start(s.at[c, :, :, lanes], pz.at[pl.ds(i * CX, CX)])
    for copy in copies[:3]:
        copy.wait()
    factor(deep, high, damp, pxe, bag, rows)
    pxo[XF:, :] = pxe[XF:, :]
    bag[pl.ds(pl.multiple_of(gx * OCR, 8), OCR), :] = pxe[XF:, :]
    for copy in copies[3:]:
        copy.wait()
    for i in range(3):
        for x in range(CX):
            for h in range(2):
                row = i * 32 + h * 16 + x
                lanes = slice(h * 128, h * 128 + 128)
                above, below = edge[0, i, x, 7:8, lanes], edge[1, i, x, 0:1, lanes]
                pye[row : row + 1, :] = jnp.where(flip, below, above)
                pyo[row : row + 1, :] = jnp.where(flip, above, below)


def factor(depth, height, wet, pxe, bag, rows):
    spread = depth[...] * depth[...] / 3.0
    scale = 1.0 / spread
    rows[0:32, :] = scale
    for base, order in ((32, reversed(range(LON))), (65, range(LON))):
        value, slope = jnp.ones((1, LAT), F32), jnp.ones((1, LAT), F32)
        last = base + (LON if base == 32 else 0)
        rows[last : last + 1, :] = value
        for j in order:
            slope = slope + value * rows[j : j + 1, :]
            value = value + slope
            at = base + (j if base == 32 else j + 1)
            rows[at : at + 1, :] = value
    down, down_next = rows[32:64, :], rows[33:65, :]
    up = rows[65:97, :]
    top, end = 1.0 / rows[32:33, :], 1.0 / rows[97:98, :]
    w = down_next / down
    left, right = down_next * top, up * end
    p_now, q_now = left * scale, right * scale
    bag[FAC : FAC + 32, :] = left
    bag[FAC + 32 : FAC + 64, :] = right
    bag[FAC + 64 : FAC + 96, :] = w
    bag[FAC + 96 : FAC + 128, :] = w * scale
    row = lax.broadcasted_iota(jnp.int32, (LON, LAT), 0)
    p_before = jnp.where(row == 0, 0.0, pltpu.roll(p_now, 1, 0))
    q_before = jnp.where(row == 0, 0.0, pltpu.roll(q_now, 1, 0))
    first_left, left_run = left[0:1, :], left[31:32, :]
    first_right, right_run = right[0:1, :], right[31:32, :]
    wet_float = wet[...].astype(F32)
    high = height[...]
    a1 = 400.0 * (p_now - p_before) * wet_float
    a2 = 400.0 * (q_now - q_before) * wet_float
    pxe[XF : XF + 32, :] = a1
    pxe[XF + 32 : XF + 64, :] = a2
    base = XF + 64
    pxe[base : base + 1, :] = jnp.sum(a1 * high, axis=0, keepdims=True)
    pxe[base + 1 : base + 2, :] = jnp.sum(a2 * high, axis=0, keepdims=True)
    pxe[base + 2 : base + 3, :] = first_left
    pxe[base + 3 : base + 4, :] = left_run
    pxe[base + 4 : base + 5, :] = first_right
    pxe[base + 5 : base + 6, :] = right_run
    pxe[base + 6 : base + 7, :] = -400.0 * p_now[31:32, :]
    pxe[base + 7 : base + 8, :] = -400.0 * q_now[31:32, :]
    pxe[base + 8 : base + 9, :] = wet_float[0:1, :]
    pxe[base + 9 : base + 10, :] = wet_float[0:1, :] * high[0:1, :]
    pxe[base + 10 : base + 16, :] = jnp.zeros((6, LAT), F32)


def slopes_z(src, out, comps):
    k = lax.broadcasted_iota(jnp.int32, (CZ, CZ), 0)
    n = lax.broadcasted_iota(jnp.int32, (CZ, CZ), 1)
    step = jnp.where(k == n + 1, 1.0, 0.0) - jnp.where(k == n - 1, 1.0, 0.0)
    step = step.astype(jnp.bfloat16)
    for i, c in enumerate(comps):
        full = src[c].reshape(CX * CY, CZ)
        total = None
        for _ in range(PARTS):
            part = full.astype(jnp.bfloat16)
            full = full - part.astype(F32)
            product = jnp.dot(part, step, preferred_element_type=F32)
            total = product if total is None else total + product
        out[i] = total.reshape(CX, CY, CZ)


def differences(src, comps, dzs, xe, xo, ye, yo, zs):
    gx, gy, gz = place()
    sub, lane = iotas()
    cx, cy, cz = comps

    def flag(cond):
        return jnp.where(cond, 1.0, 0.0).astype(F32)

    m_xd, m_xu = flag(gx > 0), flag(gx < NB - 1)
    m_yd, m_yu = flag(gy > 0), flag(gy < NB - 1)
    top, bottom = sub == 7, sub == 0
    far, near = (lane == 127) & (gz == 0), (lane == 0) & (gz == 1)
    shift = jnp.where(gz == 0, 127, 1)

    flip_x, flip_y = odd("gx"), odd("gy")

    def halo_x(one, two, mask, i, t, h):
        row = i * 64 + h * 32 + t * 8
        return jnp.where(flip_x, one[row : row + 8, :], two[row : row + 8, :]) * mask

    def halo_y(one, two, mask, row):
        line = jnp.where(flip_y, one[row : row + 1, :], two[row : row + 1, :]) * mask
        return jnp.broadcast_to(line, (8, 128))

    def dx(x, i, t, h):
        c = cx[i]
        low = halo_x(xe, xo, m_xd, i, t, h) if x == 0 else tile(src, c, x - 1, t, h)
        high = halo_x(xo, xe, m_xu, i, t, h) if x == CX - 1 else tile(src, c, x + 1, t, h)
        return high - low

    def dy(x, i, tiles):
        out = [[None, None] for _ in range(4)]
        for h in range(2):
            up = [pltpu.roll(tiles[t][h], 7, 0) for t in range(4)]
            dn = [pltpu.roll(tiles[t][h], 1, 0) for t in range(4)]
            row = i * 32 + h * 16 + x
            up.append(halo_y(yo, ye, m_yu, row))
            dn.insert(0, halo_y(ye, yo, m_yd, row))
            for t in range(4):
                out[t][h] = jnp.where(top, up[t + 1], up[t]) - jnp.where(bottom, dn[t], dn[t + 1])
        return out

    def dz(x, i):
        out = [[None, None] for _ in range(4)]
        for t in range(4):
            slab = pltpu.roll(zs[i * CX + x, t * 8 : t * 8 + 8, :], shift, 1)
            out[t][0] = tile(dzs, i, x, t, 0) - jnp.where(near, slab, 0.0)
            out[t][1] = tile(dzs, i, x, t, 1) + jnp.where(far, slab, 0.0)
        return out

    return dx, dy, dz


def grab(ref, c, x):
    return [[tile(ref, c, x, t, h) for h in range(2)] for t in range(4)]


def lookup(tab, mat, coef, rows):
    table = [tab[i * 8 : i * 8 + 8, :] for i in rows]

    def plane(x, carry):
        for t in range(4):
            for h in range(2):
                index = mat[x, t * 8 : t * 8 + 8, h * 128 : h * 128 + 128]
                for i in range(len(rows)):
                    coef[i, x, t * 8 : t * 8 + 8, h * 128 : h * 128 + 128] = jnp.take_along_axis(
                        table[i], index, axis=1, mode="promise_in_bounds"
                    )
        return carry

    lax.fori_loop(0, CX, plane, 0)


def fetch(v_hbm, s_hbm, mat_hbm, owners, cell_rows, tab, v, s, mat, coef, dzs, owner, cell, sems):
    gx, gy, _ = place()
    wanted = [
        (s_hbm.at[pl.ds(2, 3)], s.at[pl.ds(2, 3)]),
        (mat_hbm, mat),
        (s_hbm.at[pl.ds(0, 2)], s.at[pl.ds(0, 2)]),
        (s_hbm.at[5], s.at[5]),
        (v_hbm, v),
        (owners.at[gx * NB + gy], owner),
        (cell_rows.at[pl.ds(pl.multiple_of(gx * NB, 8), 8), :], cell),
    ]
    copies = [pltpu.make_async_copy(a, b, sems.at[i]) for i, (a, b) in enumerate(wanted)]
    for copy in copies:
        copy.start()
    copies[0].wait()
    slopes_z(s, dzs, SZ)
    copies[1].wait()
    lookup(tab, mat, coef, (0,))
    for copy in copies[2:]:
        copy.wait()


def lame(tab, mat, v, coef, dzs):
    slopes_z(v, dzs, VA)
    lookup(tab, mat, coef, (1, 2))


def collect(distance, xe, xo, bag):
    gx = lax.axis_index("gx")
    first = jnp.where(odd("gx"), NB - distance, distance)
    for ref, steps in ((xe, first), (xo, NB - first)):
        row = pl.multiple_of(lax.rem(gx + steps, NB) * OCR, 8)
        bag[pl.ds(row, OCR), :] = ref[XF:, :]


def move(distance, has_lift, v, s, coef, dzs, xe, xo, ye, yo, zs, bag_in, *refs):
    if has_lift:
        lift_in, pxe, pxo, pye, pyo, pz, lift_out, v_hbm, bag_hbm, vo, bag, sems = refs
        copies = [pltpu.make_async_copy(bag, bag_hbm, sems.at[CX])]
        bag[...] = bag_in[...]
    else:
        vo, pxe, pxo, pye, pyo, pz, lift_out, bag = refs
    gz = lax.axis_index("gz")
    flip = odd("gy")
    sub, lane = iotas()
    collect(distance, xe, xo, bag)
    if has_lift:
        copies[0].start()
    dx, dy, dz = differences(s, (SX, SY, SZ), dzs, xe, xo, ye, yo, zs)
    lift = [lift_in[t * 8 : t * 8 + 8, :] if has_lift else jnp.zeros((8, 128), F32) for t in range(4)]
    for x in range(CX):
        for i in range(3):
            ey = dy(x, i, grab(s, SY[i], x))
            ez = dz(x, i)
            new = [[None, None] for _ in range(4)]
            for t in range(4):
                for h in range(2):
                    force = dx(x, i, t, h) + ey[t][h] + ez[t][h]
                    new[t][h] = tile(v, i, x, t, h) + tile(coef, 0, x, t, h) * force
                    vo[i, x, t * 8 : t * 8 + 8, h * 128 : h * 128 + 128] = new[t][h]
            put_y(flip, x, i, new, pye, pyo)
            put_z(gz, x, i, new, pz)
        if has_lift:
            copies.append(pltpu.make_async_copy(vo.at[:, x], v_hbm.at[:, x], sems.at[x]))
            copies[-1].start()
        for t in range(4):
            lift[t] = jnp.where(lane == x, lift[t] - 0.25 * pltpu.roll(new[t][0], x, 1), lift[t])
    for t in range(4):
        lift_out[t * 8 : t * 8 + 8, :] = lift[t]
        if has_lift:
            pz[3 * CX, t * 8 : t * 8 + 8, :] = lift[t]
    put_x_faces(vo, VA, pxe, pxo)
    pxe[XF:, :] = xo[XF:, :]
    pxo[XF:, :] = xe[XF:, :]
    if has_lift:
        for copy in copies:
            copy.wait()


def strain(distance, s, v, coef, dzs, xe, xo, ye, yo, zs, bag_in, so, pxe, pxo, pye, pyo, pz, bag, s_hbm, sems):
    copies = []
    collect(distance, xe, xo, bag)
    gz, flip = lax.axis_index("gz"), odd("gy")

    def done(x, new):
        for i in range(3):
            put_y(flip, x, i, new[SY[i]], pye, pyo)
            put_z(gz, x, i, new[SZ[i]], pz)
        if x < HALF:
            copies.append(pltpu.make_async_copy(so.at[:, x], s_hbm.at[:, x], sems.at[x]))
            copies[-1].start()

    stretch(s, v, coef, dzs, xe, xo, ye, yo, zs, so, done)
    put_x_faces(so, SX, pxe, pxo)
    pxe[XF:, :] = xo[XF:, :]
    pxo[XF:, :] = xe[XF:, :]
    for copy in copies:
        copy.wait()


def finish(s_low, s_high, v_in, coef_in, zs_in, xe, xo, ye, yo, s_hbm, far_hbm, s, v, coef, zs, dzs, sems):
    early = [
        pltpu.make_async_copy(v_in, v, sems.at[0]),
        pltpu.make_async_copy(zs_in, zs, sems.at[1]),
        pltpu.make_async_copy(coef_in, coef, sems.at[2]),
        pltpu.make_async_copy(xe.at[pl.ds(XF, OCR), :], far_hbm, sems.at[3]),
    ]
    parts = [
        pltpu.make_async_copy(ref.at[:, pl.ds(at, 4)], s.at[:, pl.ds(i * 4, 4)], sems.at[4 + i])
        for i, (ref, at) in enumerate(((s_low, 0), (s_low, 4), (s_high, 0), (s_high, 4)))
    ]
    for copy in early + parts:
        copy.start()
    early[0].wait()
    slopes_z(v, dzs, VA)
    for copy in early[1:]:
        copy.wait()
    late = []

    def done(x, new):
        late.append(pltpu.make_async_copy(s.at[:, x], s_hbm.at[:, x], sems.at[8 + x]))
        late[-1].start()

    def ready(x):
        if x % 4 == 0:
            parts[x // 4].wait()

    stretch(s, v, coef, dzs, xe, xo, ye, yo, zs, s, done, ready)
    for copy in late:
        copy.wait()


def stretch(s, v, coef, dzs, xe, xo, ye, yo, zs, so, done, ready=lambda x: None):
    dx, dy, dz = differences(v, (VA, VA, VA), dzs, xe, xo, ye, yo, zs)
    for x in range(CX):
        ready(x)
        ey = [dy(x, c, grab(v, c, x)) for c in range(3)]
        ez = [dz(x, c) for c in range(3)]
        new = [[[None, None] for _ in range(4)] for _ in range(6)]
        for t in range(4):
            for h in range(2):
                ex = [dx(x, c, t, h) for c in range(3)]
                mu = tile(coef, 1, x, t, h)
                bulk = tile(coef, 0, x, t, h) * (ex[0] + ey[1][t][h] + ez[2][t][h])
                mu2 = mu + mu
                change = (
                    bulk + mu2 * ex[0],
                    bulk + mu2 * ey[1][t][h],
                    bulk + mu2 * ez[2][t][h],
                    mu * (ez[1][t][h] + ey[2][t][h]),
                    mu * (ez[0][t][h] + ex[2]),
                    mu * (ey[0][t][h] + ex[1]),
                )
                for c in range(6):
                    new[c][t][h] = tile(s, c, x, t, h) + change[c]
                    so[c, x, t * 8 : t * 8 + 8, h * 128 : h * 128 + 128] = new[c][t][h]
        done(x, new)


def as_column(row, sub, lane):
    parts = []
    for i in range(4):
        part = jnp.broadcast_to(row[:, i * 128 : i * 128 + 128], (128, 128))
        parts.append(jnp.sum(jnp.where(sub == lane, part, 0.0), axis=1, keepdims=True))
    return jnp.concatenate(parts, axis=0)


def address(owner, cell, coef, s, group, slot, code, coef_hbm, s_hbm, sems):
    gx, gy, gz = place()
    copies = [
        pltpu.make_async_copy(s.at[:, pl.ds(HALF, CX - HALF)], s_hbm, sems.at[0]),
        pltpu.make_async_copy(coef, coef_hbm, sems.at[1]),
    ]
    for copy in copies:
        copy.start()
    sub = lax.broadcasted_iota(jnp.int32, (128, 128), 0)
    lane = lax.broadcasted_iota(jnp.int32, (128, 128), 1)
    own = owner[...]
    column = as_column(own.astype(F32), sub, lane).astype(jnp.int32)
    cells = as_column(cell[pl.ds(gy, 1), :].astype(F32) + 1.0, sub, lane)
    wide = lax.broadcasted_iota(jnp.int32, (512, 128), 1)
    same = (jnp.broadcast_to(column, (512, 128)) == wide).astype(F32)
    earlier = (
        lax.broadcasted_iota(jnp.int32, (512, 512), 1) < lax.broadcasted_iota(jnp.int32, (512, 512), 0)
    ).astype(F32)
    before = jnp.dot(earlier, same, preferred_element_type=F32)
    position = jnp.sum(same * before, axis=1, keepdims=True).astype(jnp.int32)
    spot = (column >> 4) * 8 + position
    taken = (jnp.broadcast_to(spot, (512, 128)) == wide).astype(F32)
    slot[...] = taken
    rows = lax.broadcasted_iota(jnp.int32, (8, 512), 0)
    mine = jnp.broadcast_to(own, (8, 512))
    chosen = ((((mine >> 1) & 7) == rows) & ((mine & 1) == gz)).astype(F32)
    group[...] = chosen
    found = jnp.dot(chosen, taken * cells, precision=HIGH, preferred_element_type=F32)
    code[...] = pltpu.roll(found, 64, 1)
    for copy in copies:
        copy.wait()


def pack_lift(lift_here, zs, group, slot, code, out, wide):
    lift = jnp.where(lax.axis_index("gz") == 0, lift_here[...], zs[3 * CX])
    for x in range(CX):
        rows = slice(x * 32, x * 32 + 32)
        wide[rows, :] = slot[rows, :] * jnp.broadcast_to(lift[:, x : x + 1], (32, 128))
    row, rest = code[...], wide[...]
    for _ in range(3):
        part = rest.astype(jnp.bfloat16).astype(F32)
        rest = rest - part
        row = row + jnp.dot(group[...], part, preferred_element_type=F32)
    for i in range(8):
        out[i * 8 : i * 8 + 8, :] = row


def ocean(arrived, far_in, bag_in, height_in, current_in, wet_in, ho, co, far, bag, height, current, wet, hot, val, pair, src, ends, sweep, sems):
    gx = lax.axis_index("gx")
    copies = [
        pltpu.make_async_copy(a, b, sems.at[i])
        for i, (a, b) in enumerate(
            (
                (far_in, far),
                (bag_in, bag),
                (height_in, height),
                (current_in, current),
                (wet_in, wet),
            )
        )
    ]
    for copy in copies:
        copy.start()
    b16 = jnp.bfloat16
    lane = lax.broadcasted_iota(jnp.int32, (32, 128), 1)
    half = lane < 64
    one, two = arrived[0:32, :], arrived[32:64, :]
    value = jnp.where(half, one, pltpu.roll(two, 64, 1))
    cell = jnp.where(half, pltpu.roll(one, 64, 1), two).astype(jnp.int32) - 1
    band = (lane & 63) >> 3
    pair[0:32, :] = jnp.where(cell >= 0, band * 32 + (cell >> 7), -1).astype(F32)
    pair[32:64, :] = (cell & 127).astype(F32)
    coarse = value.astype(b16).astype(F32)
    val[0:32, :] = coarse
    val[32:64, :] = value - coarse
    lon_rows = lax.broadcasted_iota(jnp.int32, (256, 128), 0).astype(F32).astype(b16)
    lat_rows = lon_rows[0:128, :]
    one16, zero16 = jnp.ones((), b16), jnp.zeros((), b16)

    def line(ref, r, rows):
        return jnp.broadcast_to(jnp.broadcast_to(ref[r : r + 1, :], (16, 128)).astype(b16)[0:1, :], (rows, 128))

    for r in range(32):
        cols = slice(r * 128, r * 128 + 128)
        hot[0:256, cols] = jnp.where(lon_rows == line(pair, r, 256), one16, zero16)
        here = lat_rows == line(pair, 32 + r, 128)
        hot[256:384, cols] = jnp.where(here, line(val, r, 128), zero16)
        hot[384:512, cols] = jnp.where(here, line(val, 32 + r, 128), zero16)
    both = lax.dot_general(
        hot[0:256, :], hot[256:512, :], (((1,), (1,)), ((), ())), preferred_element_type=F32
    )
    src[...] = both[:, 0:128] + both[:, 128:256]
    for copy in copies:
        copy.wait()
    opposite = lax.rem(gx + 4, NB) * OCR
    bag_rows = lambda b, k, n: jnp.where(opposite == b * OCR, far[k : k + n, :], bag[b * OCR + k : b * OCR + k + n, :])
    zero = jnp.zeros((1, LAT), F32)

    def extra(b, k):
        return bag_rows(b, 64 + k, 1)

    head = [extra(b, 8) * src[b * 32 : b * 32 + 1, :] + extra(b, 9) for b in range(NB)] + [zero]
    y0, yl = [], []
    for b in range(NB):
        s_b = src[b * 32 : b * 32 + 32, :]
        y0.append(jnp.sum(bag_rows(b, 0, 32) * s_b, axis=0, keepdims=True) + extra(b, 0) + extra(b, 6) * head[b + 1])
        yl.append(jnp.sum(bag_rows(b, 32, 32) * s_b, axis=0, keepdims=True) + extra(b, 1) + extra(b, 7) * head[b + 1])
    a = [zero] * (NB + 1)
    m = [zero] * (NB + 1)
    zc = [zero] * NB
    zl = [zero] * NB
    for b in reversed(range(NB)):
        scale = 1.0 / (1.0 - extra(b, 5) * m[b + 1])
        zc[b] = scale * (yl[b] + extra(b, 5) * a[b + 1])
        zl[b] = scale * extra(b, 3)
        a[b] = y0[b] + extra(b, 4) * (a[b + 1] + m[b + 1] * zc[b])
        m[b] = extra(b, 2) + extra(b, 4) * m[b + 1] * zl[b]
    z = zero
    ends[0:1, :] = zero
    ends[16 + NB : 17 + NB, :] = zero
    for b in range(NB):
        ends[16 + b : 17 + b, :] = a[b] + m[b] * z
        z = zc[b] + zl[b] * z
        ends[b + 1 : b + 2, :] = z
    left = ends[pl.ds(gx, 1), :]
    right = ends[pl.ds(gx + 17, 1), :]
    wet_float = wet[...].astype(F32)
    new_height = wet_float * (height[...] + src[pl.ds(pl.multiple_of(gx * 32, 32), 32), :])
    ho[...] = new_height
    sweep[0:32, :] = new_height
    nxt = lax.rem(gx + 1, NB)
    next_head = bag[pl.ds(nxt * OCR + 72, 1), :] * src[pl.ds(nxt * 32, 1), :] + bag[pl.ds(nxt * OCR + 73, 1), :]
    sweep[32:33, :] = jnp.where(gx == NB - 1, 0.0, next_head)
    forced = bag[FAC + 96 : FAC + 128, :] * (-400.0 * (sweep[1:33, :] - new_height))
    sweep[40:72, :] = forced
    run = zero
    offs = [None] * LON
    for j in reversed(range(LON)):
        offs[j] = run = sweep[40 + j : 41 + j, :] + bag[FAC + 64 + j : FAC + 65 + j, :] * run
    run = zero
    for j in range(LON):
        run = offs[j] + bag[FAC + 64 + j : FAC + 65 + j, :] * run
        sweep[40 + j : 41 + j, :] = run
    increment = sweep[40:72, :] + bag[FAC : FAC + 32, :] * left + bag[FAC + 32 : FAC + 64, :] * right
    co[...] = wet_float * (current[...] + increment)


def swap(value, axis, first):
    n = lax.axis_size(axis)
    pairs = [(i, (i + 1) % n) for i in range(0 if first else 1, n, 2)]
    return lax.ppermute(value, axis, pairs + [(j, i) for i, j in pairs])


def exchange(payload):
    pxe, pxo, pye, pyo, pz = payload
    zs = swap(pz, "gz", True)
    xe, xo = swap(pxe, "gx", True), swap(pxo, "gx", False)
    ye, yo = swap(pye, "gy", True), swap(pyo, "gy", False)
    return xe, xo, ye, yo, zs


def local(velocity, stress, material, properties, owner_map, cell_map, height, current, sea_depth, wet_mask):
    scaled = 0.125 * properties.T
    tab = jnp.pad(jnp.concatenate([scaled[2:3], scaled[0:1], scaled[1:2]]), ((0, 0), (0, 112)))
    tab = jnp.repeat(tab, 8, axis=0)
    pz_shape, pz_lift = shape(3 * CX, CY, 128), shape(3 * CX + 1, CY, 128)
    v_shape, s_shape = resident(3, CX, CY, CZ), resident(6, CX, CY, CZ)
    bag_shape = shape(BAG, 128)
    plane_z = pltpu.VMEM((3, CX, CY, CZ), F32)
    *sent, bag = call(
        prepare,
        PAYLOAD + [pz_shape, bag_shape],
        *outside(stress, sea_depth, height, wet_mask),
        ins=[HB] * 4,
        scratch=[
            pltpu.VMEM((104, LAT), F32),
            pltpu.VMEM((LON, LAT), F32),
            pltpu.VMEM((LON, LAT), F32),
            pltpu.VMEM((LON, LAT), jnp.int32),
            pltpu.VMEM((2, 3, CX, 8, CZ), F32),
            pltpu.SemaphoreType.DMA((24,)),
        ],
    )
    r1 = exchange(sent)
    velocity, stress, mat, coef, dzs, owner, cell = call(
        fetch,
        [
            v_shape, s_shape, pltpu.VMEM((CX, CY, CZ), jnp.int32), resident(1, CX, CY, CZ), v_shape,
            pltpu.VMEM((1, 512), jnp.int32), pltpu.VMEM((8, 512), jnp.int32),
        ],
        *outside(velocity, stress, material, owner_map.reshape(64, 1, 512), cell_map), tab,
        ins=[HB] * 5 + [VM],
        scratch=[pltpu.SemaphoreType.DMA((7,))],
    )
    v1, *sent, lift, bag = call(
        functools.partial(move, 1, False),
        [v_shape] + PAYLOAD + [pz_shape, shape(32, 128), bag_shape],
        velocity, stress, coef, dzs, *r1, bag,
        aliases={0: 0, 9: 7},
    )
    r2 = exchange(sent)
    mat, v1 = lax.optimization_barrier((mat, v1))
    coef2, dzs = call(lame, [resident(2, CX, CY, CZ), v_shape], tab, mat, v1)
    s1, *sent, bag, s_low = call(
        functools.partial(strain, 2),
        [s_shape] + PAYLOAD + [pz_shape, bag_shape] + [pltpu.HBM((6, HALF, CY, CZ), F32)],
        stress, v1, coef2, dzs, *r2, bag,
        outs_at=[VM] * 7 + [HB],
        scratch=[pltpu.SemaphoreType.DMA((HALF,))], aliases={0: 0, 9: 6},
    )
    r3 = exchange(sent)
    owner, cell, s1 = lax.optimization_barrier((owner, cell, s1))
    group, slot, code, coef_copy, s_high = call(
        address,
        [shape(8, 512), shape(512, 128), shape(8, 128)]
        + [pltpu.HBM((2, CX, CY, CZ), F32), pltpu.HBM((6, CX - HALF, CY, CZ), F32)],
        owner, cell, coef2, s1,
        outs_at=[VM] * 3 + [HB] * 2,
        scratch=[pltpu.SemaphoreType.DMA((2,))],
    )
    (dzs,) = call(functools.partial(slopes_z, comps=SZ), [v_shape], s1)
    r3, group, slot, code, coef_copy, s_high = lax.optimization_barrier((r3, group, slot, code, coef_copy, s_high))
    *sent, lift, v_out, bag = call(
        functools.partial(move, 3, True),
        PAYLOAD + [pz_lift, shape(32, 128)] + [pltpu.HBM(dims, F32) for dims in ((3, CX, CY, CZ), (BAG, 128))],
        v1, s1, coef, dzs, *r3, bag, lift,
        outs_at=[VM] * 6 + [HB] * 2,
        scratch=[plane_z, pltpu.VMEM((BAG, 128), F32), pltpu.SemaphoreType.DMA((CX + 1,))],
    )
    *r4, zs = exchange(sent)
    (out,) = call(
        pack_lift,
        [shape(64, 128)],
        lift, zs, group, slot, code,
        scratch=[pltpu.VMEM((512, 128), F32)],
    )
    s2, far = call(
        finish,
        [pltpu.HBM(dims, F32) for dims in ((6, CX, CY, CZ), (OCR, 128))],
        *outside(s_low, s_high, v_out, coef_copy, zs), *r4,
        ins=[HB] * 5 + [VM] * 4,
        outs_at=[HB] * 2,
        scratch=[
            pltpu.VMEM((6, CX, CY, CZ), F32),
            plane_z,
            pltpu.VMEM((2, CX, CY, CZ), F32),
            pltpu.VMEM((3 * CX + 1, CY, 128), F32),
            plane_z,
            pltpu.SemaphoreType.DMA((8 + CX,)),
        ],
    )
    arrived = lax.all_to_all(out, ("gx", "gy"), split_axis=0, concat_axis=0, tiled=True)
    block = pltpu.VMEM((LON, LAT), F32)
    height_out, current_out = call(
        ocean, [shape(LON, LAT)] * 2,
        arrived, *outside(far, bag, height, current, wet_mask),
        ins=[VM] + [HB] * 5,
        scratch=[
            pltpu.VMEM((OCR, 128), F32), pltpu.VMEM((BAG, 128), F32),
            block, block, pltpu.VMEM((LON, LAT), jnp.int32),
            pltpu.VMEM((512, 4096), jnp.bfloat16),
            pltpu.VMEM((64, 128), F32),
            pltpu.VMEM((64, 128), F32),
            pltpu.VMEM((256, 128), F32),
            pltpu.VMEM((32, 128), F32),
            pltpu.VMEM((72, 128), F32),
            pltpu.SemaphoreType.DMA((5,)),
        ],
    )
    return v_out, s2, height_out, current_out


def solution(mesh):
    return jax.shard_map(
        local,
        mesh=mesh,
        in_specs=(
            P(None, "gx", "gy", "gz"),
            P(None, "gx", "gy", "gz"),
            P("gx", "gy", "gz"),
            P(),
            P(),
            P(),
            P("gx", ("gy", "gz")),
            P("gx", ("gy", "gz")),
            P("gx", ("gy", "gz")),
            P("gx", ("gy", "gz")),
        ),
        out_specs=(
            P(None, "gx", "gy", "gz"),
            P(None, "gx", "gy", "gz"),
            P("gx", ("gy", "gz")),
            P("gx", ("gy", "gz")),
        ),
        check_vma=False,
    )
```
